32 devices in a mesh: req: 32 (over z, y, x, core).
Axes of the slice: x: 2, y: 2, z: 4, core: 2. Of those that a mesh axis runs over, the one named last changes fastest.
Arguments:
- queries: bfloat16 [4096, 2560], P('req'), may hold values from -8 to 8
- prefix_keys: bfloat16 [8192, 640], P('req'), may hold values from -6 to 6
- prefix_values: bfloat16 [8192, 640], P('req'), may hold values from -6 to 6
- pool_keys: bfloat16 [4096, 16, 640], P('req'), may hold values from -6 to 6
- pool_values: bfloat16 [4096, 16, 640], P('req'), may hold values from -6 to 6
- page_table: int32 [4096, 8], P('req'), may hold values from 0 to 127
- private_length: int32 [4096], P('req'), may hold values from 1 to 128
- group_ids: int32 [4096, 1], P('req'), may hold values from 0 to 31; in each aligned block of 128 rows (0 to 127, 128 to 255, ...) at most 8 rows name the same one
- live_rows: int32 [32], P('req'), may hold values from 1 to 128, 2048 in all
- out_weight: bfloat16 [2560, 2560], replicated, may hold values from -0.75 to 0.75
Outputs:
- projected: bfloat16 [4096, 2560], P('req')
The draws below stay inside these ranges and needn't reach their ends.
Inputs may be any that keep to these rules, and one draw needn't show every extreme that they name: `group_ids`: the group of a row is also the index of the device that holds that group's prompt; at most 8 rows of one device name one group. `live_rows`: the counts sum to 2048.
All inputs are finite; a program needn't handle non-finite values. No bound on the sum of `live_rows` on one device may be relied on, other than what follows from the above.
Results may differ from the reference program's by a relative error of at most 0.007.
Values may be sent and summed in bfloat16 or wider, within the bound.
No kernel may reach another device: no remote copies, remote signals or barrier semaphores. Data moves between devices by JAX's collectives and lax.ppermute only.
A program may use at most 128 MiB of HBM per device.

```python
import math
import jax
import jax.numpy as jnp
import numpy as np
from jax import lax

D = 2560
H = 32
KVH = 8
HD = 80
Q_DEV = 128
PREF = 256
PAGE = 16
MAXP = 8
POOL = 128
KW = 640
GROUPS = 32
ROWS = 4096
PREFS = 8192
POOLS = 4096
PRIV = 128
GMOST = 8
BAL = 64
N_REQ = 32


def draw_queries(key, part):
    normal_part = jnp.clip(jax.random.normal(jax.random.fold_in(key, 11), (ROWS, D), jnp.float32), -6.0, 6.0)
    return normal_part.astype(jnp.bfloat16)


def draw_prefix_keys(key, part):
    normal_part = jnp.clip(jax.random.normal(jax.random.fold_in(key, 21), (PREFS, KW), jnp.float32), -6.0, 6.0)
    return normal_part.astype(jnp.bfloat16)


def draw_pool_keys(key, part):
    normal_part = jnp.clip(jax.random.normal(jax.random.fold_in(key, 31), (POOLS, PAGE, KW), jnp.float32), -6.0, 6.0)
    return normal_part.astype(jnp.bfloat16)


def with_ends(result, own_key, smallest, top_value):
    shape = result.shape
    spot = [jax.random.randint(jax.random.fold_in(own_key, axis), (), 0, shape[axis]) for axis in range(len(shape))]
    result = result.at[tuple(spot)].set(smallest)
    longest = shape.index(max(shape))
    spot[longest] = (spot[longest] + 1) % shape[longest]
    return result.at[tuple(spot)].set(top_value)


def steps_of(key, dims, split, least, high):
    factor_of = 1.0
    for dim, parts in split:
        steps = jax.random.uniform(jax.random.fold_in(jax.random.fold_in(key, 6), dim), (parts,), jnp.float32, least / len(split), high / len(split))
        factor_of = factor_of * jnp.repeat(jnp.exp(steps), dims[dim] // parts).reshape((-1,) + (1,) * (len(dims) - 1 - dim))
    return factor_of


def profile(count, total, reach, skew):
    weights = [(1 << 20) // math.isqrt(grade ** skew) + 1 for grade in range(2, count + 1)]
    rest, holding = total - reach - (count - 1), [1] * (count - 1)
    while rest > 0:
        free = [i for i in range(count - 1) if holding[i] < reach]
        whole, left = sum([weights[i] for i in free]), rest
        for i in free:
            more = min(reach - holding[i], max(1, left * weights[i] // whole), rest)
            holding[i] = holding[i] + more
            rest = rest - more
    return np.array([reach] + holding)


def uneven(rng, number_of, total, reach, lean):
    if number_of == 2:
        one = jax.random.randint(rng, (), max(1, total - reach), min(reach, total - 1) + 1)
        return jnp.stack([one, total - one])
    sizes = jnp.asarray(profile(number_of, total, reach, lean), jnp.int32)
    pairs = (number_of - 1) // 2
    source_of, receiver = sizes[1:1 + 2 * pairs:2], sizes[2:2 + 2 * pairs:2]
    room = jnp.minimum(source_of - 1, reach - receiver)
    moved = jax.random.randint(jax.random.fold_in(rng, 1), (pairs,), 0, 1 << 20) % (room + 1)
    sizes = sizes.at[1:1 + 2 * pairs:2].set(source_of - moved).at[2:2 + 2 * pairs:2].set(receiver + moved)
    return sizes[jax.random.permutation(jax.random.fold_in(rng, 2), number_of)]


def deal_out(rng, own, number, rows, number_of, top, reach, skew):
    order = jax.random.permutation(rng, number_of)
    heavy_load, usual = shares(number_of, rows * top, reach, skew, True), shares(number_of, rows * top, reach, skew, False)
    places = jnp.arange(number_of)

    def named(sizes, offset_by):
        used = int((sizes > 0).sum())
        fixed = max(1, used // 4)
        passed = fixed + (places - fixed + offset_by * (used - fixed)) % max(1, number_of - fixed)
        return jnp.zeros((number_of,), jnp.int32).at[order[jnp.where(places < fixed, places, passed)]].set(jnp.asarray(sizes, jnp.int32))

    sizes = jnp.where(number % 4 == 0, named(heavy_load, number // 4), named(usual, number - number // 4 - 1))
    mixed = jax.random.permutation(jax.random.fold_in(own, 3), number_of)
    source_of, taker = mixed[0:number_of // 2 * 2:2], mixed[1:number_of // 2 * 2:2]
    margin = jnp.minimum(sizes[source_of] - 1, reach - sizes[taker]) // 2
    margin = jnp.where((source_of == order[0]) | (taker == order[0]) | (sizes[taker] == 0), 0, jnp.maximum(margin, 0))
    passed = jax.random.randint(jax.random.fold_in(own, 4), (number_of // 2,), 0, 1 << 20) % (margin + 1)
    sizes = sizes.at[source_of].add(-passed).at[taker].add(passed)
    members = jnp.searchsorted(jnp.cumsum(sizes), jnp.arange(rows * top), side="right").astype(jnp.int32)
    listing = members.reshape(top, rows).T
    listing = listing[jax.random.permutation(jax.random.fold_in(own, 1), rows)]
    offset_by = jax.random.randint(jax.random.fold_in(own, 2), (rows, 1), 0, top)
    return jnp.take_along_axis(listing, (jnp.arange(top)[None, :] + offset_by) % top, axis=1)


def shares(number_of, total, bound, skew, full):
    portions = [(1 << 20) // math.isqrt(grade ** skew) + 1 for grade in range(1, number_of + 1)]
    largest = bound if full else min(bound, max(-(-total // number_of), total * portions[0] // sum(portions)))
    least = 1 if total - largest >= number_of - 1 else 0
    counts, spare = [largest] + [least] * (number_of - 1), total - largest - least * (number_of - 1)
    while spare > 0:
        candidates = [i for i in range(1, number_of) if counts[i] < largest] or [i for i in range(1, number_of) if counts[i] < bound]
        pool, remaining = sum([portions[i] for i in candidates]), spare
        for i in candidates:
            more = min(bound - counts[i], max(1, remaining * portions[i] // pool), spare)
            counts[i] = counts[i] + more
            spare = spare - more
    return np.array(counts)


def normal_values(key, extent, spread, most, shards=(), held_as=jnp.bfloat16):
    values = jax.random.normal(key, extent, jnp.float32) * spread
    if len(shards) > 0:
        values = steps_of(key, extent, shards, -0.22, 0.18) * values
    return jnp.clip(values, min=-most, max=most).astype(held_as)


def setup_inputs(seed: int = 0) -> dict:
    seeds = jax.random.split(jax.random.key(seed), 11)
    queries = draw_queries(jax.random.fold_in(seeds[10], 71), 0)
    prefix_keys = draw_prefix_keys(jax.random.fold_in(seeds[10], 71), 0)
    prefix_values = normal_values(seeds[2], (PREFS, KW), 1.0, 6.0, ((0, 32),))
    pool_keys = draw_pool_keys(jax.random.fold_in(seeds[10], 71), 0)
    pool_values = normal_values(seeds[4], (POOLS, PAGE, KW), 1.0, 6.0, ((0, 32),))
    page_table = with_ends(jax.random.randint(seeds[5], (ROWS, MAXP), 0, POOL), jax.random.fold_in(seeds[5], 1), 0, POOL - 1).astype(jnp.int32)
    private_length = with_ends(jax.random.randint(seeds[6], (ROWS,), 1, PRIV + 1), jax.random.fold_in(seeds[6], 1), 1, PRIV).astype(jnp.int32)
    group_ids_keys = jax.random.split(jax.random.fold_in(seeds[7], 1), ROWS // Q_DEV)
    group_ids_turns = jax.random.permutation(jax.random.fold_in(seeds[7], 3), ROWS // Q_DEV)
    group_ids = jax.vmap(lambda own, number: deal_out(jax.random.fold_in(seeds[7], 2), own, number, Q_DEV, GROUPS, 1, GMOST, 2))(group_ids_keys, group_ids_turns).reshape((ROWS, 1))
    live_rows = uneven(seeds[8], N_REQ, N_REQ * BAL, Q_DEV, 2).astype(jnp.int32)
    out_weight = normal_values(seeds[9], (D, D), (D // 40) ** -0.5, 0.75)
    return {"queries": queries, "prefix_keys": prefix_keys, "prefix_values": prefix_values, "pool_keys": pool_keys, "pool_values": pool_values, "page_table": page_table, "private_length": private_length, "group_ids": group_ids, "live_rows": live_rows, "out_weight": out_weight}


def weigh(scores, values, spec):
    largest = jnp.max(scores, axis=-1, keepdims=True)
    weights = jnp.exp(scores - largest)
    weight_sum = jnp.sum(weights, axis=-1)
    rounded = lax.optimization_barrier(weights.astype(jnp.bfloat16)).astype(jnp.float32)
    summed = jnp.einsum(spec, rounded, values)
    return summed / weight_sum[..., None], largest[..., 0] + jnp.log(weight_sum)


def reference(queries, prefix_keys, prefix_values, pool_keys, pool_values, page_table, private_length, group_ids, live_rows, out_weight):
    block_rows = 32
    block_count = ROWS // block_rows
    group_size = H // KVH
    scale = HD ** -0.5
    prefix_table = prefix_keys.reshape(GROUPS, PREF, KVH, HD)
    prefix_store = prefix_values.reshape(GROUPS, PREF, KVH, HD)

    def one_block(block_index):
        first_row = block_index * block_rows
        query_block = lax.dynamic_slice_in_dim(queries, first_row, block_rows, 0).astype(jnp.float32)
        query_block = query_block.reshape(block_rows, KVH, group_size, HD)
        groups = lax.dynamic_slice_in_dim(group_ids[:, 0], first_row, block_rows, 0)
        key_rows = prefix_table[groups].astype(jnp.float32)
        value_rows = prefix_store[groups].astype(jnp.float32)
        scores = jnp.einsum("rkgd,rtkd->rkgt", query_block, key_rows) * scale
        prefix_out, prefix_lse = weigh(scores, value_rows, "rkgt,rtkd->rkgd")
        prefix_out = lax.optimization_barrier(prefix_out.astype(jnp.bfloat16)).astype(jnp.float32)
        device = (first_row // Q_DEV).astype(jnp.int32)
        page_rows = lax.dynamic_slice_in_dim(page_table, first_row, block_rows, 0) + device * POOL
        private_keys = pool_keys[page_rows].reshape(block_rows, PRIV, KVH, HD).astype(jnp.float32)
        private_values = pool_values[page_rows].reshape(block_rows, PRIV, KVH, HD).astype(jnp.float32)
        lengths = lax.dynamic_slice_in_dim(private_length, first_row, block_rows, 0)
        visible = jnp.arange(PRIV, dtype=jnp.int32)[None, :] < lengths[:, None]
        scores = jnp.einsum("rkgd,rtkd->rkgt", query_block, private_keys) * scale
        scores = jnp.where(visible[:, None, None, :], scores, -1e30)
        private_out, private_lse = weigh(scores, private_values, "rkgt,rtkd->rkgd")
        largest = jnp.maximum(prefix_lse, private_lse)
        prefix_share = jnp.exp(prefix_lse - largest)
        private_share = jnp.exp(private_lse - largest)
        combined = (prefix_share[..., None] * prefix_out + private_share[..., None] * private_out) / (prefix_share + private_share)[..., None]
        return combined.reshape(block_rows, D).astype(jnp.bfloat16)

    attended = lax.map(one_block, jnp.arange(block_count, dtype=jnp.int32)).reshape(ROWS, D)
    projected = jnp.dot(attended, out_weight, preferred_element_type=jnp.float32)
    row_index = jnp.arange(ROWS, dtype=jnp.int32)
    is_live = (row_index % Q_DEV) < live_rows[row_index // Q_DEV]
    return jnp.where(is_live[:, None], projected, 0.0).astype(jnp.bfloat16)
```

```python
import functools
import math

import jax
import jax.numpy as jnp
from jax import lax
from jax.experimental import pallas as pl
from jax.experimental.pallas import tpu as pltpu
from jax.sharding import PartitionSpec as P

H = 32
KVH = 8
HD = 80
GROUP = H // KVH
LANES = 128
WIN = 256
SCALE = HD ** (-0.5) * math.log2(math.e)
LN2 = math.log(2.0)
NEVER = -1e30
VMEM_LIMIT = 60 * 1024 * 1024


def window(start, width):
    base = min(start // LANES * LANES, width - WIN)
    return base, start - base


def iota(shape, axis):
    return lax.broadcasted_iota(jnp.int32, shape, axis)


def moved(block, source, target):
    shift = (target - source) % WIN
    if shift:
        block = pltpu.roll(block, shift, 1)
    lane = iota(block.shape, 1)
    return jnp.where((lane >= target) & (lane < target + HD), block, 0.0)


def padded_queries(q_ref, head, key_offset):
    base, offset = window(head * HD, q_ref.shape[1])
    block = q_ref[:, base : base + WIN].astype(jnp.float32)
    return moved(block, offset, key_offset).astype(jnp.bfloat16)


def as_row(column):
    n = column.shape[0]
    same = iota((n, n), 0) == iota((n, n), 1)
    return jnp.sum(jnp.where(same, column, 0), axis=0, keepdims=True)


def slots_of(groups, half, slot_count):
    n = groups.shape[0]
    row = as_row(groups)
    earlier = iota((n, n), 1) < iota((n, n), 0)
    rank = jnp.sum(jnp.where((groups == row) & earlier, 1, 0), axis=1, keepdims=True)
    upper = jnp.where(groups >= half, 1, 0)
    return (groups - upper * half) * slot_count + rank, upper


def place_kernel(half, slot_count, side_ref, groups_ref, q_ref, own_ref, other_ref):
    n = q_ref.shape[0]
    slot, upper = slots_of(groups_ref[...], half, slot_count)
    slot_row, upper_row = as_row(slot), as_row(upper)
    hit = slot_row == iota((n, n), 0)
    side = side_ref[0]
    for out_ref, wanted in ((own_ref, side), (other_ref, 1 - side)):
        spread = jnp.where(hit & (upper_row == wanted), 1.0, 0.0).astype(jnp.bfloat16)
        for base in range(0, q_ref.shape[1], 512):
            cols = slice(base, base + 512)
            out_ref[:, cols] = jnp.dot(
                spread, q_ref[:, cols], preferred_element_type=jnp.float32
            ).astype(jnp.bfloat16)


def place(queries, group_ids, side, half, slot_count):
    shape = jax.ShapeDtypeStruct(queries.shape, queries.dtype)
    return pl.pallas_call(
        functools.partial(place_kernel, half, slot_count),
        out_shape=(shape, shape),
        in_specs=[
            pl.BlockSpec(memory_space=pltpu.SMEM),
            pl.BlockSpec(memory_space=pltpu.VMEM),
            pl.BlockSpec(memory_space=pltpu.VMEM),
        ],
        out_specs=(pl.BlockSpec(memory_space=pltpu.VMEM),) * 2,
        compiler_params=pltpu.CompilerParams(vmem_limit_bytes=VMEM_LIMIT),
        cost_estimate=pl.CostEstimate(
            flops=4 * 128 * 128 * 2560, bytes_accessed=3 * 128 * 2560 * 2, transcendentals=0
        ),
        name="place",
    )(side, group_ids, queries)


def prefix_kernel(q_ref, k_ref, v_ref, out_ref, acc_ref):
    n, width = q_ref.shape
    acc_ref[...] = jnp.zeros_like(acc_ref)
    lane = iota((n, LANES), 1)
    lse = jnp.zeros((n, LANES), jnp.float32)
    for k in range(KVH):
        base, key_offset = window(k * HD, k_ref.shape[1])
        keys = k_ref[:, base : base + WIN]
        values = v_ref[:, base : base + WIN]
        for g in range(GROUP):
            head = k * GROUP + g
            q = padded_queries(q_ref, head, key_offset)
            scores = lax.dot_general(
                q, keys, (((1,), (1,)), ((), ())), preferred_element_type=jnp.float32
            )
            scores = scores * SCALE
            top = jnp.max(scores, axis=1, keepdims=True)
            weights = jnp.exp2(scores - top)
            total = jnp.sum(weights, axis=1, keepdims=True)
            summed = jnp.dot(
                weights.astype(jnp.bfloat16), values, preferred_element_type=jnp.float32
            )
            to, offset = window(head * HD, width)
            acc_ref[:, to : to + WIN] += moved(summed / total, key_offset, offset)
            lse = jnp.where(lane == head, (top + jnp.log2(total)) * LN2, lse)
    out_ref[:, :width] = acc_ref[...].astype(jnp.bfloat16)
    packed = jnp.zeros((n, LANES), jnp.float32)
    for part in range(3):
        piece = lse.astype(jnp.bfloat16).astype(jnp.float32)
        lse = lse - piece
        packed += pltpu.roll(piece, part * H, 1) if part else piece
    out_ref[:, width:] = packed.astype(jnp.bfloat16)


def prefix_part(rows, keys, values):
    n, width = rows.shape
    return pl.pallas_call(
        prefix_kernel,
        out_shape=jax.ShapeDtypeStruct((n, width + LANES), jnp.bfloat16),
        in_specs=[pl.BlockSpec(memory_space=pltpu.VMEM)] * 3,
        out_specs=pl.BlockSpec(memory_space=pltpu.VMEM),
        scratch_shapes=[pltpu.VMEM((n, width), jnp.float32)],
        compiler_params=pltpu.CompilerParams(vmem_limit_bytes=VMEM_LIMIT),
        cost_estimate=pl.CostEstimate(
            flops=4 * n * 256 * width, bytes_accessed=4 * n * width * 2, transcendentals=n * 256 * H
        ),
        name="prefix",
    )(rows, keys, values)


def private_bias(pages, lengths, token_count, page_size):
    n, most = pages.shape
    page_count = token_count // page_size
    page = iota((n, page_count), 1)
    full = jnp.zeros((n, page_count), jnp.float32)
    partial = jnp.zeros((n, page_count), jnp.float32)
    for j in range(most):
        same = pages[:, j : j + 1] == page
        whole = lengths >= (j + 1) * page_size
        some = (lengths > j * page_size) & (lengths < (j + 1) * page_size)
        full += jnp.where(same & whole, 1.0, 0.0)
        partial += jnp.where(same & some, 1.0, 0.0)
    token = iota((page_count, token_count), 1)
    first = iota((page_count, token_count), 0) * page_size
    expand = jnp.where((token >= first) & (token < first + page_size), 1.0, 0.0).astype(jnp.bfloat16)
    full = jnp.dot(full.astype(jnp.bfloat16), expand, preferred_element_type=jnp.float32)
    partial = jnp.dot(partial.astype(jnp.bfloat16), expand, preferred_element_type=jnp.float32)
    within = iota((n, token_count), 1) % page_size
    seen = within < lengths % page_size
    multiple = full + jnp.where(seen, partial, 0.0)
    return jnp.where(multiple > 0.0, jnp.log2(jnp.maximum(multiple, 1.0)), NEVER)


def private_kernel(
    first_head, heads, page_size, q_ref, k_ref, v_ref, pages_ref, lengths_ref,
    out_ref, lse_ref, qs_ref, bias_ref, sum_ref, acc_ref
):
    n = q_ref.shape[0]
    tokens, key_width = k_ref.shape
    bias_ref[...] = private_bias(pages_ref[...], lengths_ref[...], tokens, page_size)
    for i in range(heads):
        k = first_head + i
        _, key_offset = window(k * HD, key_width)
        for g in range(GROUP):
            qs_ref[i * GROUP + g] = padded_queries(q_ref, k * GROUP + g, key_offset)
    lane = iota((n, LANES), 1)

    def one(i, lse):
        k = first_head + i // GROUP
        base = pl.multiple_of(jnp.minimum(k * HD // LANES * LANES, key_width - WIN), LANES)
        scores = lax.dot_general(
            qs_ref[i],
            k_ref[:, pl.ds(base, WIN)],
            (((1,), (1,)), ((), ())),
            preferred_element_type=jnp.float32,
        )
        scores = scores * SCALE + bias_ref[...]
        top = jnp.max(scores, axis=1, keepdims=True)
        weights = jnp.exp2(scores - top)
        total = jnp.sum(weights, axis=1, keepdims=True)
        summed = jnp.dot(
            weights.astype(jnp.bfloat16),
            v_ref[:, pl.ds(base, WIN)],
            preferred_element_type=jnp.float32,
        )
        sum_ref[i] = summed / total
        return jnp.where(lane == i, (top + jnp.log2(total)) * LN2, lse)

    lse_ref[...] = lax.fori_loop(0, heads * GROUP, one, jnp.zeros((n, LANES), jnp.float32))
    acc_ref[...] = jnp.zeros_like(acc_ref)
    for i in range(heads):
        _, key_offset = window((first_head + i) * HD, key_width)
        for g in range(GROUP):
            to, offset = window((i * GROUP + g) * HD, acc_ref.shape[1])
            acc_ref[:, to : to + WIN] += moved(sum_ref[i * GROUP + g], key_offset, offset)
    out_ref[...] = acc_ref[...]


def private_part(queries, keys, values, page_table, lengths, page_size, first_head, heads):
    n = queries.shape[0]
    tokens = keys.shape[0]
    width = heads * GROUP * HD
    return pl.pallas_call(
        functools.partial(private_kernel, first_head, heads, page_size),
        out_shape=(
            jax.ShapeDtypeStruct((n, width), jnp.float32),
            jax.ShapeDtypeStruct((n, LANES), jnp.float32),
        ),
        in_specs=[pl.BlockSpec(memory_space=pltpu.VMEM)] * 5,
        out_specs=(pl.BlockSpec(memory_space=pltpu.VMEM),) * 2,
        scratch_shapes=[
            pltpu.VMEM((heads * GROUP, n, WIN), jnp.bfloat16),
            pltpu.VMEM((n, tokens), jnp.float32),
            pltpu.VMEM((heads * GROUP, n, WIN), jnp.float32),
            pltpu.VMEM((n, width), jnp.float32),
        ],
        compiler_params=pltpu.CompilerParams(vmem_limit_bytes=VMEM_LIMIT),
        cost_estimate=pl.CostEstimate(
            flops=4 * n * tokens * heads * GROUP * WIN,
            bytes_accessed=2 * tokens * 640 * 2,
            transcendentals=n * tokens * heads * GROUP,
        ),
        name="private",
    )(queries, keys, values, page_table, lengths)


def expand_heads(share, width):
    n = share.shape[0]
    lane = iota((n, LANES), 1)
    share = jnp.where(lane < H, share, 0.0)
    high = share.astype(jnp.bfloat16).astype(jnp.float32)
    both = (high + pltpu.roll(share - high, H, 1)).astype(jnp.bfloat16)
    row = iota((LANES, width), 0)
    head = jnp.where(row >= H, row - H, row)
    first = head * HD
    column = iota((LANES, width), 1)
    spread = (row < 2 * H) & (column >= first) & (column < first + HD)
    return jnp.dot(
        both, jnp.where(spread, 1.0, 0.0).astype(jnp.bfloat16), preferred_element_type=jnp.float32
    )


def finish_kernel(
    half, slot_count, chunk, side_ref, live_ref, groups_ref, own_ref, other_ref,
    low_ref, high_ref, low_lse_ref, high_lse_ref, w_hbm, out_ref, w_ref, sems
):
    n, width = out_ref.shape
    copies = []
    for i in range(width // chunk):
        cols = pl.ds(i * chunk, chunk)
        copy = pltpu.make_async_copy(w_hbm.at[:, cols], w_ref.at[:, cols], sems.at[i])
        copy.start()
        copies.append(copy)
    slot, upper = slots_of(groups_ref[...], half, slot_count)
    hit = slot == iota((n, n), 1)
    side = side_ref[0]
    own = jnp.where(hit & (upper == side), 1.0, 0.0).astype(jnp.bfloat16)
    other = jnp.where(hit & (upper != side), 1.0, 0.0).astype(jnp.bfloat16)
    pick = jnp.concatenate([own, other], axis=1)

    def picked(cols):
        both = jnp.concatenate([own_ref[:, cols], other_ref[:, cols]], axis=0)
        return jnp.dot(pick, both, preferred_element_type=jnp.float32)

    pieces = picked(slice(width, width + LANES))
    lane = iota((n, LANES), 1)
    prefix_lse = (
        pieces + pltpu.roll(pieces, LANES - H, 1) + pltpu.roll(pieces, LANES - 2 * H, 1)
    )
    prefix_lse = jnp.where(lane < H, prefix_lse, 0.0)
    private_lse = jnp.where(
        lane < H // 2, low_lse_ref[...], pltpu.roll(high_lse_ref[...], H // 2, 1)
    )
    private_lse = jnp.where(lane < H, private_lse, 0.0)
    top = jnp.maximum(prefix_lse, private_lse)
    a, b = jnp.exp(prefix_lse - top), jnp.exp(private_lse - top)
    prefix_share = expand_heads(a / (a + b), width)
    private_share = expand_heads(b / (a + b), width)
    private = jnp.concatenate([low_ref[...], high_ref[...]], axis=1)
    attended = prefix_share * picked(slice(0, width)) + private_share * private
    attended = attended.astype(jnp.bfloat16)
    is_live = iota((n, 1), 0) < live_ref[0]
    for i, copy in enumerate(copies):
        copy.wait()
        cols = slice(i * chunk, (i + 1) * chunk)
        projected = jnp.dot(attended, w_ref[:, cols], preferred_element_type=jnp.float32)
        out_ref[:, cols] = jnp.where(is_live, projected, 0.0).astype(out_ref.dtype)


def finish(side, live, group_ids, own, other, low, high, low_lse, high_lse, weight, half, slot_count):
    n = own.shape[0]
    width = weight.shape[1]
    chunk = 512
    vmem = pl.BlockSpec(memory_space=pltpu.VMEM)
    smem = pl.BlockSpec(memory_space=pltpu.SMEM)
    return pl.pallas_call(
        functools.partial(finish_kernel, half, slot_count, chunk),
        out_shape=jax.ShapeDtypeStruct((n, width), jnp.bfloat16),
        in_specs=[smem, smem] + [vmem] * 7 + [pl.BlockSpec(memory_space=pl.ANY)],
        out_specs=vmem,
        scratch_shapes=[
            pltpu.VMEM(weight.shape, weight.dtype),
            pltpu.SemaphoreType.DMA((width // chunk,)),
        ],
        compiler_params=pltpu.CompilerParams(vmem_limit_bytes=VMEM_LIMIT),
        cost_estimate=pl.CostEstimate(
            flops=2 * n * width * width, bytes_accessed=2 * width * width, transcendentals=0
        ),
        name="finish",
    )(side, live, group_ids, own, other, low, high, low_lse, high_lse, weight)


def per_device(
    queries,
    prefix_keys,
    prefix_values,
    pool_keys,
    pool_values,
    page_table,
    private_length,
    group_ids,
    live_rows,
    out_weight,
):
    devices = lax.axis_size("req")
    half = devices // 2
    row_count, width = queries.shape
    slot_count = 2 * row_count // devices
    page_size = pool_keys.shape[1]
    halves = [list(range(half)), list(range(half, devices))]
    across = [(i, (i + half) % devices) for i in range(devices)]
    side = (lax.axis_index("req") // half).astype(jnp.int32).reshape(1)

    far_keys = lax.ppermute(prefix_keys, "req", across)
    far_values = lax.ppermute(prefix_values, "req", across)
    own, other = place(queries, group_ids, side, half, slot_count)

    def exchange(rows):
        blocks = rows.reshape(half, slot_count, rows.shape[1])
        blocks = lax.all_to_all(
            blocks, "req", split_axis=0, concat_axis=0, tiled=True, axis_index_groups=halves
        )
        return blocks.reshape(rows.shape)

    own_back = exchange(prefix_part(exchange(own), prefix_keys, prefix_values))
    other_back = exchange(prefix_part(exchange(other), far_keys, far_values))

    lengths = private_length.reshape(row_count, 1)
    flat_keys = pool_keys.reshape(-1, pool_keys.shape[2])
    flat_values = pool_values.reshape(-1, pool_values.shape[2])
    private = functools.partial(
        private_part, queries, flat_keys, flat_values, page_table, lengths, page_size
    )
    low, low_lse = private(0, KVH // 2)
    high, high_lse = private(KVH // 2, KVH // 2)
    return finish(
        side, live_rows, group_ids, own_back, other_back, low, high, low_lse, high_lse,
        out_weight, half, slot_count,
    )


def solution(mesh):
    placed = (
        P("req", None),
        P("req", None),
        P("req", None),
        P("req", None, None),
        P("req", None, None),
        P("req", None),
        P("req"),
        P("req", None),
        P("req"),
        P(),
    )
    return jax.shard_map(
        per_device, mesh=mesh, in_specs=placed, out_specs=P("req", None), check_vma=False
    )
```

```python
import functools
import math

import jax
import jax.numpy as jnp
from jax import lax
from jax.experimental import pallas as pl
from jax.experimental.pallas import tpu as pltpu
from jax.sharding import PartitionSpec as P

H = 32
KVH = 8
HD = 80
GROUP = H // KVH
LANES = 128
WIN = 256
SCALE = HD ** (-0.5) * math.log2(math.e)
LN2 = math.log(2.0)
NEVER = -1e30
VMEM = pl.BlockSpec(memory_space=pltpu.VMEM)
SMEM = pl.BlockSpec(memory_space=pltpu.SMEM)
ANY = pl.BlockSpec(memory_space=pl.ANY)


def window(start, width):
    base = min(start // LANES * LANES, width - WIN)
    return base, start - base


def iota(shape, axis):
    return lax.broadcasted_iota(jnp.int32, shape, axis)


def params(mib):
    return pltpu.CompilerParams(vmem_limit_bytes=mib * 1024 * 1024)


def transpose_into(target, source):
    rows, cols = source.shape
    for c in range(0, cols, LANES):
        for r in range(0, rows, LANES):
            target[c : c + LANES, r : r + LANES] = source[r : r + LANES, c : c + LANES].T


def as_column(row):
    n = row.shape[1]
    same = iota((n, n), 0) == iota((n, n), 1)
    return jnp.sum(jnp.where(same, row, 0), axis=1, keepdims=True)


def slots_of(groups, half, slot_count):
    n = groups.shape[1]
    earlier = iota((n, n), 0) < iota((n, n), 1)
    same = (as_column(groups) == groups) & earlier
    rank = jnp.sum(jnp.where(same, 1, 0), axis=0, keepdims=True)
    upper = jnp.where(groups >= half, 1, 0)
    return (groups - upper * half) * slot_count + rank, upper


def place_kernel(half, slot_count, side_ref, groups_ref, q_ref, own_ref, other_ref):
    n = q_ref.shape[0]
    slot, upper = slots_of(groups_ref[...], half, slot_count)
    hit = slot == iota((n, n), 0)
    side = side_ref[0]
    own = jnp.where(hit & (upper == side), 1.0, 0.0).astype(jnp.bfloat16)
    other = jnp.where(hit & (upper != side), 1.0, 0.0).astype(jnp.bfloat16)
    spread = jnp.concatenate([own, other], axis=0)
    for base in range(0, q_ref.shape[1], 512):
        cols = slice(base, base + 512)
        both = jnp.dot(spread, q_ref[:, cols], preferred_element_type=jnp.float32)
        both = both.astype(jnp.bfloat16)
        own_ref[:, cols] = both[:n]
        other_ref[:, cols] = both[n:]


def place(queries, groups, side, half, slot_count):
    n, width = queries.shape
    shape = jax.ShapeDtypeStruct(queries.shape, queries.dtype)
    return pl.pallas_call(
        functools.partial(place_kernel, half, slot_count),
        out_shape=(shape, shape),
        in_specs=[SMEM, VMEM, VMEM],
        out_specs=(VMEM, VMEM),
        compiler_params=params(16),
        cost_estimate=pl.CostEstimate(
            flops=4 * n * n * width, bytes_accessed=6 * n * width, transcendentals=0
        ),
        name="place",
    )(side, groups, queries)


def place_queries(qs_ref, i, qt_ref, k, key_width):
    n = qt_ref.shape[1]
    _, first = window(k * HD, key_width)
    if first:
        qs_ref[i, :first] = jnp.zeros((first, GROUP * n), jnp.bfloat16)
    if first + HD < WIN:
        qs_ref[i, first + HD :] = jnp.zeros((WIN - first - HD, GROUP * n), jnp.bfloat16)
    for g in range(GROUP):
        row = (i * GROUP + g) * HD
        qs_ref[i, first : first + HD, g * n : (g + 1) * n] = qt_ref[row : row + HD]


def prefix_kernel(q_ref, k_ref, v_ref, after_ref, out_ref, qt_ref, vt_ref, qs_ref, ot_ref, lse_ref):
    del after_ref
    n, width = q_ref.shape
    key_width = k_ref.shape[1]
    transpose_into(qt_ref, q_ref)
    transpose_into(vt_ref, v_ref)
    for k in range(KVH):
        place_queries(qs_ref, k, qt_ref, k, key_width)
    for k in range(KVH):
        base, _ = window(k * HD, key_width)
        scores = jnp.dot(
            k_ref[:, base : base + WIN], qs_ref[k], preferred_element_type=jnp.float32
        )
        scores = scores * SCALE
        top = jnp.max(scores, axis=0, keepdims=True)
        weights = jnp.exp2(scores - top)
        total = jnp.sum(weights, axis=0, keepdims=True)
        summed = jnp.dot(
            vt_ref[k * HD : (k + 1) * HD],
            weights.astype(jnp.bfloat16),
            preferred_element_type=jnp.float32,
        )
        result = (summed * (1.0 / total)).astype(jnp.bfloat16)
        lse = (top + jnp.log2(total)) * LN2
        for g in range(GROUP):
            head = k * GROUP + g
            ot_ref[head * HD : (head + 1) * HD] = result[:, g * n : (g + 1) * n]
            lse_ref[head : head + 1] = lse[:, g * n : (g + 1) * n]
    transpose_into(out_ref.at[:, :width], ot_ref)
    lse = lse_ref[...]
    high = lse.astype(jnp.bfloat16).astype(jnp.float32)
    middle = (lse - high).astype(jnp.bfloat16).astype(jnp.float32)
    pieces = jnp.concatenate([high, middle, lse - high - middle, jnp.zeros_like(lse)], axis=0)
    out_ref[:, width:] = pieces.T.astype(jnp.bfloat16)


def prefix_part(rows, keys, values, after):
    n, width = rows.shape
    tokens, key_width = keys.shape
    return pl.pallas_call(
        prefix_kernel,
        out_shape=jax.ShapeDtypeStruct((n, width + LANES), jnp.bfloat16),
        in_specs=[VMEM, VMEM, VMEM, ANY],
        out_specs=VMEM,
        scratch_shapes=[
            pltpu.VMEM((width, n), jnp.bfloat16),
            pltpu.VMEM((key_width, tokens), jnp.bfloat16),
            pltpu.VMEM((KVH, WIN, GROUP * n), jnp.bfloat16),
            pltpu.VMEM((width, n), jnp.bfloat16),
            pltpu.VMEM((H, n), jnp.float32),
        ],
        compiler_params=params(24),
        cost_estimate=pl.CostEstimate(
            flops=4 * n * 256 * width, bytes_accessed=4 * n * width * 2, transcendentals=n * 256 * H
        ),
        name="prefix",
    )(rows, keys, values, after)


def fill_bias(bias_ref, pages, lengths, page_size):
    most, n = pages.shape
    page_count = bias_ref.shape[0] // page_size
    page = iota((page_count, n), 0)
    full = jnp.zeros((page_count, n), jnp.float32)
    partial = jnp.zeros((page_count, n), jnp.float32)
    for j in range(most):
        same = pages[j : j + 1] == page
        whole = lengths >= (j + 1) * page_size
        some = (lengths > j * page_size) & (lengths < (j + 1) * page_size)
        full += jnp.where(same & whole, 1.0, 0.0)
        partial += jnp.where(same & some, 1.0, 0.0)
    seen = jnp.where(iota((page_size, n), 0) < lengths % page_size, 1.0, 0.0)
    for p in range(page_count):
        multiple = full[p : p + 1] + seen * partial[p : p + 1]
        bias_ref[p * page_size : (p + 1) * page_size] = jnp.where(
            multiple > 0.0, jnp.log2(jnp.maximum(multiple, 1.0)), NEVER
        )


def private_kernel(
    first_head, heads, page_size, q_ref, k_ref, v_ref, pages_ref, lengths_ref, after_ref,
    out_ref, lse_ref, qt_ref, vt_ref, qs_ref, bias_ref, ot_ref, lses_ref,
    scores_a, scores_b, top_a, top_b, weights_ref
):
    del after_ref
    n = q_ref.shape[0]
    tokens, key_width = k_ref.shape
    rows = GROUP * n
    tile = 256
    query0 = first_head * GROUP * HD
    transpose_into(qt_ref, q_ref.at[:, query0 : query0 + heads * GROUP * HD])
    value0 = first_head * HD // LANES * LANES
    value1 = -(-(first_head + heads) * HD // LANES) * LANES
    transpose_into(vt_ref.at[value0:value1], v_ref.at[:, value0:value1])
    fill_bias(bias_ref, pages_ref[...], lengths_ref[...], page_size)
    for i in range(heads):
        place_queries(qs_ref, i, qt_ref, first_head + i, key_width)

    def score(i, scores_ref, top_ref):
        k = first_head + i
        base = pl.multiple_of(jnp.minimum(k * HD // LANES * LANES, key_width - WIN), LANES)
        top = None
        for t in range(0, tokens, tile):
            scores = jnp.dot(
                k_ref[t : t + tile, pl.ds(base, WIN)],
                qs_ref[i],
                preferred_element_type=jnp.float32,
            )
            bias = bias_ref[t : t + tile]
            scores = scores * SCALE + jnp.concatenate([bias] * GROUP, axis=1)
            scores_ref[t : t + tile] = scores
            highest = jnp.max(scores.reshape(tile // 8, 8, rows), axis=0)
            top = highest if top is None else jnp.maximum(top, highest)
        top_ref[...] = top

    def weigh(i, scores_ref, top_ref, lses):
        top = jnp.max(top_ref[...], axis=0, keepdims=True)
        total = jnp.zeros((8, rows), jnp.float32)
        for t in range(0, tokens, tile):
            weights = jnp.exp2(scores_ref[t : t + tile] - top)
            total += jnp.sum(weights.reshape(tile // 8, 8, rows), axis=0)
            weights_ref[t : t + tile] = weights.astype(jnp.bfloat16)
        total = jnp.sum(total, axis=0, keepdims=True)
        values = vt_ref[pl.ds(pl.multiple_of((first_head + i) * HD, 16), HD)]
        summed = jnp.dot(values, weights_ref[...], preferred_element_type=jnp.float32)
        result = summed * (1.0 / total)
        lse = (top + jnp.log2(total)) * LN2
        row = iota(lses.shape, 0)
        for g in range(GROUP):
            head = i * GROUP + g
            ot_ref[pl.ds(pl.multiple_of(head * HD, 16), HD)] = result[:, g * n : (g + 1) * n]
            lses = jnp.where(row == head, lse[:, g * n : (g + 1) * n], lses)
        return lses

    score(0, scores_a, top_a)

    def two(j, lses):
        i = 2 * j
        score(i + 1, scores_b, top_b)
        lses = weigh(i, scores_a, top_a, lses)
        score(jnp.minimum(i + 2, heads - 1), scores_a, top_a)
        return weigh(i + 1, scores_b, top_b, lses)

    lses_ref[...] = jnp.zeros_like(lses_ref)
    lses_ref[:H] = lax.fori_loop(0, heads // 2, two, jnp.zeros((H, n), jnp.float32))
    lse_ref[...] = lses_ref[...].T
    transpose_into(out_ref, ot_ref)


def private_part(queries, keys, values, pages, lengths, after, page_size, first_head, heads):
    n = queries.shape[0]
    tokens, key_width = keys.shape
    width = heads * GROUP * HD
    return pl.pallas_call(
        functools.partial(private_kernel, first_head, heads, page_size),
        out_shape=(
            jax.ShapeDtypeStruct((n, width), jnp.float32),
            jax.ShapeDtypeStruct((n, LANES), jnp.float32),
        ),
        in_specs=[VMEM] * 5 + [ANY],
        out_specs=(VMEM, VMEM),
        scratch_shapes=[
            pltpu.VMEM((width, n), jnp.bfloat16),
            pltpu.VMEM((key_width, tokens), jnp.bfloat16),
            pltpu.VMEM((heads, WIN, GROUP * n), jnp.bfloat16),
            pltpu.VMEM((tokens, n), jnp.float32),
            pltpu.VMEM((width, n), jnp.float32),
            pltpu.VMEM((LANES, n), jnp.float32),
            pltpu.VMEM((tokens, GROUP * n), jnp.float32),
            pltpu.VMEM((tokens, GROUP * n), jnp.float32),
            pltpu.VMEM((8, GROUP * n), jnp.float32),
            pltpu.VMEM((8, GROUP * n), jnp.float32),
            pltpu.VMEM((tokens, GROUP * n), jnp.bfloat16),
        ],
        compiler_params=params(36),
        cost_estimate=pl.CostEstimate(
            flops=4 * n * tokens * heads * GROUP * WIN,
            bytes_accessed=4 * tokens * key_width,
            transcendentals=n * tokens * heads * GROUP,
        ),
        name="private",
    )(queries, keys, values, pages, lengths, after)


def expand_heads(share, width):
    n = share.shape[0]
    lane = iota((n, LANES), 1)
    share = jnp.where(lane < H, share, 0.0)
    high = share.astype(jnp.bfloat16).astype(jnp.float32)
    both = (high + pltpu.roll(share - high, H, 1)).astype(jnp.bfloat16)
    row = iota((LANES, width), 0)
    head = jnp.where(row >= H, row - H, row)
    first = head * HD
    column = iota((LANES, width), 1)
    spread = (row < 2 * H) & (column >= first) & (column < first + HD)
    return jnp.dot(
        both, jnp.where(spread, 1.0, 0.0).astype(jnp.bfloat16), preferred_element_type=jnp.float32
    )


def finish_kernel(
    half, slot_count, chunk, side_ref, live_ref, groups_ref, own_ref, other_ref,
    low_ref, high_ref, low_lse_ref, high_lse_ref, w_hbm, out_ref, w_ref, sems
):
    n, width = out_ref.shape
    copies = []
    for i in range(width // chunk):
        cols = pl.ds(i * chunk, chunk)
        copy = pltpu.make_async_copy(w_hbm.at[:, cols], w_ref.at[:, cols], sems.at[i])
        copy.start()
        copies.append(copy)
    slot, upper = slots_of(groups_ref[...], half, slot_count)
    slot, upper = as_column(slot), as_column(upper)
    hit = slot == iota((n, n), 1)
    side = side_ref[0]
    own = jnp.where(hit & (upper == side), 1.0, 0.0).astype(jnp.bfloat16)
    other = jnp.where(hit & (upper != side), 1.0, 0.0).astype(jnp.bfloat16)
    pick = jnp.concatenate([own, other], axis=1)

    def picked(cols):
        both = jnp.concatenate([own_ref[:, cols], other_ref[:, cols]], axis=0)
        return jnp.dot(pick, both, preferred_element_type=jnp.float32)

    pieces = picked(slice(width, width + LANES))
    lane = iota((n, LANES), 1)
    prefix_lse = (
        pieces + pltpu.roll(pieces, LANES - H, 1) + pltpu.roll(pieces, LANES - 2 * H, 1)
    )
    prefix_lse = jnp.where(lane < H, prefix_lse, 0.0)
    private_lse = jnp.where(
        lane < H // 2, low_lse_ref[...], pltpu.roll(high_lse_ref[...], H // 2, 1)
    )
    private_lse = jnp.where(lane < H, private_lse, 0.0)
    top = jnp.maximum(prefix_lse, private_lse)
    a, b = jnp.exp(prefix_lse - top), jnp.exp(private_lse - top)
    prefix_share = expand_heads(a / (a + b), width)
    private_share = expand_heads(b / (a + b), width)
    private = jnp.concatenate([low_ref[...], high_ref[...]], axis=1)
    attended = prefix_share * picked(slice(0, width)) + private_share * private
    attended = attended.astype(jnp.bfloat16)
    is_live = iota((n, 1), 0) < live_ref[0]
    for i, copy in enumerate(copies):
        copy.wait()
        cols = slice(i * chunk, (i + 1) * chunk)
        projected = jnp.dot(attended, w_ref[:, cols], preferred_element_type=jnp.float32)
        out_ref[:, cols] = jnp.where(is_live, projected, 0.0).astype(out_ref.dtype)


def finish(side, live, groups, own, other, low, high, low_lse, high_lse, weight, half, slot_count):
    n = own.shape[0]
    width = weight.shape[1]
    chunk = 512
    return pl.pallas_call(
        functools.partial(finish_kernel, half, slot_count, chunk),
        out_shape=jax.ShapeDtypeStruct((n, width), jnp.bfloat16),
        in_specs=[SMEM, SMEM] + [VMEM] * 7 + [ANY],
        out_specs=VMEM,
        scratch_shapes=[
            pltpu.VMEM(weight.shape, weight.dtype),
            pltpu.SemaphoreType.DMA((width // chunk,)),
        ],
        compiler_params=params(32),
        cost_estimate=pl.CostEstimate(
            flops=2 * n * width * width, bytes_accessed=2 * width * width, transcendentals=0
        ),
        name="finish",
    )(side, live, groups, own, other, low, high, low_lse, high_lse, weight)


def per_device(
    queries,
    prefix_keys,
    prefix_values,
    pool_keys,
    pool_values,
    page_table,
    private_length,
    group_ids,
    live_rows,
    out_weight,
):
    devices = lax.axis_size("req")
    half = devices // 2
    row_count, width = queries.shape
    slot_count = 2 * row_count // devices
    page_size = pool_keys.shape[1]
    halves = [list(range(half)), list(range(half, devices))]
    across = [(i, (i + half) % devices) for i in range(devices)]
    side = (lax.axis_index("req") // half).astype(jnp.int32).reshape(1)

    groups = group_ids.reshape(1, row_count)
    lengths = private_length.reshape(1, row_count)
    pages = page_table.T
    flat_keys = pool_keys.reshape(-1, pool_keys.shape[2])
    flat_values = pool_values.reshape(-1, pool_values.shape[2])

    def exchange(rows):
        blocks = rows.reshape(half, slot_count, rows.shape[1])
        blocks = lax.all_to_all(
            blocks, "req", split_axis=0, concat_axis=0, tiled=True, axis_index_groups=halves
        )
        return blocks.reshape(rows.shape)

    far_keys = lax.ppermute(prefix_keys, "req", across)
    far_values = lax.ppermute(prefix_values, "req", across)
    own, other = place(queries, groups, side, half, slot_count)
    own_rows, other_rows = exchange(own), exchange(other)
    private = functools.partial(
        private_part, queries, flat_keys, flat_values, pages, lengths
    )
    low, low_lse = private(own, page_size, 0, KVH // 2)
    own_out = prefix_part(own_rows, prefix_keys, prefix_values, low_lse)
    own_back = exchange(own_out)
    other_out = prefix_part(other_rows, far_keys, far_values, own_out)
    other_back = exchange(other_out)
    high, high_lse = private(other_out, page_size, KVH // 2, KVH // 2)
    return finish(
        side, live_rows, groups, own_back, other_back, low, high, low_lse, high_lse,
        out_weight, half, slot_count,
    )


def solution(mesh):
    placed = (
        P("req", None),
        P("req", None),
        P("req", None),
        P("req", None, None),
        P("req", None, None),
        P("req", None),
        P("req"),
        P("req", None),
        P("req"),
        P(),
    )
    return jax.shard_map(
        per_device, mesh=mesh, in_specs=placed, out_specs=P("req", None), check_vma=False
    )
```

```python
import functools
import math

import jax
import jax.numpy as jnp
from jax import lax
from jax.experimental import pallas as pl
from jax.experimental.pallas import tpu as pltpu
from jax.sharding import PartitionSpec as P

H = 32
KVH = 8
HD = 80
GROUP = H // KVH
LANES = 128
WIN = 256
SCALE = HD ** (-0.5) * math.log2(math.e)
LN2 = math.log(2.0)
NEVER = -1e30
VMEM = pl.BlockSpec(memory_space=pltpu.VMEM)
SMEM = pl.BlockSpec(memory_space=pltpu.SMEM)
ANY = pl.BlockSpec(memory_space=pl.ANY)


def window(start, width):
    base = min(start // LANES * LANES, width - WIN)
    return base, start - base


def iota(shape, axis):
    return lax.broadcasted_iota(jnp.int32, shape, axis)


def params(mib):
    return pltpu.CompilerParams(vmem_limit_bytes=mib * 1024 * 1024)


def transpose_into(target, source):
    rows, cols = source.shape
    for c in range(0, cols, LANES):
        for r in range(0, rows, LANES):
            target[c : c + LANES, r : r + LANES] = source[r : r + LANES, c : c + LANES].T


def as_column(row):
    n = row.shape[1]
    same = iota((n, n), 0) == iota((n, n), 1)
    return jnp.sum(jnp.where(same, row, 0), axis=1, keepdims=True)


def slots_of(groups, half, slot_count):
    n = groups.shape[1]
    earlier = iota((n, n), 0) < iota((n, n), 1)
    same = (as_column(groups) == groups) & earlier
    rank = jnp.sum(jnp.where(same, 1, 0), axis=0, keepdims=True)
    upper = jnp.where(groups >= half, 1, 0)
    return (groups - upper * half) * slot_count + rank, upper


def place_kernel(half, slot_count, side_ref, groups_ref, q_hbm, out_ref, q_ref, sems):
    n, width = q_ref.shape
    chunk = width // sems.shape[0]
    copies = []
    for i in range(sems.shape[0]):
        cols = pl.ds(i * chunk, chunk)
        copies.append(pltpu.make_async_copy(q_hbm.at[:, cols], q_ref.at[:, cols], sems.at[i]))
        copies[i].start()
    slot, upper = slots_of(groups_ref[...], half, slot_count)
    hit = slot == iota((n, n), 0)
    side = side_ref[0]
    own = jnp.where(hit & (upper == side), 1.0, 0.0).astype(jnp.bfloat16)
    other = jnp.where(hit & (upper != side), 1.0, 0.0).astype(jnp.bfloat16)
    spread = jnp.concatenate([own, other], axis=0)
    for i, copy in enumerate(copies):
        copy.wait()
        cols = slice(i * chunk, (i + 1) * chunk)
        both = jnp.dot(spread, q_ref[:, cols], preferred_element_type=jnp.float32)
        both = both.astype(jnp.bfloat16)
        out_ref[:, i * chunk : (i + 1) * chunk] = both[:n]
        out_ref[:, width + i * chunk : width + (i + 1) * chunk] = both[n:]


def place(queries, groups, side, half, slot_count):
    n, width = queries.shape
    return pl.pallas_call(
        functools.partial(place_kernel, half, slot_count),
        out_shape=jax.ShapeDtypeStruct((n, 2 * width), queries.dtype),
        in_specs=[SMEM, VMEM, ANY],
        out_specs=VMEM,
        scratch_shapes=[pltpu.VMEM((n, width), queries.dtype), pltpu.SemaphoreType.DMA((4,))],
        compiler_params=params(48),
        cost_estimate=pl.CostEstimate(
            flops=4 * n * n * width, bytes_accessed=6 * n * width, transcendentals=0
        ),
        name="place",
    )(side, groups, queries)


def place_queries(qs_ref, i, qt_ref, k, key_width):
    n = qt_ref.shape[1]
    _, first = window(k * HD, key_width)
    if first:
        qs_ref[i, :first] = jnp.zeros((first, GROUP * n), jnp.bfloat16)
    if first + HD < WIN:
        qs_ref[i, first + HD :] = jnp.zeros((WIN - first - HD, GROUP * n), jnp.bfloat16)
    for g in range(GROUP):
        row = (i * GROUP + g) * HD
        qs_ref[i, first : first + HD, g * n : (g + 1) * n] = qt_ref[row : row + HD]


def prefix_kernel(
    part, rows_ref, k_ref, v_ref, before_ref, out_ref, qt_ref, vt_ref, qs_ref, ot_ref, lse_ref
):
    n, width = rows_ref.shape
    width //= 2
    key_width = k_ref.shape[1]
    transpose_into(qt_ref, rows_ref.at[:, part * width : (part + 1) * width])
    if part:
        out_ref[:, : width + LANES] = before_ref[...]
    out_ref = out_ref.at[:, part * (width + LANES) : (part + 1) * (width + LANES)]
    transpose_into(vt_ref, v_ref)
    for k in range(KVH):
        place_queries(qs_ref, k, qt_ref, k, key_width)
    for k in range(KVH):
        base, _ = window(k * HD, key_width)
        scores = jnp.dot(
            k_ref[:, base : base + WIN], qs_ref[k], preferred_element_type=jnp.float32
        )
        scores = scores * SCALE
        top = jnp.max(scores, axis=0, keepdims=True)
        weights = jnp.exp2(scores - top)
        total = jnp.sum(weights, axis=0, keepdims=True)
        summed = jnp.dot(
            vt_ref[k * HD : (k + 1) * HD],
            weights.astype(jnp.bfloat16),
            preferred_element_type=jnp.float32,
        )
        result = (summed * (1.0 / total)).astype(jnp.bfloat16)
        lse = (top + jnp.log2(total)) * LN2
        for g in range(GROUP):
            head = k * GROUP + g
            ot_ref[head * HD : (head + 1) * HD] = result[:, g * n : (g + 1) * n]
            lse_ref[head : head + 1] = lse[:, g * n : (g + 1) * n]
    transpose_into(out_ref.at[:, :width], ot_ref)
    lse = lse_ref[...]
    high = lse.astype(jnp.bfloat16).astype(jnp.float32)
    middle = (lse - high).astype(jnp.bfloat16).astype(jnp.float32)
    pieces = jnp.concatenate([high, middle, lse - high - middle, jnp.zeros_like(lse)], axis=0)
    out_ref[:, width:] = pieces.T.astype(jnp.bfloat16)


def prefix_part(part, rows, keys, values, before):
    n, width = rows.shape
    width //= 2
    tokens, key_width = keys.shape
    return pl.pallas_call(
        functools.partial(prefix_kernel, part),
        out_shape=jax.ShapeDtypeStruct((n, (part + 1) * (width + LANES)), jnp.bfloat16),
        in_specs=[VMEM, VMEM, VMEM, VMEM if part else ANY],
        out_specs=VMEM,
        scratch_shapes=[
            pltpu.VMEM((width, n), jnp.bfloat16),
            pltpu.VMEM((key_width, tokens), jnp.bfloat16),
            pltpu.VMEM((KVH, WIN, GROUP * n), jnp.bfloat16),
            pltpu.VMEM((width, n), jnp.bfloat16),
            pltpu.VMEM((H, n), jnp.float32),
        ],
        compiler_params=params(24),
        cost_estimate=pl.CostEstimate(
            flops=8000 * n * 256 * width, bytes_accessed=4 * n * width * 2, transcendentals=n * 256 * H
        ),
        name="prefix",
    )(rows, keys, values, before)


def fill_bias(bias_ref, pages, lengths, page_size):
    most, n = pages.shape
    page_count = bias_ref.shape[0] // page_size
    page = iota((page_count, n), 0)
    full = jnp.zeros((page_count, n), jnp.float32)
    partial = jnp.zeros((page_count, n), jnp.float32)
    for j in range(most):
        same = pages[j : j + 1] == page
        whole = lengths >= (j + 1) * page_size
        some = (lengths > j * page_size) & (lengths < (j + 1) * page_size)
        full += jnp.where(same & whole, 1.0, 0.0)
        partial += jnp.where(same & some, 1.0, 0.0)
    seen = jnp.where(iota((page_size, n), 0) < lengths % page_size, 1.0, 0.0)
    for p in range(page_count):
        multiple = full[p : p + 1] + seen * partial[p : p + 1]
        bias_ref[p * page_size : (p + 1) * page_size] = jnp.where(
            multiple > 0.0, jnp.log2(jnp.maximum(multiple, 1.0)), NEVER
        )


def private_kernel(
    first_head, heads, page_size, q_hbm, k_hbm, v_hbm, pages_ref, lengths_ref, after_ref,
    out_ref, lse_ref, q_ref, k_ref, v_ref, qt_ref, vt_ref, qs_ref, bias_ref, ot_ref, lses_ref,
    scores_a, scores_b, top_a, top_b, weights_ref, sems
):
    del after_ref
    copies = [
        pltpu.make_async_copy(source, target, sems.at[i])
        for i, (source, target) in enumerate(((q_hbm, q_ref), (k_hbm, k_ref), (v_hbm, v_ref)))
    ]
    for copy in copies:
        copy.start()
    n = q_ref.shape[0]
    tokens, key_width = k_ref.shape
    rows = GROUP * n
    tile = 256
    fill_bias(bias_ref, pages_ref[...], lengths_ref[...], page_size)
    copies[0].wait()
    query0 = first_head * GROUP * HD
    transpose_into(qt_ref, q_ref.at[:, query0 : query0 + heads * GROUP * HD])
    for i in range(heads):
        place_queries(qs_ref, i, qt_ref, first_head + i, key_width)
    copies[1].wait()

    def score(i, scores_ref, top_ref):
        k = first_head + i
        base = pl.multiple_of(jnp.minimum(k * HD // LANES * LANES, key_width - WIN), LANES)
        top = None
        for t in range(0, tokens, tile):
            scores = jnp.dot(
                k_ref[t : t + tile, pl.ds(base, WIN)],
                qs_ref[i],
                preferred_element_type=jnp.float32,
            )
            bias = bias_ref[t : t + tile]
            scores = scores * SCALE + jnp.concatenate([bias] * GROUP, axis=1)
            scores_ref[t : t + tile] = scores
            highest = jnp.max(scores.reshape(tile // 8, 8, rows), axis=0)
            top = highest if top is None else jnp.maximum(top, highest)
        top_ref[...] = top

    def weigh(i, scores_ref, top_ref, lses):
        top = jnp.max(top_ref[...], axis=0, keepdims=True)
        total = jnp.zeros((8, rows), jnp.float32)
        for t in range(0, tokens, tile):
            weights = jnp.exp2(scores_ref[t : t + tile] - top)
            total += jnp.sum(weights.reshape(tile // 8, 8, rows), axis=0)
            weights_ref[t : t + tile] = weights.astype(jnp.bfloat16)
        total = jnp.sum(total, axis=0, keepdims=True)
        values = vt_ref[pl.ds(pl.multiple_of((first_head + i) * HD, 16), HD)]
        summed = jnp.dot(values, weights_ref[...], preferred_element_type=jnp.float32)
        result = summed * (1.0 / total)
        lse = (top + jnp.log2(total)) * LN2
        row = iota(lses.shape, 0)
        for g in range(GROUP):
            head = i * GROUP + g
            ot_ref[pl.ds(pl.multiple_of(head * HD, 16), HD)] = result[:, g * n : (g + 1) * n]
            lses = jnp.where(row == head, lse[:, g * n : (g + 1) * n], lses)
        return lses

    score(0, scores_a, top_a)
    copies[2].wait()
    value0 = first_head * HD // LANES * LANES
    value1 = -(-(first_head + heads) * HD // LANES) * LANES
    transpose_into(vt_ref.at[value0:value1], v_ref.at[:, value0:value1])

    def two(j, lses):
        i = 2 * j
        score(i + 1, scores_b, top_b)
        lses = weigh(i, scores_a, top_a, lses)
        score(jnp.minimum(i + 2, heads - 1), scores_a, top_a)
        return weigh(i + 1, scores_b, top_b, lses)

    lses_ref[...] = jnp.zeros_like(lses_ref)
    lses_ref[:H] = lax.fori_loop(0, heads // 2, two, jnp.zeros((H, n), jnp.float32))
    lse_ref[...] = lses_ref[...].T
    transpose_into(out_ref, ot_ref)


def private_part(queries, keys, values, pages, lengths, after, page_size, first_head, heads):
    n = queries.shape[0]
    tokens, key_width = keys.shape
    width = heads * GROUP * HD
    return pl.pallas_call(
        functools.partial(private_kernel, first_head, heads, page_size),
        out_shape=(
            jax.ShapeDtypeStruct((n, width), jnp.float32),
            jax.ShapeDtypeStruct((n, LANES), jnp.float32),
        ),
        in_specs=[ANY] * 3 + [VMEM] * 2 + [ANY],
        out_specs=(VMEM, VMEM),
        scratch_shapes=[
            pltpu.VMEM(queries.shape, queries.dtype),
            pltpu.VMEM(keys.shape, keys.dtype),
            pltpu.VMEM(values.shape, values.dtype),
            pltpu.VMEM((width, n), jnp.bfloat16),
            pltpu.VMEM((key_width, tokens), jnp.bfloat16),
            pltpu.VMEM((heads, WIN, GROUP * n), jnp.bfloat16),
            pltpu.VMEM((tokens, n), jnp.float32),
            pltpu.VMEM((width, n), jnp.float32),
            pltpu.VMEM((LANES, n), jnp.float32),
            pltpu.VMEM((tokens, GROUP * n), jnp.float32),
            pltpu.VMEM((tokens, GROUP * n), jnp.float32),
            pltpu.VMEM((8, GROUP * n), jnp.float32),
            pltpu.VMEM((8, GROUP * n), jnp.float32),
            pltpu.VMEM((tokens, GROUP * n), jnp.bfloat16),
            pltpu.SemaphoreType.DMA((3,)),
        ],
        compiler_params=params(48),
        cost_estimate=pl.CostEstimate(
            flops=1200 * n * tokens * heads * GROUP * WIN,
            bytes_accessed=4 * tokens * key_width,
            transcendentals=n * tokens * heads * GROUP,
        ),
        name="private",
    )(queries, keys, values, pages, lengths, after)


def expand_heads(share, width):
    n = share.shape[0]
    lane = iota((n, LANES), 1)
    share = jnp.where(lane < H, share, 0.0)
    high = share.astype(jnp.bfloat16).astype(jnp.float32)
    both = (high + pltpu.roll(share - high, H, 1)).astype(jnp.bfloat16)
    row = iota((LANES, width), 0)
    head = jnp.where(row >= H, row - H, row)
    first = head * HD
    column = iota((LANES, width), 1)
    spread = (row < 2 * H) & (column >= first) & (column < first + HD)
    return jnp.dot(
        both, jnp.where(spread, 1.0, 0.0).astype(jnp.bfloat16), preferred_element_type=jnp.float32
    )


def load_kernel(w_hbm, after_ref, w_ref, sems):
    del after_ref
    chunk = w_ref.shape[1] // sems.shape[0]
    copies = []
    for i in range(sems.shape[0]):
        cols = pl.ds(i * chunk, chunk)
        copies.append(pltpu.make_async_copy(w_hbm.at[:, cols], w_ref.at[:, cols], sems.at[i]))
        copies[i].start()
    for copy in copies:
        copy.wait()


def load(weight, after):
    return pl.pallas_call(
        load_kernel,
        out_shape=jax.ShapeDtypeStruct(weight.shape, weight.dtype),
        in_specs=[ANY, ANY],
        out_specs=VMEM,
        scratch_shapes=[pltpu.SemaphoreType.DMA((5,))],
        compiler_params=params(32),
        cost_estimate=pl.CostEstimate(
            flops=10**10, bytes_accessed=2 * weight.size * 2, transcendentals=0
        ),
        name="load",
    )(weight, after)


def finish_kernel(
    half, slot_count, side_ref, live_ref, groups_ref, back_ref, private_ref, private_lse_ref,
    w_ref, out_ref
):
    n, width = out_ref.shape
    part = width + LANES
    slot, upper = slots_of(groups_ref[...], half, slot_count)
    slot, upper = as_column(slot), as_column(upper)
    hit = slot == iota((n, n), 1)
    side = side_ref[0]
    own = jnp.where(hit & (upper == side), 1.0, 0.0).astype(jnp.bfloat16)
    other = jnp.where(hit & (upper != side), 1.0, 0.0).astype(jnp.bfloat16)
    pick = jnp.concatenate([own, other], axis=1)

    def picked(first, last):
        both = jnp.concatenate(
            [back_ref[:, first:last], back_ref[:, part + first : part + last]], axis=0
        )
        return jnp.dot(pick, both, preferred_element_type=jnp.float32)

    pieces = picked(width, part)
    lane = iota((n, LANES), 1)
    prefix_lse = (
        pieces + pltpu.roll(pieces, LANES - H, 1) + pltpu.roll(pieces, LANES - 2 * H, 1)
    )
    prefix_lse = jnp.where(lane < H, prefix_lse, 0.0)
    private_lse = private_lse_ref[...]
    top = jnp.maximum(prefix_lse, private_lse)
    a, b = jnp.exp(prefix_lse - top), jnp.exp(private_lse - top)
    prefix_share = expand_heads(a / (a + b), width)
    private_share = expand_heads(b / (a + b), width)
    attended = prefix_share * picked(0, width) + private_share * private_ref[...]
    attended = attended.astype(jnp.bfloat16)
    is_live = iota((n, 1), 0) < live_ref[0]
    for first in range(0, width, 512):
        projected = jnp.dot(
            attended, w_ref[:, first : first + 512], preferred_element_type=jnp.float32
        )
        out_ref[:, first : first + 512] = jnp.where(is_live, projected, 0.0).astype(out_ref.dtype)


def finish(side, live, groups, back, private, private_lse, weight, half, slot_count):
    n = back.shape[0]
    width = weight.shape[1]
    return pl.pallas_call(
        functools.partial(finish_kernel, half, slot_count),
        out_shape=jax.ShapeDtypeStruct((n, width), jnp.bfloat16),
        in_specs=[SMEM, SMEM] + [VMEM] * 5,
        out_specs=VMEM,
        compiler_params=params(24),
        cost_estimate=pl.CostEstimate(
            flops=2 * n * width * width, bytes_accessed=2 * width * width, transcendentals=0
        ),
        name="finish",
    )(side, live, groups, back, private, private_lse, weight)


def per_device(
    queries,
    prefix_keys,
    prefix_values,
    pool_keys,
    pool_values,
    page_table,
    private_length,
    group_ids,
    live_rows,
    out_weight,
):
    devices = lax.axis_size("req")
    half = devices // 2
    row_count, width = queries.shape
    slot_count = 2 * row_count // devices
    page_size = pool_keys.shape[1]
    halves = [list(range(half)), list(range(half, devices))]
    across = [(i, (i + half) % devices) for i in range(devices)]
    side = (lax.axis_index("req") // half).astype(jnp.int32).reshape(1)

    groups = group_ids.reshape(1, row_count)
    lengths = private_length.reshape(1, row_count)
    pages = page_table.T
    flat_keys = pool_keys.reshape(-1, pool_keys.shape[2])
    flat_values = pool_values.reshape(-1, pool_values.shape[2])

    def exchange(rows):
        blocks = rows.reshape(half, slot_count, rows.shape[1])
        blocks = lax.all_to_all(
            blocks, "req", split_axis=0, concat_axis=0, tiled=True, axis_index_groups=halves
        )
        return blocks.reshape(rows.shape)

    far_keys = lax.ppermute(prefix_keys, "req", across)
    far_values = lax.ppermute(prefix_values, "req", across)
    placed = place(queries, groups, side, half, slot_count)
    rows = exchange(placed)
    private, private_lse = private_part(
        queries, flat_keys, flat_values, pages, lengths, placed, page_size, 0, KVH
    )
    own_out = prefix_part(0, rows, prefix_keys, prefix_values, private_lse)
    out = prefix_part(1, rows, far_keys, far_values, own_out)
    back = exchange(out)
    weight = load(out_weight, out)
    return finish(
        side, live_rows, groups, back, private, private_lse, weight, half, slot_count
    )


def solution(mesh):
    placed = (
        P("req", None),
        P("req", None),
        P("req", None),
        P("req", None, None),
        P("req", None, None),
        P("req", None),
        P("req"),
        P("req", None),
        P("req"),
        P(),
    )
    return jax.shard_map(
        per_device, mesh=mesh, in_specs=placed, out_specs=P("req", None), check_vma=False
    )
```

```python
import functools
import math

import jax
import jax.numpy as jnp
from jax import lax
from jax.experimental import pallas as pl
from jax.experimental.pallas import tpu as pltpu
from jax.sharding import PartitionSpec as P

H = 32
KVH = 8
HD = 80
GROUP = H // KVH
LANES = 128
WIN = 256
SCALE = HD ** (-0.5) * math.log2(math.e)
LN2 = math.log(2.0)
NEVER = -1e30
VMEM = pl.BlockSpec(memory_space=pltpu.VMEM)
SMEM = pl.BlockSpec(memory_space=pltpu.SMEM)
ANY = pl.BlockSpec(memory_space=pl.ANY)


def window(start, width):
    base = min(start // LANES * LANES, width - WIN)
    return base, start - base


def iota(shape, axis):
    return lax.broadcasted_iota(jnp.int32, shape, axis)


def params(mib):
    return pltpu.CompilerParams(vmem_limit_bytes=mib * 1024 * 1024)


def transpose_into(target, source):
    rows, cols = source.shape
    for c in range(0, cols, LANES):
        for r in range(0, rows, LANES):
            target[c : c + LANES, r : r + LANES] = source[r : r + LANES, c : c + LANES].T


def as_column(row):
    n = row.shape[1]
    same = iota((n, n), 0) == iota((n, n), 1)
    return jnp.sum(jnp.where(same, row, 0), axis=1, keepdims=True)


def slots_of(groups, half, slot_count):
    n = groups.shape[1]
    earlier = iota((n, n), 0) < iota((n, n), 1)
    same = (as_column(groups) == groups) & earlier
    rank = jnp.sum(jnp.where(same, 1, 0), axis=0, keepdims=True)
    upper = jnp.where(groups >= half, 1, 0)
    return (groups - upper * half) * slot_count + rank, upper


def place_kernel(
    half, slot_count, side_ref, groups_ref, q_hbm, out_hbm, token_ref, q_ref, out_ref, in_sems, out_sems
):
    token_ref[...] = jnp.zeros_like(token_ref)
    n, width = q_ref.shape
    steps = in_sems.shape[0]
    chunk = width // steps
    arrivals = []
    for i in range(steps):
        cols = pl.ds(i * chunk, chunk)
        arrivals.append(pltpu.make_async_copy(q_hbm.at[:, cols], q_ref.at[:, cols], in_sems.at[i]))
        arrivals[i].start()
    slot, upper = slots_of(groups_ref[...], half, slot_count)
    hit = slot == iota((n, n), 0)
    side = side_ref[0]
    own = jnp.where(hit & (upper == side), 1.0, 0.0).astype(jnp.bfloat16)
    other = jnp.where(hit & (upper != side), 1.0, 0.0).astype(jnp.bfloat16)
    spread = jnp.concatenate([own, other], axis=0)
    departures = []
    for i, arrival in enumerate(arrivals):
        arrival.wait()
        both = jnp.dot(
            spread, q_ref[:, i * chunk : (i + 1) * chunk], preferred_element_type=jnp.float32
        ).astype(jnp.bfloat16)
        for part in range(2):
            cols = pl.ds(part * width + i * chunk, chunk)
            out_ref[:, cols] = both[part * n : (part + 1) * n]
            departures.append(
                pltpu.make_async_copy(
                    out_ref.at[:, cols], out_hbm.at[:, cols], out_sems.at[2 * i + part]
                )
            )
            departures[-1].start()
    for departure in departures:
        departure.wait()


def place(queries, groups, side, half, slot_count):
    n, width = queries.shape
    steps = 4
    return pl.pallas_call(
        functools.partial(place_kernel, half, slot_count),
        out_shape=(
            jax.ShapeDtypeStruct((n, 2 * width), queries.dtype),
            jax.ShapeDtypeStruct((8, LANES), jnp.float32),
        ),
        in_specs=[SMEM, VMEM, ANY],
        out_specs=(ANY, VMEM),
        scratch_shapes=[
            pltpu.VMEM((n, width), queries.dtype),
            pltpu.VMEM((n, 2 * width), queries.dtype),
            pltpu.SemaphoreType.DMA((steps,)),
            pltpu.SemaphoreType.DMA((2 * steps,)),
        ],
        compiler_params=params(60),
        cost_estimate=pl.CostEstimate(
            flops=4 * n * n * width, bytes_accessed=6 * n * width, transcendentals=0
        ),
        name="place",
    )(side, groups, queries)


def clear_queries(qs_ref, i, k, key_width):
    _, first = window(k * HD, key_width)
    width = qs_ref.shape[2]
    if first:
        qs_ref[i, :first] = jnp.zeros((first, width), jnp.bfloat16)
    if first + HD < WIN:
        qs_ref[i, first + HD :] = jnp.zeros((WIN - first - HD, width), jnp.bfloat16)


def fill_queries(qs_ref, i, qt_ref, k, key_width):
    n = qt_ref.shape[1]
    _, first = window(k * HD, key_width)
    for g in range(GROUP):
        row = (k * GROUP + g) * HD
        qs_ref[i, first : first + HD, g * n : (g + 1) * n] = qt_ref[row : row + HD]


def prefix_kernel(
    rows_hbm, near_k, near_v, far_k, far_v, after_ref, out_hbm,
    rows_ref, k_ref, v_ref, qt_ref, vt_ref, qs_ref, ot_ref, lse_ref, scores_ref, out_ref,
    in_sems, out_sems
):
    del after_ref
    n, width = rows_ref.shape
    width //= 2
    part_width = width + LANES
    key_width = k_ref.shape[2]
    arrivals = []
    for part, (keys, values) in enumerate(((near_k, near_v), (far_k, far_v))):
        cols = pl.ds(part * width, width)
        for source, target in (
            (values, v_ref.at[part]),
            (rows_hbm.at[:, cols], rows_ref.at[:, cols]),
            (keys, k_ref.at[part]),
        ):
            arrivals.append(pltpu.make_async_copy(source, target, in_sems.at[len(arrivals)]))
            arrivals[-1].start()
    for u in range(2 * KVH):
        clear_queries(qs_ref, u, u % KVH, key_width)

    def prepare(part):
        arrivals[3 * part].wait()
        transpose_into(vt_ref.at[part], v_ref.at[part])
        arrivals[3 * part + 1].wait()
        transpose_into(qt_ref, rows_ref.at[:, part * width : (part + 1) * width])
        for k in range(KVH):
            fill_queries(qs_ref, part * KVH + k, qt_ref, k, key_width)
        arrivals[3 * part + 2].wait()

    def score(u):
        part, k = divmod(u, KVH)
        base, _ = window(k * HD, key_width)
        scores = jnp.dot(
            k_ref[part, :, base : base + WIN], qs_ref[u], preferred_element_type=jnp.float32
        )
        scores_ref[u % 2] = scores * SCALE

    def weigh(u):
        part, k = divmod(u, KVH)
        scores = scores_ref[u % 2]
        top = jnp.max(scores, axis=0, keepdims=True)
        weights = jnp.exp2(scores - top)
        total = jnp.sum(weights, axis=0, keepdims=True)
        summed = jnp.dot(
            vt_ref[part, k * HD : (k + 1) * HD],
            weights.astype(jnp.bfloat16),
            preferred_element_type=jnp.float32,
        )
        result = (summed * (1.0 / total)).astype(jnp.bfloat16)
        lse = (top + jnp.log2(total)) * LN2
        for g in range(GROUP):
            head = k * GROUP + g
            ot_ref[head * HD : (head + 1) * HD] = result[:, g * n : (g + 1) * n]
            lse_ref[head : head + 1] = lse[:, g * n : (g + 1) * n]

    def send(part):
        cols = pl.ds(part * part_width, part_width)
        view = out_ref.at[:, cols]
        transpose_into(view.at[:, :width], ot_ref)
        lse = lse_ref[...]
        high = lse.astype(jnp.bfloat16).astype(jnp.float32)
        middle = (lse - high).astype(jnp.bfloat16).astype(jnp.float32)
        pieces = jnp.concatenate([high, middle, lse - high - middle, jnp.zeros_like(lse)], axis=0)
        view[:, width:] = pieces.T.astype(jnp.bfloat16)
        copy = pltpu.make_async_copy(view, out_hbm.at[:, cols], out_sems.at[part])
        copy.start()
        return copy

    prepare(0)
    score(0)
    departures = []
    for u in range(2 * KVH):
        if u == KVH - 2:
            prepare(1)
        if u + 1 < 2 * KVH:
            score(u + 1)
        weigh(u)
        if u % KVH == KVH - 1:
            departures.append(send(u // KVH))
    for departure in departures:
        departure.wait()


def prefix_part(rows, near_k, near_v, far_k, far_v, after):
    n, width = rows.shape
    width //= 2
    tokens, key_width = near_k.shape
    return pl.pallas_call(
        prefix_kernel,
        out_shape=jax.ShapeDtypeStruct((n, 2 * (width + LANES)), jnp.bfloat16),
        in_specs=[ANY] * 6,
        out_specs=ANY,
        scratch_shapes=[
            pltpu.VMEM(rows.shape, rows.dtype),
            pltpu.VMEM((2, tokens, key_width), jnp.bfloat16),
            pltpu.VMEM((2, tokens, key_width), jnp.bfloat16),
            pltpu.VMEM((width, n), jnp.bfloat16),
            pltpu.VMEM((2, key_width, tokens), jnp.bfloat16),
            pltpu.VMEM((2 * KVH, WIN, GROUP * n), jnp.bfloat16),
            pltpu.VMEM((width, n), jnp.bfloat16),
            pltpu.VMEM((H, n), jnp.float32),
            pltpu.VMEM((2, tokens, GROUP * n), jnp.float32),
            pltpu.VMEM((n, 2 * (width + LANES)), jnp.bfloat16),
            pltpu.SemaphoreType.DMA((6,)),
            pltpu.SemaphoreType.DMA((2,)),
        ],
        compiler_params=params(60),
        cost_estimate=pl.CostEstimate(
            flops=16000 * n * 256 * width,
            bytes_accessed=8 * n * width * 2,
            transcendentals=n * 512 * H,
        ),
        name="prefix",
    )(rows, near_k, near_v, far_k, far_v, after)


def fill_bias(bias_ref, pages, lengths, page_size):
    most, n = pages.shape
    page_count = bias_ref.shape[0] // page_size
    page = iota((page_count, n), 0)
    full = jnp.zeros((page_count, n), jnp.float32)
    partial = jnp.zeros((page_count, n), jnp.float32)
    for j in range(most):
        same = pages[j : j + 1] == page
        whole = lengths >= (j + 1) * page_size
        some = (lengths > j * page_size) & (lengths < (j + 1) * page_size)
        full += jnp.where(same & whole, 1.0, 0.0)
        partial += jnp.where(same & some, 1.0, 0.0)
    seen = jnp.where(iota((page_size, n), 0) < lengths % page_size, 1.0, 0.0)
    for p in range(page_count):
        multiple = full[p : p + 1] + seen * partial[p : p + 1]
        bias_ref[p * page_size : (p + 1) * page_size] = jnp.where(
            multiple > 0.0, jnp.log2(jnp.maximum(multiple, 1.0)), NEVER
        )


def private_kernel(
    page_size, q_hbm, k_hbm, v_hbm, pages_ref, lengths_ref, after_ref,
    out_ref, lse_ref, q_ref, k_ref, v_ref, qt_ref, vt_ref, qs_ref, bias_ref, ot_ref, lses_ref,
    scores_a, scores_b, top_a, top_b, weights_ref, sems
):
    del after_ref
    copies = [
        pltpu.make_async_copy(source, target, sems.at[i])
        for i, (source, target) in enumerate(((q_hbm, q_ref), (k_hbm, k_ref), (v_hbm, v_ref)))
    ]
    for copy in copies:
        copy.start()
    n = q_ref.shape[0]
    tokens, key_width = k_ref.shape
    rows = GROUP * n
    tile = 256
    fill_bias(bias_ref, pages_ref[...], lengths_ref[...], page_size)
    copies[0].wait()
    transpose_into(qt_ref, q_ref)
    for k in range(KVH):
        clear_queries(qs_ref, k, k, key_width)
        fill_queries(qs_ref, k, qt_ref, k, key_width)
    copies[1].wait()

    def score(k, scores_ref, top_ref):
        base = pl.multiple_of(jnp.minimum(k * HD // LANES * LANES, key_width - WIN), LANES)
        top = None
        for t in range(0, tokens, tile):
            scores = jnp.dot(
                k_ref[t : t + tile, pl.ds(base, WIN)],
                qs_ref[k],
                preferred_element_type=jnp.float32,
            )
            bias = bias_ref[t : t + tile]
            scores = scores * SCALE + jnp.concatenate([bias] * GROUP, axis=1)
            scores_ref[t : t + tile] = scores
            highest = jnp.max(scores.reshape(tile // 8, 8, rows), axis=0)
            top = highest if top is None else jnp.maximum(top, highest)
        top_ref[...] = top

    def weigh(k, scores_ref, top_ref, lses):
        top = jnp.max(top_ref[...], axis=0, keepdims=True)
        total = jnp.zeros((8, rows), jnp.float32)
        for t in range(0, tokens, tile):
            weights = jnp.exp2(scores_ref[t : t + tile] - top)
            total += jnp.sum(weights.reshape(tile // 8, 8, rows), axis=0)
            weights_ref[t : t + tile] = weights.astype(jnp.bfloat16)
        total = jnp.sum(total, axis=0, keepdims=True)
        values = vt_ref[pl.ds(pl.multiple_of(k * HD, 16), HD)]
        summed = jnp.dot(values, weights_ref[...], preferred_element_type=jnp.float32)
        result = summed * (1.0 / total)
        lse = (top + jnp.log2(total)) * LN2
        row = iota(lses.shape, 0)
        for g in range(GROUP):
            head = k * GROUP + g
            ot_ref[pl.ds(pl.multiple_of(head * HD, 16), HD)] = result[:, g * n : (g + 1) * n]
            lses = jnp.where(row == head, lse[:, g * n : (g + 1) * n], lses)
        return lses

    score(0, scores_a, top_a)
    copies[2].wait()
    transpose_into(vt_ref, v_ref)

    def two(j, lses):
        k = 2 * j
        score(k + 1, scores_b, top_b)
        lses = weigh(k, scores_a, top_a, lses)
        score(jnp.minimum(k + 2, KVH - 1), scores_a, top_a)
        return weigh(k + 1, scores_b, top_b, lses)

    lses_ref[...] = jnp.zeros_like(lses_ref)
    lses_ref[:H] = lax.fori_loop(0, KVH // 2, two, jnp.zeros((H, n), jnp.float32))
    lse_ref[...] = lses_ref[...].T
    transpose_into(out_ref, ot_ref)


def private_part(queries, keys, values, pages, lengths, after, page_size):
    n, width = queries.shape
    tokens, key_width = keys.shape
    return pl.pallas_call(
        functools.partial(private_kernel, page_size),
        out_shape=(
            jax.ShapeDtypeStruct((n, width), jnp.float32),
            jax.ShapeDtypeStruct((n, LANES), jnp.float32),
        ),
        in_specs=[ANY] * 3 + [VMEM] * 2 + [ANY],
        out_specs=(VMEM, VMEM),
        scratch_shapes=[
            pltpu.VMEM(queries.shape, queries.dtype),
            pltpu.VMEM(keys.shape, keys.dtype),
            pltpu.VMEM(values.shape, values.dtype),
            pltpu.VMEM((width, n), jnp.bfloat16),
            pltpu.VMEM((key_width, tokens), jnp.bfloat16),
            pltpu.VMEM((KVH, WIN, GROUP * n), jnp.bfloat16),
            pltpu.VMEM((tokens, n), jnp.float32),
            pltpu.VMEM((width, n), jnp.float32),
            pltpu.VMEM((LANES, n), jnp.float32),
            pltpu.VMEM((tokens, GROUP * n), jnp.float32),
            pltpu.VMEM((tokens, GROUP * n), jnp.float32),
            pltpu.VMEM((8, GROUP * n), jnp.float32),
            pltpu.VMEM((8, GROUP * n), jnp.float32),
            pltpu.VMEM((tokens, GROUP * n), jnp.bfloat16),
            pltpu.SemaphoreType.DMA((3,)),
        ],
        compiler_params=params(48),
        cost_estimate=pl.CostEstimate(
            flops=1200 * n * tokens * H * WIN,
            bytes_accessed=4 * tokens * key_width,
            transcendentals=n * tokens * H,
        ),
        name="private",
    )(queries, keys, values, pages, lengths, after)


def expand_heads(share, width):
    n = share.shape[0]
    lane = iota((n, LANES), 1)
    share = jnp.where(lane < H, share, 0.0)
    high = share.astype(jnp.bfloat16).astype(jnp.float32)
    both = (high + pltpu.roll(share - high, H, 1)).astype(jnp.bfloat16)
    row = iota((LANES, width), 0)
    head = jnp.where(row >= H, row - H, row)
    first = head * HD
    column = iota((LANES, width), 1)
    spread = (row < 2 * H) & (column >= first) & (column < first + HD)
    return jnp.dot(
        both, jnp.where(spread, 1.0, 0.0).astype(jnp.bfloat16), preferred_element_type=jnp.float32
    )


def finish_kernel(
    half, slot_count, side_ref, live_ref, groups_ref, back_ref, private_lse_ref, private_hbm, w_hbm,
    out_hbm, private_ref, w_ref, out_ref, in_sems, out_sems
):
    n, width = out_ref.shape
    part = width + LANES
    steps = out_sems.shape[0]
    chunk = width // steps
    private_copy = pltpu.make_async_copy(private_hbm, private_ref, in_sems.at[steps])
    private_copy.start()
    arrivals = []
    for i in range(steps):
        cols = pl.ds(i * chunk, chunk)
        arrivals.append(pltpu.make_async_copy(w_hbm.at[:, cols], w_ref.at[:, cols], in_sems.at[i]))
        arrivals[i].start()
    slot, upper = slots_of(groups_ref[...], half, slot_count)
    slot, upper = as_column(slot), as_column(upper)
    hit = slot == iota((n, n), 1)
    side = side_ref[0]
    own = jnp.where(hit & (upper == side), 1.0, 0.0).astype(jnp.bfloat16)
    other = jnp.where(hit & (upper != side), 1.0, 0.0).astype(jnp.bfloat16)
    pick = jnp.concatenate([own, other], axis=1)

    def picked(first, last):
        both = jnp.concatenate(
            [back_ref[:, first:last], back_ref[:, part + first : part + last]], axis=0
        )
        return jnp.dot(pick, both, preferred_element_type=jnp.float32)

    pieces = picked(width, part)
    lane = iota((n, LANES), 1)
    prefix_lse = (
        pieces + pltpu.roll(pieces, LANES - H, 1) + pltpu.roll(pieces, LANES - 2 * H, 1)
    )
    prefix_lse = jnp.where(lane < H, prefix_lse, 0.0)
    private_lse = private_lse_ref[...]
    top = jnp.maximum(prefix_lse, private_lse)
    a, b = jnp.exp(prefix_lse - top), jnp.exp(private_lse - top)
    prefix_share = expand_heads(a / (a + b), width)
    private_share = expand_heads(b / (a + b), width)
    prefix = picked(0, width)
    private_copy.wait()
    attended = prefix_share * prefix + private_share * private_ref[...]
    attended = attended.astype(jnp.bfloat16)
    is_live = iota((n, 1), 0) < live_ref[0]
    departures = []
    for i, arrival in enumerate(arrivals):
        arrival.wait()
        cols = pl.ds(i * chunk, chunk)
        projected = jnp.dot(attended, w_ref[:, cols], preferred_element_type=jnp.float32)
        out_ref[:, cols] = jnp.where(is_live, projected, 0.0).astype(out_ref.dtype)
        departures.append(
            pltpu.make_async_copy(out_ref.at[:, cols], out_hbm.at[:, cols], out_sems.at[i])
        )
        departures[i].start()
    for departure in departures:
        departure.wait()


def finish(side, live, groups, back, private, private_lse, weight, half, slot_count):
    n = back.shape[0]
    width = weight.shape[1]
    steps = 5
    return pl.pallas_call(
        functools.partial(finish_kernel, half, slot_count),
        out_shape=jax.ShapeDtypeStruct((n, width), jnp.bfloat16),
        in_specs=[SMEM, SMEM] + [VMEM] * 3 + [ANY] * 2,
        out_specs=ANY,
        scratch_shapes=[
            pltpu.VMEM((n, width), jnp.float32),
            pltpu.VMEM(weight.shape, weight.dtype),
            pltpu.VMEM((n, width), jnp.bfloat16),
            pltpu.SemaphoreType.DMA((steps + 1,)),
            pltpu.SemaphoreType.DMA((steps,)),
        ],
        compiler_params=params(52),
        cost_estimate=pl.CostEstimate(
            flops=2 * n * width * width, bytes_accessed=2 * width * width, transcendentals=0
        ),
        name="finish",
    )(side, live, groups, back, private_lse, private, weight)


def per_device(
    queries,
    prefix_keys,
    prefix_values,
    pool_keys,
    pool_values,
    page_table,
    private_length,
    group_ids,
    live_rows,
    out_weight,
):
    devices = lax.axis_size("req")
    half = devices // 2
    row_count, width = queries.shape
    slot_count = 2 * row_count // devices
    page_size = pool_keys.shape[1]
    halves = [list(range(half)), list(range(half, devices))]
    across = [(i, (i + half) % devices) for i in range(devices)]
    side = (lax.axis_index("req") // half).astype(jnp.int32).reshape(1)

    groups = group_ids.reshape(1, row_count)
    lengths = private_length.reshape(1, row_count)
    pages = page_table.T
    flat_keys = pool_keys.reshape(-1, pool_keys.shape[2])
    flat_values = pool_values.reshape(-1, pool_values.shape[2])

    def exchange(rows):
        blocks = rows.reshape(half, slot_count, rows.shape[1])
        blocks = lax.all_to_all(
            blocks, "req", split_axis=0, concat_axis=0, tiled=True, axis_index_groups=halves
        )
        return blocks.reshape(rows.shape)

    far_keys = lax.ppermute(prefix_keys, "req", across)
    far_values = lax.ppermute(prefix_values, "req", across)
    placed, token = place(queries, groups, side, half, slot_count)
    rows = exchange(placed)
    private, private_lse = private_part(
        queries, flat_keys, flat_values, pages, lengths, token, page_size
    )
    out = prefix_part(rows, prefix_keys, prefix_values, far_keys, far_values, private_lse)
    back = exchange(out)
    return finish(
        side, live_rows, groups, back, private, private_lse, out_weight, half, slot_count
    )


def solution(mesh):
    placed = (
        P("req", None),
        P("req", None),
        P("req", None),
        P("req", None, None),
        P("req", None, None),
        P("req", None),
        P("req"),
        P("req", None),
        P("req"),
        P(),
    )
    return jax.shard_map(
        per_device, mesh=mesh, in_specs=placed, out_specs=P("req", None), check_vma=False
    )
```

```python
import functools
import math

import jax
import jax.numpy as jnp
from jax import lax
from jax.experimental import pallas as pl
from jax.experimental.pallas import tpu as pltpu
from jax.sharding import PartitionSpec as P

H = 32
KVH = 8
HD = 80
GROUP = H // KVH
LANES = 128
WIN = 256
SCALE = HD ** (-0.5) * math.log2(math.e)
LN2 = math.log(2.0)
NEVER = -1e30
VMEM = pl.BlockSpec(memory_space=pltpu.VMEM)
SMEM = pl.BlockSpec(memory_space=pltpu.SMEM)
ANY = pl.BlockSpec(memory_space=pl.ANY)


def window(start, width):
    base = min(start // LANES * LANES, width - WIN)
    return base, start - base


def iota(shape, axis):
    return lax.broadcasted_iota(jnp.int32, shape, axis)


def params(mib):
    return pltpu.CompilerParams(vmem_limit_bytes=mib * 1024 * 1024)


def transpose_into(target, source):
    rows, cols = source.shape
    for c in range(0, cols, LANES):
        for r in range(0, rows, LANES):
            target[c : c + LANES, r : r + LANES] = source[r : r + LANES, c : c + LANES].T


def as_column(row):
    n = row.shape[1]
    same = iota((n, n), 0) == iota((n, n), 1)
    return jnp.sum(jnp.where(same, row, 0), axis=1, keepdims=True)


def slots_of(groups, half, slot_count):
    n = groups.shape[1]
    earlier = iota((n, n), 0) < iota((n, n), 1)
    same = (as_column(groups) == groups) & earlier
    rank = jnp.sum(jnp.where(same, 1, 0), axis=0, keepdims=True)
    upper = jnp.where(groups >= half, 1, 0)
    return (groups - upper * half) * slot_count + rank, upper


def place_kernel(
    half, slot_count, groups_hbm, q_hbm, out_ref, token_ref, groups_ref, q_ref,
    group_sem, in_sems
):
    n, width = q_ref.shape
    steps = in_sems.shape[0]
    chunk = width // steps
    groups_copy = pltpu.make_async_copy(groups_hbm, groups_ref, group_sem)
    groups_copy.start()
    arrivals = []
    for i in range(steps):
        cols = pl.ds(i * chunk, chunk)
        arrivals.append(pltpu.make_async_copy(q_hbm.at[:, cols], q_ref.at[:, cols], in_sems.at[i]))
        arrivals[i].start()
    token_ref[...] = jnp.zeros_like(token_ref)
    side = lax.axis_index("req") // half
    groups_copy.wait()
    slot, upper = slots_of(groups_ref[...], half, slot_count)
    hit = slot == iota((n, n), 0)
    own = jnp.where(hit & (upper == side), 1.0, 0.0).astype(jnp.bfloat16)
    other = jnp.where(hit & (upper != side), 1.0, 0.0).astype(jnp.bfloat16)
    spread = jnp.concatenate([own, other], axis=0)
    for i, arrival in enumerate(arrivals):
        arrival.wait()
        both = jnp.dot(
            spread, q_ref[:, i * chunk : (i + 1) * chunk], preferred_element_type=jnp.float32
        ).astype(jnp.bfloat16)
        for part in range(2):
            cols = pl.ds(part * width + i * chunk, chunk)
            out_ref[:, cols] = both[part * n : (part + 1) * n]


def place(queries, groups, half, slot_count):
    n, width = queries.shape
    steps = 2
    return pl.pallas_call(
        functools.partial(place_kernel, half, slot_count),
        out_shape=(
            jax.ShapeDtypeStruct((n, 2 * width), queries.dtype),
            jax.ShapeDtypeStruct((8, LANES), jnp.float32),
        ),
        in_specs=[ANY, ANY],
        out_specs=(VMEM, VMEM),
        scratch_shapes=[
            pltpu.VMEM(groups.shape, groups.dtype),
            pltpu.VMEM((n, width), queries.dtype),
            pltpu.SemaphoreType.DMA(()),
            pltpu.SemaphoreType.DMA((steps,)),
        ],
        compiler_params=params(60),
        cost_estimate=pl.CostEstimate(
            flops=4 * n * n * width, bytes_accessed=6 * n * width, transcendentals=0
        ),
        name="place",
    )(groups, queries)


def clear_queries(qs_ref, i, k, key_width):
    _, first = window(k * HD, key_width)
    width = qs_ref.shape[2]
    if first:
        qs_ref[i, :first] = jnp.zeros((first, width), jnp.bfloat16)
    if first + HD < WIN:
        qs_ref[i, first + HD :] = jnp.zeros((WIN - first - HD, width), jnp.bfloat16)


def fill_queries(qs_ref, i, qt_ref, k, key_width):
    n = qt_ref.shape[1]
    _, first = window(k * HD, key_width)
    for g in range(GROUP):
        row = (k * GROUP + g) * HD
        qs_ref[i, first : first + HD, g * n : (g + 1) * n] = qt_ref[row : row + HD]


def prefix_kernel(
    rows_hbm, near_k, near_v, far_k, far_v, after_ref, out_hbm,
    rows_ref, k_ref, v_ref, qt_ref, vt_ref, qs_ref, ot_ref, lse_ref, scores_ref, out_ref,
    in_sems, out_sems
):
    del after_ref
    n, width = rows_ref.shape
    width //= 2
    part_width = width + LANES
    key_width = k_ref.shape[2]
    arrivals = []
    for part, (keys, values) in enumerate(((near_k, near_v), (far_k, far_v))):
        cols = pl.ds(part * width, width)
        for source, target in (
            (values, v_ref.at[part]),
            (rows_hbm.at[:, cols], rows_ref.at[:, cols]),
            (keys, k_ref.at[part]),
        ):
            arrivals.append(pltpu.make_async_copy(source, target, in_sems.at[len(arrivals)]))
            arrivals[-1].start()
    for u in range(2 * KVH):
        clear_queries(qs_ref, u, u % KVH, key_width)

    def prepare(part):
        arrivals[3 * part].wait()
        transpose_into(vt_ref.at[part], v_ref.at[part])
        arrivals[3 * part + 1].wait()
        transpose_into(qt_ref, rows_ref.at[:, part * width : (part + 1) * width])
        for k in range(KVH):
            fill_queries(qs_ref, part * KVH + k, qt_ref, k, key_width)
        arrivals[3 * part + 2].wait()

    def score(u):
        part, k = divmod(u, KVH)
        base, _ = window(k * HD, key_width)
        scores = jnp.dot(
            k_ref[part, :, base : base + WIN], qs_ref[u], preferred_element_type=jnp.float32
        )
        scores_ref[u % 2] = scores * SCALE

    def weigh(u):
        part, k = divmod(u, KVH)
        scores = scores_ref[u % 2]
        top = jnp.max(scores, axis=0, keepdims=True)
        weights = jnp.exp2(scores - top)
        total = jnp.sum(weights, axis=0, keepdims=True)
        summed = jnp.dot(
            vt_ref[part, k * HD : (k + 1) * HD],
            weights.astype(jnp.bfloat16),
            preferred_element_type=jnp.float32,
        )
        result = (summed * (1.0 / total)).astype(jnp.bfloat16)
        lse = (top + jnp.log2(total)) * LN2
        for g in range(GROUP):
            head = k * GROUP + g
            ot_ref[head * HD : (head + 1) * HD] = result[:, g * n : (g + 1) * n]
            lse_ref[head : head + 1] = lse[:, g * n : (g + 1) * n]

    def depart(cols):
        departures.append(
            pltpu.make_async_copy(
                out_ref.at[:, cols], out_hbm.at[:, cols], out_sems.at[len(departures)]
            )
        )
        departures[-1].start()

    def send(u):
        part, k = divmod(u, KVH)
        quarter = width // 4
        first = k // 2 * quarter
        cols = pl.ds(part * part_width + first, quarter)
        transpose_into(out_ref.at[:, cols], ot_ref.at[first : first + quarter])
        depart(cols)
        if k < KVH - 1:
            return
        lse = lse_ref[...]
        high = lse.astype(jnp.bfloat16).astype(jnp.float32)
        middle = (lse - high).astype(jnp.bfloat16).astype(jnp.float32)
        pieces = jnp.concatenate([high, middle, lse - high - middle, jnp.zeros_like(lse)], axis=0)
        cols = pl.ds(part * part_width + width, LANES)
        out_ref[:, cols] = pieces.T.astype(jnp.bfloat16)
        depart(cols)

    departures = []
    prepare(0)
    score(0)
    for u in range(2 * KVH):
        if u == KVH - 2:
            prepare(1)
        if u + 1 < 2 * KVH:
            score(u + 1)
        weigh(u)
        if u % 2:
            send(u)
    for departure in departures:
        departure.wait()


def prefix_part(rows, near_k, near_v, far_k, far_v, after):
    n, width = rows.shape
    width //= 2
    tokens, key_width = near_k.shape
    return pl.pallas_call(
        prefix_kernel,
        out_shape=jax.ShapeDtypeStruct((n, 2 * (width + LANES)), jnp.bfloat16),
        in_specs=[ANY] * 6,
        out_specs=ANY,
        scratch_shapes=[
            pltpu.VMEM(rows.shape, rows.dtype),
            pltpu.VMEM((2, tokens, key_width), jnp.bfloat16),
            pltpu.VMEM((2, tokens, key_width), jnp.bfloat16),
            pltpu.VMEM((width, n), jnp.bfloat16),
            pltpu.VMEM((2, key_width, tokens), jnp.bfloat16),
            pltpu.VMEM((2 * KVH, WIN, GROUP * n), jnp.bfloat16),
            pltpu.VMEM((width, n), jnp.bfloat16),
            pltpu.VMEM((H, n), jnp.float32),
            pltpu.VMEM((2, tokens, GROUP * n), jnp.float32),
            pltpu.VMEM((n, 2 * (width + LANES)), jnp.bfloat16),
            pltpu.SemaphoreType.DMA((6,)),
            pltpu.SemaphoreType.DMA((10,)),
        ],
        compiler_params=params(24),
        cost_estimate=pl.CostEstimate(
            flops=16000 * n * 256 * width,
            bytes_accessed=8 * n * width * 2,
            transcendentals=n * 512 * H,
        ),
        name="prefix",
    )(rows, near_k, near_v, far_k, far_v, after)


def fill_bias(bias_ref, pages, lengths, page_size):
    most, n = pages.shape
    page_count = bias_ref.shape[0] // page_size
    page = iota((page_count, n), 0)
    full = jnp.zeros((page_count, n), jnp.float32)
    partial = jnp.zeros((page_count, n), jnp.float32)
    for j in range(most):
        same = pages[j : j + 1] == page
        whole = lengths >= (j + 1) * page_size
        some = (lengths > j * page_size) & (lengths < (j + 1) * page_size)
        full += jnp.where(same & whole, 1.0, 0.0)
        partial += jnp.where(same & some, 1.0, 0.0)
    seen = jnp.where(iota((page_size, n), 0) < lengths % page_size, 1.0, 0.0)
    for p in range(page_count):
        multiple = full[p : p + 1] + seen * partial[p : p + 1]
        bias_ref[p * page_size : (p + 1) * page_size] = jnp.where(
            multiple > 0.0, jnp.log2(jnp.maximum(multiple, 1.0)), NEVER
        )


def private_kernel(
    page_size, q_hbm, k_hbm, v_hbm, pages_ref, lengths_ref, after_ref,
    out_ref, lse_ref, q_ref, k_ref, v_ref, qt_ref, vt_ref, qs_ref, bias_ref, ot_ref, lses_ref,
    scores_a, scores_b, top_a, top_b, weights_ref, sems
):
    del after_ref
    copies = [
        pltpu.make_async_copy(source, target, sems.at[i])
        for i, (source, target) in enumerate(((q_hbm, q_ref), (k_hbm, k_ref), (v_hbm, v_ref)))
    ]
    for copy in copies:
        copy.start()
    n = q_ref.shape[0]
    tokens, key_width = k_ref.shape
    rows = GROUP * n
    tile = 256
    fill_bias(bias_ref, pages_ref[...], lengths_ref[...], page_size)
    copies[0].wait()
    transpose_into(qt_ref, q_ref)
    for k in range(KVH):
        clear_queries(qs_ref, k, k, key_width)
        fill_queries(qs_ref, k, qt_ref, k, key_width)
    copies[1].wait()

    def score(k, scores_ref, top_ref):
        base = pl.multiple_of(jnp.minimum(k * HD // LANES * LANES, key_width - WIN), LANES)
        top = None
        for t in range(0, tokens, tile):
            scores = jnp.dot(
                k_ref[t : t + tile, pl.ds(base, WIN)],
                qs_ref[k],
                preferred_element_type=jnp.float32,
            )
            bias = bias_ref[t : t + tile]
            scores = scores * SCALE + jnp.concatenate([bias] * GROUP, axis=1)
            scores_ref[t : t + tile] = scores
            highest = jnp.max(scores.reshape(tile // 8, 8, rows), axis=0)
            top = highest if top is None else jnp.maximum(top, highest)
        top_ref[...] = top

    def weigh(k, scores_ref, top_ref, lses):
        top = jnp.max(top_ref[...], axis=0, keepdims=True)
        total = jnp.zeros((8, rows), jnp.float32)
        for t in range(0, tokens, tile):
            weights = jnp.exp2(scores_ref[t : t + tile] - top)
            total += jnp.sum(weights.reshape(tile // 8, 8, rows), axis=0)
            weights_ref[t : t + tile] = weights.astype(jnp.bfloat16)
        total = jnp.sum(total, axis=0, keepdims=True)
        values = vt_ref[pl.ds(pl.multiple_of(k * HD, 16), HD)]
        summed = jnp.dot(values, weights_ref[...], preferred_element_type=jnp.float32)
        result = summed * (1.0 / total)
        lse = (top + jnp.log2(total)) * LN2
        row = iota(lses.shape, 0)
        for g in range(GROUP):
            head = k * GROUP + g
            ot_ref[pl.ds(pl.multiple_of(head * HD, 16), HD)] = result[:, g * n : (g + 1) * n]
            lses = jnp.where(row == head, lse[:, g * n : (g + 1) * n], lses)
        return lses

    score(0, scores_a, top_a)
    copies[2].wait()
    transpose_into(vt_ref, v_ref)

    def two(j, lses):
        k = 2 * j
        score(k + 1, scores_b, top_b)
        lses = weigh(k, scores_a, top_a, lses)
        score(jnp.minimum(k + 2, KVH - 1), scores_a, top_a)
        return weigh(k + 1, scores_b, top_b, lses)

    lses_ref[...] = jnp.zeros_like(lses_ref)
    lses_ref[:H] = lax.fori_loop(0, KVH // 2, two, jnp.zeros((H, n), jnp.float32))
    lse_ref[...] = lses_ref[...].T
    transpose_into(out_ref, ot_ref)


def private_part(queries, keys, values, pages, lengths, after, page_size):
    n, width = queries.shape
    tokens, key_width = keys.shape
    return pl.pallas_call(
        functools.partial(private_kernel, page_size),
        out_shape=(
            jax.ShapeDtypeStruct((n, width), jnp.float32),
            jax.ShapeDtypeStruct((n, LANES), jnp.float32),
        ),
        in_specs=[ANY] * 3 + [VMEM] * 2 + [ANY],
        out_specs=(VMEM, VMEM),
        scratch_shapes=[
            pltpu.VMEM(queries.shape, queries.dtype),
            pltpu.VMEM(keys.shape, keys.dtype),
            pltpu.VMEM(values.shape, values.dtype),
            pltpu.VMEM((width, n), jnp.bfloat16),
            pltpu.VMEM((key_width, tokens), jnp.bfloat16),
            pltpu.VMEM((KVH, WIN, GROUP * n), jnp.bfloat16),
            pltpu.VMEM((tokens, n), jnp.float32),
            pltpu.VMEM((width, n), jnp.float32),
            pltpu.VMEM((LANES, n), jnp.float32),
            pltpu.VMEM((tokens, GROUP * n), jnp.float32),
            pltpu.VMEM((tokens, GROUP * n), jnp.float32),
            pltpu.VMEM((8, GROUP * n), jnp.float32),
            pltpu.VMEM((8, GROUP * n), jnp.float32),
            pltpu.VMEM((tokens, GROUP * n), jnp.bfloat16),
            pltpu.SemaphoreType.DMA((3,)),
        ],
        compiler_params=params(48),
        cost_estimate=pl.CostEstimate(
            flops=1200 * n * tokens * H * WIN,
            bytes_accessed=4 * tokens * key_width,
            transcendentals=n * tokens * H,
        ),
        name="private",
    )(queries, keys, values, pages, lengths, after)


def expand_heads(share, width):
    n = share.shape[0]
    lane = iota((n, LANES), 1)
    share = jnp.where(lane < H, share, 0.0)
    high = share.astype(jnp.bfloat16).astype(jnp.float32)
    both = (high + pltpu.roll(share - high, H, 1)).astype(jnp.bfloat16)
    row = iota((LANES, width), 0)
    head = jnp.where(row >= H, row - H, row)
    first = head * HD
    column = iota((LANES, width), 1)
    spread = (row < 2 * H) & (column >= first) & (column < first + HD)
    return jnp.dot(
        both, jnp.where(spread, 1.0, 0.0).astype(jnp.bfloat16), preferred_element_type=jnp.float32
    )


def column_blocks(width):
    blocks, first = [], 0
    while first < width:
        rest = width - first
        size = min(512, max(LANES, rest // 2 // LANES * LANES))
        blocks.append(pl.ds(first, size))
        first += size
    return blocks


def finish_kernel(
    half, slot_count, live_ref, groups_ref, back_ref, private_ref, private_lse_ref, w_hbm,
    out_hbm, w_ref, out_ref, in_sems, out_sems
):
    n, width = out_ref.shape
    part = width + LANES
    blocks = column_blocks(width)
    arrivals = []
    for i, cols in enumerate(blocks):
        arrivals.append(pltpu.make_async_copy(w_hbm.at[:, cols], w_ref.at[:, cols], in_sems.at[i]))
        arrivals[i].start()
    slot, upper = slots_of(groups_ref[...], half, slot_count)
    slot, upper = as_column(slot), as_column(upper)
    hit = slot == iota((n, n), 1)
    side = lax.axis_index("req") // half
    own = jnp.where(hit & (upper == side), 1.0, 0.0).astype(jnp.bfloat16)
    other = jnp.where(hit & (upper != side), 1.0, 0.0).astype(jnp.bfloat16)
    pick = jnp.concatenate([own, other], axis=1)

    def picked(first, last):
        both = jnp.concatenate(
            [back_ref[:, first:last], back_ref[:, part + first : part + last]], axis=0
        )
        return jnp.dot(pick, both, preferred_element_type=jnp.float32)

    pieces = picked(width, part)
    lane = iota((n, LANES), 1)
    prefix_lse = (
        pieces + pltpu.roll(pieces, LANES - H, 1) + pltpu.roll(pieces, LANES - 2 * H, 1)
    )
    prefix_lse = jnp.where(lane < H, prefix_lse, 0.0)
    private_lse = private_lse_ref[...]
    top = jnp.maximum(prefix_lse, private_lse)
    a, b = jnp.exp(prefix_lse - top), jnp.exp(private_lse - top)
    prefix_share = expand_heads(a / (a + b), width)
    private_share = expand_heads(b / (a + b), width)
    prefix = picked(0, width)
    attended = prefix_share * prefix + private_share * private_ref[...]
    attended = attended.astype(jnp.bfloat16)
    is_live = iota((n, 1), 0) < live_ref[0]
    departures = []
    for i, (arrival, cols) in enumerate(zip(arrivals, blocks)):
        arrival.wait()
        projected = jnp.dot(attended, w_ref[:, cols], preferred_element_type=jnp.float32)
        out_ref[:, cols] = jnp.where(is_live, projected, 0.0).astype(out_ref.dtype)
        departures.append(
            pltpu.make_async_copy(out_ref.at[:, cols], out_hbm.at[:, cols], out_sems.at[i])
        )
        departures[i].start()
    for departure in departures:
        departure.wait()


def finish(live, groups, back, private, private_lse, weight, half, slot_count):
    n = back.shape[0]
    width = weight.shape[1]
    steps = len(column_blocks(width))
    return pl.pallas_call(
        functools.partial(finish_kernel, half, slot_count),
        out_shape=jax.ShapeDtypeStruct((n, width), jnp.bfloat16),
        in_specs=[SMEM] + [VMEM] * 4 + [ANY],
        out_specs=ANY,
        scratch_shapes=[
            pltpu.VMEM(weight.shape, weight.dtype),
            pltpu.VMEM((n, width), jnp.bfloat16),
            pltpu.SemaphoreType.DMA((steps,)),
            pltpu.SemaphoreType.DMA((steps,)),
        ],
        compiler_params=params(50),
        cost_estimate=pl.CostEstimate(
            flops=2 * n * width * width, bytes_accessed=2 * width * width, transcendentals=0
        ),
        name="finish",
    )(live, groups, back, private, private_lse, weight)


def per_device(
    queries,
    prefix_keys,
    prefix_values,
    pool_keys,
    pool_values,
    page_table,
    private_length,
    group_ids,
    live_rows,
    out_weight,
):
    devices = lax.axis_size("req")
    half = devices // 2
    row_count, width = queries.shape
    slot_count = 2 * row_count // devices
    page_size = pool_keys.shape[1]
    halves = [list(range(half)), list(range(half, devices))]
    across = [(i, (i + half) % devices) for i in range(devices)]

    groups = group_ids.reshape(1, row_count)
    lengths = private_length.reshape(1, row_count)
    pages = page_table.T
    flat_keys = pool_keys.reshape(-1, pool_keys.shape[2])
    flat_values = pool_values.reshape(-1, pool_values.shape[2])

    def exchange(rows):
        blocks = rows.reshape(half, slot_count, rows.shape[1])
        blocks = lax.all_to_all(
            blocks, "req", split_axis=0, concat_axis=0, tiled=True, axis_index_groups=halves
        )
        return blocks.reshape(rows.shape)

    far_keys = lax.ppermute(prefix_keys, "req", across)
    far_values = lax.ppermute(prefix_values, "req", across)
    placed, token = place(queries, groups, half, slot_count)
    rows = exchange(placed)
    private, private_lse = private_part(
        queries, flat_keys, flat_values, pages, lengths, token, page_size
    )
    out = prefix_part(rows, prefix_keys, prefix_values, far_keys, far_values, private_lse)
    back = exchange(out)
    return finish(
        live_rows, groups, back, private, private_lse, out_weight, half, slot_count
    )


def solution(mesh):
    placed = (
        P("req", None),
        P("req", None),
        P("req", None),
        P("req", None, None),
        P("req", None, None),
        P("req", None),
        P("req"),
        P("req", None),
        P("req"),
        P(),
    )
    return jax.shard_map(
        per_device, mesh=mesh, in_specs=placed, out_specs=P("req", None), check_vma=False
    )
```

```python
import functools
import math

import jax
import jax.numpy as jnp
from jax import lax
from jax.experimental import pallas as pl
from jax.experimental.pallas import tpu as pltpu
from jax.sharding import PartitionSpec as P

H = 32
KVH = 8
HD = 80
GROUP = H // KVH
LANES = 128
WIN = 256
SCALE = HD ** (-0.5) * math.log2(math.e)
LN2 = math.log(2.0)
NEVER = -1e30
VMEM = pl.BlockSpec(memory_space=pltpu.VMEM)
SMEM = pl.BlockSpec(memory_space=pltpu.SMEM)
ANY = pl.BlockSpec(memory_space=pl.ANY)


def window(start, width):
    base = min(start // LANES * LANES, width - WIN)
    return base, start - base


def tight_window(start, width):
    if start % LANES + HD <= LANES:
        return start // LANES * LANES, start % LANES, LANES
    return (*window(start, width), WIN)


def iota(shape, axis):
    return lax.broadcasted_iota(jnp.int32, shape, axis)


def params(mib):
    return pltpu.CompilerParams(vmem_limit_bytes=mib * 1024 * 1024)


def transpose_into(target, source):
    rows, cols = source.shape
    for c in range(0, cols, LANES):
        for r in range(0, rows, LANES):
            target[c : c + LANES, r : r + LANES] = source[r : r + LANES, c : c + LANES].T


def as_column(row):
    n = row.shape[1]
    same = iota((n, n), 0) == iota((n, n), 1)
    return jnp.sum(jnp.where(same, row, 0), axis=1, keepdims=True)


def slots_of(groups, half, slot_count):
    n = groups.shape[1]
    earlier = iota((n, n), 0) < iota((n, n), 1)
    same = (as_column(groups) == groups) & earlier
    rank = jnp.sum(jnp.where(same, 1, 0), axis=0, keepdims=True)
    upper = jnp.where(groups >= half, 1, 0)
    return (groups - upper * half) * slot_count + rank, upper


def place_kernel(
    half, slot_count, groups_hbm, q_hbm, out_ref, token_ref, groups_ref, q_ref,
    group_sem, in_sems
):
    n, width = q_ref.shape
    steps = in_sems.shape[0]
    chunk = width // steps
    groups_copy = pltpu.make_async_copy(groups_hbm, groups_ref, group_sem)
    groups_copy.start()
    arrivals = []
    for i in range(steps):
        cols = pl.ds(i * chunk, chunk)
        arrivals.append(pltpu.make_async_copy(q_hbm.at[:, cols], q_ref.at[:, cols], in_sems.at[i]))
        arrivals[i].start()
    token_ref[...] = jnp.zeros_like(token_ref)
    side = lax.axis_index("req") // half
    groups_copy.wait()
    slot, upper = slots_of(groups_ref[...], half, slot_count)
    hit = slot == iota((n, n), 0)
    own = jnp.where(hit & (upper == side), 1.0, 0.0).astype(jnp.bfloat16)
    other = jnp.where(hit & (upper != side), 1.0, 0.0).astype(jnp.bfloat16)
    spread = jnp.concatenate([own, other], axis=0)
    for i, arrival in enumerate(arrivals):
        arrival.wait()
        both = jnp.dot(
            spread, q_ref[:, i * chunk : (i + 1) * chunk], preferred_element_type=jnp.float32
        ).astype(jnp.bfloat16)
        for part in range(2):
            cols = pl.ds(part * width + i * chunk, chunk)
            out_ref[:, cols] = both[part * n : (part + 1) * n]


def place(queries, groups, half, slot_count):
    n, width = queries.shape
    steps = 2
    return pl.pallas_call(
        functools.partial(place_kernel, half, slot_count),
        out_shape=(
            jax.ShapeDtypeStruct((n, 2 * width), queries.dtype),
            jax.ShapeDtypeStruct((8, LANES), jnp.float32),
        ),
        in_specs=[ANY, ANY],
        out_specs=(VMEM, VMEM),
        scratch_shapes=[
            pltpu.VMEM(groups.shape, groups.dtype),
            pltpu.VMEM((n, width), queries.dtype),
            pltpu.SemaphoreType.DMA(()),
            pltpu.SemaphoreType.DMA((steps,)),
        ],
        compiler_params=params(60),
        cost_estimate=pl.CostEstimate(
            flops=4 * n * n * width, bytes_accessed=6 * n * width, transcendentals=0
        ),
        name="place",
    )(groups, queries)


def clear_queries(qs_ref, i, first, size):
    width = qs_ref.shape[2]
    if first:
        qs_ref[i, :first] = jnp.zeros((first, width), jnp.bfloat16)
    if first + HD < size:
        qs_ref[i, first + HD : size] = jnp.zeros((size - first - HD, width), jnp.bfloat16)


def fill_queries(qs_ref, i, qt_ref, k, first):
    n = qt_ref.shape[1]
    for g in range(GROUP):
        row = (k * GROUP + g) * HD
        qs_ref[i, first : first + HD, g * n : (g + 1) * n] = qt_ref[row : row + HD]


def prefix_kernel(
    rows_hbm, near_k, near_v, far_k, far_v, after_ref, out_hbm,
    rows_ref, k_ref, v_ref, qt_ref, vt_ref, qs_ref, ot_ref, lse_ref, scores_ref, out_ref,
    in_sems, out_sems
):
    del after_ref
    n, width = rows_ref.shape
    width //= 2
    key_width = k_ref.shape[2]
    arrivals = []
    for part, (keys, values) in enumerate(((near_k, near_v), (far_k, far_v))):
        cols = pl.ds(part * width, width)
        for source, target in (
            (values, v_ref.at[part]),
            (rows_hbm.at[:, cols], rows_ref.at[:, cols]),
            (keys, k_ref.at[part]),
        ):
            arrivals.append(pltpu.make_async_copy(source, target, in_sems.at[len(arrivals)]))
            arrivals[-1].start()
    windows = [tight_window(k * HD, key_width) for k in range(KVH)]
    for u in range(2 * KVH):
        clear_queries(qs_ref, u, *windows[u % KVH][1:])

    def prepare(part):
        arrivals[3 * part].wait()
        transpose_into(vt_ref.at[part], v_ref.at[part])
        arrivals[3 * part + 1].wait()
        transpose_into(qt_ref, rows_ref.at[:, part * width : (part + 1) * width])
        for k in range(KVH):
            fill_queries(qs_ref, part * KVH + k, qt_ref, k, windows[k][1])
        arrivals[3 * part + 2].wait()

    def score(u):
        part, k = divmod(u, KVH)
        base, _, size = windows[k]
        scores = jnp.dot(
            k_ref[part, :, base : base + size], qs_ref[u, :size], preferred_element_type=jnp.float32
        )
        scores_ref[u % 2] = scores * SCALE

    def weigh(u):
        part, k = divmod(u, KVH)
        scores = scores_ref[u % 2]
        top = jnp.max(scores, axis=0, keepdims=True)
        weights = jnp.exp2(scores - top)
        total = jnp.sum(weights, axis=0, keepdims=True)
        summed = jnp.dot(
            vt_ref[part, k * HD : (k + 1) * HD],
            weights.astype(jnp.bfloat16),
            preferred_element_type=jnp.float32,
        )
        result = (summed * (1.0 / total)).astype(jnp.bfloat16)
        lse = (top + jnp.log2(total)) * LN2
        for g in range(GROUP):
            head = k * GROUP + g
            ot_ref[head * HD : (head + 1) * HD] = result[:, g * n : (g + 1) * n]
            lse_ref[part * H + head : part * H + head + 1] = lse[:, g * n : (g + 1) * n]

    def depart(cols):
        departures.append(
            pltpu.make_async_copy(
                out_ref.at[:, cols], out_hbm.at[:, cols], out_sems.at[len(departures)]
            )
        )
        departures[-1].start()

    def send(u):
        part, k = divmod(u, KVH)
        quarter = width // 4
        first = k // 2 * quarter
        cols = pl.ds(part * width + first, quarter)
        transpose_into(out_ref.at[:, cols], ot_ref.at[first : first + quarter])
        depart(cols)
        if u < 2 * KVH - 1:
            return
        lse = lse_ref[...]
        high = lse.astype(jnp.bfloat16).astype(jnp.float32)
        rest = lse - high
        pieces = jnp.concatenate([high[:H], rest[:H], high[H:], rest[H:]], axis=0)
        cols = pl.ds(2 * width, LANES)
        out_ref[:, cols] = pieces.T.astype(jnp.bfloat16)
        depart(cols)

    departures = []
    prepare(0)
    score(0)
    for u in range(2 * KVH):
        if u == KVH - 2:
            prepare(1)
        if u + 1 < 2 * KVH:
            score(u + 1)
        weigh(u)
        if u % 2:
            send(u)
    for departure in departures:
        departure.wait()


def prefix_part(rows, near_k, near_v, far_k, far_v, after):
    n, width = rows.shape
    width //= 2
    tokens, key_width = near_k.shape
    return pl.pallas_call(
        prefix_kernel,
        out_shape=jax.ShapeDtypeStruct((n, 2 * width + LANES), jnp.bfloat16),
        in_specs=[ANY] * 6,
        out_specs=ANY,
        scratch_shapes=[
            pltpu.VMEM(rows.shape, rows.dtype),
            pltpu.VMEM((2, tokens, key_width), jnp.bfloat16),
            pltpu.VMEM((2, tokens, key_width), jnp.bfloat16),
            pltpu.VMEM((width, n), jnp.bfloat16),
            pltpu.VMEM((2, key_width, tokens), jnp.bfloat16),
            pltpu.VMEM((2 * KVH, WIN, GROUP * n), jnp.bfloat16),
            pltpu.VMEM((width, n), jnp.bfloat16),
            pltpu.VMEM((2 * H, n), jnp.float32),
            pltpu.VMEM((2, tokens, GROUP * n), jnp.float32),
            pltpu.VMEM((n, 2 * width + LANES), jnp.bfloat16),
            pltpu.SemaphoreType.DMA((6,)),
            pltpu.SemaphoreType.DMA((9,)),
        ],
        compiler_params=params(24),
        cost_estimate=pl.CostEstimate(
            flops=16000 * n * 256 * width,
            bytes_accessed=8 * n * width * 2,
            transcendentals=n * 512 * H,
        ),
        name="prefix",
    )(rows, near_k, near_v, far_k, far_v, after)


def fill_bias(bias_ref, pages, lengths, page_size):
    most, n = pages.shape
    page_count = bias_ref.shape[0] // page_size
    page = iota((page_count, n), 0)
    full = jnp.zeros((page_count, n), jnp.float32)
    partial = jnp.zeros((page_count, n), jnp.float32)
    for j in range(most):
        same = pages[j : j + 1] == page
        whole = lengths >= (j + 1) * page_size
        some = (lengths > j * page_size) & (lengths < (j + 1) * page_size)
        full += jnp.where(same & whole, 1.0, 0.0)
        partial += jnp.where(same & some, 1.0, 0.0)
    seen = jnp.where(iota((page_size, n), 0) < lengths % page_size, 1.0, 0.0)
    for p in range(page_count):
        multiple = full[p : p + 1] + seen * partial[p : p + 1]
        bias_ref[p * page_size : (p + 1) * page_size] = jnp.where(
            multiple > 0.0, jnp.log2(jnp.maximum(multiple, 1.0)), NEVER
        )


def private_kernel(
    page_size, q_hbm, k_hbm, v_hbm, pages_ref, lengths_ref, after_ref,
    out_ref, lse_ref, q_ref, k_ref, v_ref, qt_ref, vt_ref, qs_ref, bias_ref, ot_ref, lses_ref,
    scores_a, scores_b, top_a, top_b, weights_ref, sems
):
    del after_ref
    copies = [
        pltpu.make_async_copy(source, target, sems.at[i])
        for i, (source, target) in enumerate(((q_hbm, q_ref), (k_hbm, k_ref), (v_hbm, v_ref)))
    ]
    for copy in copies:
        copy.start()
    n = q_ref.shape[0]
    tokens, key_width = k_ref.shape
    rows = GROUP * n
    tile = 256
    fill_bias(bias_ref, pages_ref[...], lengths_ref[...], page_size)
    copies[0].wait()
    transpose_into(qt_ref, q_ref)
    for k in range(KVH):
        _, first = window(k * HD, key_width)
        clear_queries(qs_ref, k, first, WIN)
        fill_queries(qs_ref, k, qt_ref, k, first)
    copies[1].wait()

    def score(k, scores_ref, top_ref):
        base = pl.multiple_of(jnp.minimum(k * HD // LANES * LANES, key_width - WIN), LANES)
        top = None
        for t in range(0, tokens, tile):
            scores = jnp.dot(
                k_ref[t : t + tile, pl.ds(base, WIN)],
                qs_ref[k],
                preferred_element_type=jnp.float32,
            )
            bias = bias_ref[t : t + tile]
            scores = scores * SCALE + jnp.concatenate([bias] * GROUP, axis=1)
            scores_ref[t : t + tile] = scores
            highest = jnp.max(scores.reshape(tile // 8, 8, rows), axis=0)
            top = highest if top is None else jnp.maximum(top, highest)
        top_ref[...] = top

    def weigh(k, scores_ref, top_ref, lses):
        top = jnp.max(top_ref[...], axis=0, keepdims=True)
        total = jnp.zeros((8, rows), jnp.float32)
        for t in range(0, tokens, tile):
            weights = jnp.exp2(scores_ref[t : t + tile] - top)
            total += jnp.sum(weights.reshape(tile // 8, 8, rows), axis=0)
            weights_ref[t : t + tile] = weights.astype(jnp.bfloat16)
        total = jnp.sum(total, axis=0, keepdims=True)
        values = vt_ref[pl.ds(pl.multiple_of(k * HD, 16), HD)]
        summed = jnp.dot(values, weights_ref[...], preferred_element_type=jnp.float32)
        result = summed * (1.0 / total)
        lse = (top + jnp.log2(total)) * LN2
        row = iota(lses.shape, 0)
        for g in range(GROUP):
            head = k * GROUP + g
            ot_ref[pl.ds(pl.multiple_of(head * HD, 16), HD)] = result[:, g * n : (g + 1) * n]
            lses = jnp.where(row == head, lse[:, g * n : (g + 1) * n], lses)
        return lses

    score(0, scores_a, top_a)
    copies[2].wait()
    transpose_into(vt_ref, v_ref)

    def two(j, lses):
        k = 2 * j
        score(k + 1, scores_b, top_b)
        lses = weigh(k, scores_a, top_a, lses)
        score(jnp.minimum(k + 2, KVH - 1), scores_a, top_a)
        return weigh(k + 1, scores_b, top_b, lses)

    lses_ref[...] = jnp.zeros_like(lses_ref)
    lses_ref[:H] = lax.fori_loop(0, KVH // 2, two, jnp.zeros((H, n), jnp.float32))
    lse_ref[...] = lses_ref[...].T
    transpose_into(out_ref, ot_ref)


def private_part(queries, keys, values, pages, lengths, after, page_size):
    n, width = queries.shape
    tokens, key_width = keys.shape
    return pl.pallas_call(
        functools.partial(private_kernel, page_size),
        out_shape=(
            jax.ShapeDtypeStruct((n, width), jnp.float32),
            jax.ShapeDtypeStruct((n, LANES), jnp.float32),
        ),
        in_specs=[ANY] * 3 + [VMEM] * 2 + [ANY],
        out_specs=(VMEM, VMEM),
        scratch_shapes=[
            pltpu.VMEM(queries.shape, queries.dtype),
            pltpu.VMEM(keys.shape, keys.dtype),
            pltpu.VMEM(values.shape, values.dtype),
            pltpu.VMEM((width, n), jnp.bfloat16),
            pltpu.VMEM((key_width, tokens), jnp.bfloat16),
            pltpu.VMEM((KVH, WIN, GROUP * n), jnp.bfloat16),
            pltpu.VMEM((tokens, n), jnp.float32),
            pltpu.VMEM((width, n), jnp.float32),
            pltpu.VMEM((LANES, n), jnp.float32),
            pltpu.VMEM((tokens, GROUP * n), jnp.float32),
            pltpu.VMEM((tokens, GROUP * n), jnp.float32),
            pltpu.VMEM((8, GROUP * n), jnp.float32),
            pltpu.VMEM((8, GROUP * n), jnp.float32),
            pltpu.VMEM((tokens, GROUP * n), jnp.bfloat16),
            pltpu.SemaphoreType.DMA((3,)),
        ],
        compiler_params=params(48),
        cost_estimate=pl.CostEstimate(
            flops=1200 * n * tokens * H * WIN,
            bytes_accessed=4 * tokens * key_width,
            transcendentals=n * tokens * H,
        ),
        name="private",
    )(queries, keys, values, pages, lengths, after)


def expand_heads(share, width):
    n = share.shape[0]
    lane = iota((n, LANES), 1)
    share = jnp.where(lane < H, share, 0.0)
    high = share.astype(jnp.bfloat16).astype(jnp.float32)
    both = (high + pltpu.roll(share - high, H, 1)).astype(jnp.bfloat16)
    row = iota((LANES, width), 0)
    head = jnp.where(row >= H, row - H, row)
    first = head * HD
    column = iota((LANES, width), 1)
    spread = (row < 2 * H) & (column >= first) & (column < first + HD)
    return jnp.dot(
        both, jnp.where(spread, 1.0, 0.0).astype(jnp.bfloat16), preferred_element_type=jnp.float32
    )


def row_blocks(rows):
    blocks, first = [], 0
    while first < rows:
        rest = rows - first
        size = min(512, max(LANES, rest // 2 // LANES * LANES))
        blocks.append(slice(first, first + size))
        first += size
    return blocks


def finish_kernel(
    half, slot_count, live_ref, groups_ref, back_ref, private_ref, private_lse_ref, w_hbm,
    out_hbm, w_ref, sum_ref, out_ref, in_sems, out_sems
):
    n, width = out_ref.shape
    blocks = row_blocks(width)
    arrivals = []
    for i, block in enumerate(blocks):
        arrivals.append(pltpu.make_async_copy(w_hbm.at[block], w_ref.at[block], in_sems.at[i]))
        arrivals[i].start()
    slot, upper = slots_of(groups_ref[...], half, slot_count)
    slot, upper = as_column(slot), as_column(upper)
    hit = slot == iota((n, n), 1)
    side = lax.axis_index("req") // half
    own = jnp.where(hit & (upper == side), 1.0, 0.0).astype(jnp.bfloat16)
    other = jnp.where(hit & (upper != side), 1.0, 0.0).astype(jnp.bfloat16)
    tile = back_ref[:, 2 * width :]
    lane = iota((n, LANES), 1)
    pieces = jnp.where(
        lane < 2 * H,
        jnp.dot(own, tile, preferred_element_type=jnp.float32),
        jnp.dot(other, tile, preferred_element_type=jnp.float32),
    )
    prefix_lse = pieces
    for i in range(1, LANES // H):
        prefix_lse += pltpu.roll(pieces, LANES - i * H, 1)
    prefix_lse = jnp.where(lane < H, prefix_lse, 0.0)
    private_lse = private_lse_ref[...]
    top = jnp.maximum(prefix_lse, private_lse)
    a, b = jnp.exp(prefix_lse - top), jnp.exp(private_lse - top)
    prefix_share = expand_heads(a / (a + b), width)
    private_share = expand_heads(b / (a + b), width)
    pick = jnp.concatenate([own, other], axis=1)
    both = jnp.concatenate([back_ref[:, :width], back_ref[:, width : 2 * width]], axis=0)
    prefix = jnp.dot(pick, both, preferred_element_type=jnp.float32)
    attended = prefix_share * prefix + private_share * private_ref[...]
    attended = attended.astype(jnp.bfloat16)
    is_live = iota((n, 1), 0) < live_ref[0]
    departures = []
    for i, (arrival, block) in enumerate(zip(arrivals, blocks)):
        arrival.wait()
        for j in range(out_sems.shape[0]):
            chunk = width // out_sems.shape[0]
            cols = pl.ds(j * chunk, chunk)
            projected = jnp.dot(
                attended[:, block], w_ref[block, cols], preferred_element_type=jnp.float32
            )
            if i:
                projected += sum_ref[:, cols]
            if i < len(blocks) - 1:
                sum_ref[:, cols] = projected
                continue
            out_ref[:, cols] = jnp.where(is_live, projected, 0.0).astype(out_ref.dtype)
            departures.append(
                pltpu.make_async_copy(out_ref.at[:, cols], out_hbm.at[:, cols], out_sems.at[j])
            )
            departures[-1].start()
    for departure in departures:
        departure.wait()


def finish(live, groups, back, private, private_lse, weight, half, slot_count):
    n = back.shape[0]
    width = weight.shape[1]
    steps = len(row_blocks(width))
    return pl.pallas_call(
        functools.partial(finish_kernel, half, slot_count),
        out_shape=jax.ShapeDtypeStruct((n, width), jnp.bfloat16),
        in_specs=[SMEM] + [VMEM] * 4 + [ANY],
        out_specs=ANY,
        scratch_shapes=[
            pltpu.VMEM(weight.shape, weight.dtype),
            pltpu.VMEM((n, width), jnp.float32),
            pltpu.VMEM((n, width), jnp.bfloat16),
            pltpu.SemaphoreType.DMA((steps,)),
            pltpu.SemaphoreType.DMA((5,)),
        ],
        compiler_params=params(50),
        cost_estimate=pl.CostEstimate(
            flops=2 * n * width * width, bytes_accessed=2 * width * width, transcendentals=0
        ),
        name="finish",
    )(live, groups, back, private, private_lse, weight)


def per_device(
    queries,
    prefix_keys,
    prefix_values,
    pool_keys,
    pool_values,
    page_table,
    private_length,
    group_ids,
    live_rows,
    out_weight,
):
    devices = lax.axis_size("req")
    half = devices // 2
    row_count, width = queries.shape
    slot_count = 2 * row_count // devices
    page_size = pool_keys.shape[1]
    halves = [list(range(half)), list(range(half, devices))]
    across = [(i, (i + half) % devices) for i in range(devices)]

    groups = group_ids.reshape(1, row_count)
    lengths = private_length.reshape(1, row_count)
    pages = page_table.T
    flat_keys = pool_keys.reshape(-1, pool_keys.shape[2])
    flat_values = pool_values.reshape(-1, pool_values.shape[2])

    def exchange(rows):
        blocks = rows.reshape(half, slot_count, rows.shape[1])
        blocks = lax.all_to_all(
            blocks, "req", split_axis=0, concat_axis=0, tiled=True, axis_index_groups=halves
        )
        return blocks.reshape(rows.shape)

    far_keys = lax.ppermute(prefix_keys, "req", across)
    far_values = lax.ppermute(prefix_values, "req", across)
    placed, token = place(queries, groups, half, slot_count)
    rows = exchange(placed)
    private, private_lse = private_part(
        queries, flat_keys, flat_values, pages, lengths, token, page_size
    )
    out = prefix_part(rows, prefix_keys, prefix_values, far_keys, far_values, private_lse)
    back = exchange(out)
    return finish(
        live_rows, groups, back, private, private_lse, out_weight, half, slot_count
    )


def solution(mesh):
    placed = (
        P("req", None),
        P("req", None),
        P("req", None),
        P("req", None, None),
        P("req", None, None),
        P("req", None),
        P("req"),
        P("req", None),
        P("req"),
        P(),
    )
    return jax.shard_map(
        per_device, mesh=mesh, in_specs=placed, out_specs=P("req", None), check_vma=False
    )
```

```python
import functools
import math

import jax
import jax.numpy as jnp
from jax import lax
from jax.experimental import pallas as pl
from jax.experimental.pallas import tpu as pltpu
from jax.sharding import PartitionSpec as P

H = 32
KVH = 8
HD = 80
GROUP = H // KVH
LANES = 128
WIN = 256
SCALE = HD ** (-0.5) * math.log2(math.e)
LN2 = math.log(2.0)
NEVER = -1e30
VMEM = pl.BlockSpec(memory_space=pltpu.VMEM)
SMEM = pl.BlockSpec(memory_space=pltpu.SMEM)
ANY = pl.BlockSpec(memory_space=pl.ANY)


def window(start, width):
    base = min(start // LANES * LANES, width - WIN)
    return base, start - base


def tight_window(start, width):
    if start % LANES + HD <= LANES:
        return start // LANES * LANES, start % LANES, LANES
    return (*window(start, width), WIN)


def iota(shape, axis):
    return lax.broadcasted_iota(jnp.int32, shape, axis)


def params(mib):
    return pltpu.CompilerParams(vmem_limit_bytes=mib * 1024 * 1024)


def transpose_into(target, source):
    rows, cols = source.shape
    for c in range(0, cols, LANES):
        for r in range(0, rows, LANES):
            target[c : c + LANES, r : r + LANES] = source[r : r + LANES, c : c + LANES].T


def as_column(row):
    n = row.shape[1]
    same = iota((n, n), 0) == iota((n, n), 1)
    return jnp.sum(jnp.where(same, row, 0), axis=1, keepdims=True)


def slots_of(groups, half, side, slot_count):
    n = groups.shape[1]
    quarter = half // 2
    earlier = iota((n, n), 0) < iota((n, n), 1)
    same = (as_column(groups) == groups) & earlier
    rank = jnp.sum(jnp.where(same, 1, 0), axis=0, keepdims=True)
    upper = jnp.where(groups >= half, 1, 0)
    far = jnp.where(upper != side, 1, 0)
    host = groups - upper * half + far * quarter
    host = jnp.where(host >= half, host - half, host)
    return host * slot_count + rank, far


def place_kernel(
    half, slot_count, groups_hbm, q_hbm, out_ref, token_ref, groups_ref, q_ref,
    group_sem, in_sems
):
    n, width = q_ref.shape
    steps = in_sems.shape[0]
    chunk = width // steps
    groups_copy = pltpu.make_async_copy(groups_hbm, groups_ref, group_sem)
    groups_copy.start()
    arrivals = []
    for i in range(steps):
        cols = pl.ds(i * chunk, chunk)
        arrivals.append(pltpu.make_async_copy(q_hbm.at[:, cols], q_ref.at[:, cols], in_sems.at[i]))
        arrivals[i].start()
    token_ref[...] = jnp.zeros_like(token_ref)
    side = lax.axis_index("req") // half
    groups_copy.wait()
    slot, far = slots_of(groups_ref[...], half, side, slot_count)
    hit = slot == iota((n, n), 0)
    own = jnp.where(hit & (far == 0), 1.0, 0.0).astype(jnp.bfloat16)
    other = jnp.where(hit & (far == 1), 1.0, 0.0).astype(jnp.bfloat16)
    spread = jnp.concatenate([own, other], axis=0)
    for i, arrival in enumerate(arrivals):
        arrival.wait()
        both = jnp.dot(
            spread, q_ref[:, i * chunk : (i + 1) * chunk], preferred_element_type=jnp.float32
        ).astype(jnp.bfloat16)
        for part in range(2):
            cols = pl.ds(part * width + i * chunk, chunk)
            out_ref[:, cols] = both[part * n : (part + 1) * n]


def place(queries, groups, half, slot_count):
    n, width = queries.shape
    steps = 2
    return pl.pallas_call(
        functools.partial(place_kernel, half, slot_count),
        out_shape=(
            jax.ShapeDtypeStruct((n, 2 * width), queries.dtype),
            jax.ShapeDtypeStruct((8, LANES), jnp.float32),
        ),
        in_specs=[ANY, ANY],
        out_specs=(VMEM, VMEM),
        scratch_shapes=[
            pltpu.VMEM(groups.shape, groups.dtype),
            pltpu.VMEM((n, width), queries.dtype),
            pltpu.SemaphoreType.DMA(()),
            pltpu.SemaphoreType.DMA((steps,)),
        ],
        compiler_params=params(60),
        cost_estimate=pl.CostEstimate(
            flops=4 * n * n * width, bytes_accessed=6 * n * width, transcendentals=0
        ),
        name="place",
    )(groups, queries)


def clear_queries(qs_ref, i, first, size):
    width = qs_ref.shape[2]
    if first:
        qs_ref[i, :first] = jnp.zeros((first, width), jnp.bfloat16)
    if first + HD < size:
        qs_ref[i, first + HD : size] = jnp.zeros((size - first - HD, width), jnp.bfloat16)


def fill_queries(qs_ref, i, qt_ref, k, first):
    n = qt_ref.shape[1]
    for g in range(GROUP):
        row = (k * GROUP + g) * HD
        qs_ref[i, first : first + HD, g * n : (g + 1) * n] = qt_ref[row : row + HD]


def prefix_kernel(
    quarter, rows_hbm, near_k, near_v, outer_k, outer_v, inner_k, inner_v, after_ref, out_hbm,
    rows_ref, k_ref, v_ref, qt_ref, vt_ref, qs_ref, ot_ref, lse_ref, scores_ref, out_ref,
    in_sems, out_sems
):
    del after_ref
    n, width = rows_ref.shape
    width //= 2
    key_width = k_ref.shape[2]
    place = lax.axis_index("req") // quarter
    is_outer = (place == 0) | (place == 3)
    arrivals = []

    def arrive(target, source, inner=None):
        sem = in_sems.at[len(arrivals)]
        arrivals.append(pltpu.make_async_copy(source, target, sem))
        if inner is None:
            arrivals[-1].start()
            return
        pl.when(is_outer)(arrivals[-1].start)
        pl.when(jnp.logical_not(is_outer))(pltpu.make_async_copy(inner, target, sem).start)

    arrive(v_ref.at[0], near_v)
    arrive(rows_ref.at[:, :width], rows_hbm.at[:, :width])
    arrive(k_ref.at[0], near_k)
    arrive(v_ref.at[1], outer_v, inner_v)
    arrive(rows_ref.at[:, width:], rows_hbm.at[:, width:])
    arrive(k_ref.at[1], outer_k, inner_k)
    windows = [tight_window(k * HD, key_width) for k in range(KVH)]
    for u in range(2 * KVH):
        clear_queries(qs_ref, u, *windows[u % KVH][1:])

    def prepare(part):
        arrivals[3 * part].wait()
        transpose_into(vt_ref.at[part], v_ref.at[part])
        arrivals[3 * part + 1].wait()
        transpose_into(qt_ref.at[part * width : (part + 1) * width], rows_ref.at[:, part * width : (part + 1) * width])
        for k in range(KVH):
            fill_queries(qs_ref, part * KVH + k, qt_ref.at[part * width : (part + 1) * width], k, windows[k][1])
        arrivals[3 * part + 2].wait()

    def score(u):
        part, k = divmod(u, KVH)
        base, _, size = windows[k]
        scores = jnp.dot(
            k_ref[part, :, base : base + size], qs_ref[u, :size], preferred_element_type=jnp.float32
        )
        scores_ref[u % 2] = scores * SCALE

    def weigh(u):
        part, k = divmod(u, KVH)
        scores = scores_ref[u % 2]
        top = jnp.max(scores, axis=0, keepdims=True)
        weights = jnp.exp2(scores - top)
        total = jnp.sum(weights, axis=0, keepdims=True)
        summed = jnp.dot(
            vt_ref[part, k * HD : (k + 1) * HD],
            weights.astype(jnp.bfloat16),
            preferred_element_type=jnp.float32,
        )
        result = (summed * (1.0 / total)).astype(jnp.bfloat16)
        lse = (top + jnp.log2(total)) * LN2
        for g in range(GROUP):
            head = k * GROUP + g
            ot_ref[head * HD : (head + 1) * HD] = result[:, g * n : (g + 1) * n]
            lse_ref[part * H + head : part * H + head + 1] = lse[:, g * n : (g + 1) * n]

    def depart(cols):
        departures.append(
            pltpu.make_async_copy(
                out_ref.at[:, cols], out_hbm.at[:, cols], out_sems.at[len(departures)]
            )
        )
        departures[-1].start()

    def send(u):
        part, k = divmod(u, KVH)
        quarter = width // 4
        first = k // 2 * quarter
        cols = pl.ds(part * width + first, quarter)
        transpose_into(out_ref.at[:, cols], ot_ref.at[first : first + quarter])
        depart(cols)
        if u < 2 * KVH - 1:
            return
        lse = lse_ref[...]
        high = lse.astype(jnp.bfloat16).astype(jnp.float32)
        rest = lse - high
        pieces = jnp.concatenate([high[:H], rest[:H], high[H:], rest[H:]], axis=0)
        cols = pl.ds(2 * width, LANES)
        out_ref[:, cols] = pieces.T.astype(jnp.bfloat16)
        depart(cols)

    departures = []
    prepare(0)
    score(0)
    prepare(1)
    for u in range(2 * KVH):
        if u + 1 < 2 * KVH:
            score(u + 1)
        weigh(u)
        if u % 2:
            send(u)
    for departure in departures:
        departure.wait()


def prefix_part(quarter, rows, near, outer, inner, after):
    n, width = rows.shape
    width //= 2
    tokens, key_width = near[0].shape
    return pl.pallas_call(
        functools.partial(prefix_kernel, quarter),
        out_shape=jax.ShapeDtypeStruct((n, 2 * width + LANES), jnp.bfloat16),
        in_specs=[ANY] * 8,
        out_specs=ANY,
        scratch_shapes=[
            pltpu.VMEM(rows.shape, rows.dtype),
            pltpu.VMEM((2, tokens, key_width), jnp.bfloat16),
            pltpu.VMEM((2, tokens, key_width), jnp.bfloat16),
            pltpu.VMEM((2 * width, n), jnp.bfloat16),
            pltpu.VMEM((2, key_width, tokens), jnp.bfloat16),
            pltpu.VMEM((2 * KVH, WIN, GROUP * n), jnp.bfloat16),
            pltpu.VMEM((width, n), jnp.bfloat16),
            pltpu.VMEM((2 * H, n), jnp.float32),
            pltpu.VMEM((2, tokens, GROUP * n), jnp.float32),
            pltpu.VMEM((n, 2 * width + LANES), jnp.bfloat16),
            pltpu.SemaphoreType.DMA((6,)),
            pltpu.SemaphoreType.DMA((9,)),
        ],
        compiler_params=params(24),
        cost_estimate=pl.CostEstimate(
            flops=16000 * n * 256 * width,
            bytes_accessed=8 * n * width * 2,
            transcendentals=n * 512 * H,
        ),
        name="prefix",
    )(rows, *near, *outer, *inner, after)


def fill_bias(bias_ref, pages, lengths, page_size):
    most, n = pages.shape
    page_count = bias_ref.shape[0] // page_size
    page = iota((page_count, n), 0)
    full = jnp.zeros((page_count, n), jnp.float32)
    partial = jnp.zeros((page_count, n), jnp.float32)
    for j in range(most):
        same = pages[j : j + 1] == page
        whole = lengths >= (j + 1) * page_size
        some = (lengths > j * page_size) & (lengths < (j + 1) * page_size)
        full += jnp.where(same & whole, 1.0, 0.0)
        partial += jnp.where(same & some, 1.0, 0.0)
    seen = jnp.where(iota((page_size, n), 0) < lengths % page_size, 1.0, 0.0)
    for p in range(page_count):
        multiple = full[p : p + 1] + seen * partial[p : p + 1]
        bias_ref[p * page_size : (p + 1) * page_size] = jnp.where(
            multiple > 0.0, jnp.log2(jnp.maximum(multiple, 1.0)), NEVER
        )


def private_kernel(
    page_size, q_hbm, k_hbm, v_hbm, pages_ref, lengths_ref, *refs
):
    (
        out_ref, lse_ref, q_ref, k_ref, v_ref, qt_ref, vt_ref, qs_ref, bias_ref, ot_ref, lses_ref,
        scores_a, scores_b, top_a, top_b, weights_ref, sems,
    ) = refs[-17:]
    copies = [
        pltpu.make_async_copy(source, target, sems.at[i])
        for i, (source, target) in enumerate(((q_hbm, q_ref), (k_hbm, k_ref), (v_hbm, v_ref)))
    ]
    for copy in copies:
        copy.start()
    n = q_ref.shape[0]
    tokens, key_width = k_ref.shape
    rows = GROUP * n
    tile = 256
    fill_bias(bias_ref, pages_ref[...], lengths_ref[...], page_size)
    copies[0].wait()
    transpose_into(qt_ref, q_ref)
    for k in range(KVH):
        _, first = window(k * HD, key_width)
        clear_queries(qs_ref, k, first, WIN)
        fill_queries(qs_ref, k, qt_ref, k, first)
    copies[1].wait()

    def score(k, scores_ref, top_ref):
        base = pl.multiple_of(jnp.minimum(k * HD // LANES * LANES, key_width - WIN), LANES)
        top = None
        for t in range(0, tokens, tile):
            scores = jnp.dot(
                k_ref[t : t + tile, pl.ds(base, WIN)],
                qs_ref[k],
                preferred_element_type=jnp.float32,
            )
            bias = bias_ref[t : t + tile]
            scores = scores * SCALE + jnp.concatenate([bias] * GROUP, axis=1)
            scores_ref[t : t + tile] = scores
            highest = jnp.max(scores.reshape(tile // 8, 8, rows), axis=0)
            top = highest if top is None else jnp.maximum(top, highest)
        top_ref[...] = top

    def weigh(k, scores_ref, top_ref, lses):
        top = jnp.max(top_ref[...], axis=0, keepdims=True)
        total = jnp.zeros((8, rows), jnp.float32)
        for t in range(0, tokens, tile):
            weights = jnp.exp2(scores_ref[t : t + tile] - top)
            total += jnp.sum(weights.reshape(tile // 8, 8, rows), axis=0)
            weights_ref[t : t + tile] = weights.astype(jnp.bfloat16)
        total = jnp.sum(total, axis=0, keepdims=True)
        values = vt_ref[pl.ds(pl.multiple_of(k * HD, 16), HD)]
        summed = jnp.dot(values, weights_ref[...], preferred_element_type=jnp.float32)
        result = summed * (1.0 / total)
        lse = (top + jnp.log2(total)) * LN2
        row = iota(lses.shape, 0)
        for g in range(GROUP):
            head = k * GROUP + g
            ot_ref[pl.ds(pl.multiple_of(head * HD, 16), HD)] = result[:, g * n : (g + 1) * n]
            lses = jnp.where(row == head, lse[:, g * n : (g + 1) * n], lses)
        return lses

    score(0, scores_a, top_a)
    copies[2].wait()
    transpose_into(vt_ref, v_ref)

    def two(j, lses):
        k = 2 * j
        score(k + 1, scores_b, top_b)
        lses = weigh(k, scores_a, top_a, lses)
        score(jnp.minimum(k + 2, KVH - 1), scores_a, top_a)
        return weigh(k + 1, scores_b, top_b, lses)

    lses_ref[...] = jnp.zeros_like(lses_ref)
    lses_ref[:H] = lax.fori_loop(0, KVH // 2, two, jnp.zeros((H, n), jnp.float32))
    lse_ref[...] = lses_ref[...].T
    transpose_into(out_ref, ot_ref)


def private_part(queries, keys, values, pages, lengths, after, page_size):
    n, width = queries.shape
    tokens, key_width = keys.shape
    return pl.pallas_call(
        functools.partial(private_kernel, page_size),
        out_shape=(
            jax.ShapeDtypeStruct((n, width), jnp.float32),
            jax.ShapeDtypeStruct((n, LANES), jnp.float32),
        ),
        in_specs=[ANY] * 3 + [VMEM] * 2 + [ANY] * len(after),
        out_specs=(VMEM, VMEM),
        scratch_shapes=[
            pltpu.VMEM(queries.shape, queries.dtype),
            pltpu.VMEM(keys.shape, keys.dtype),
            pltpu.VMEM(values.shape, values.dtype),
            pltpu.VMEM((width, n), jnp.bfloat16),
            pltpu.VMEM((key_width, tokens), jnp.bfloat16),
            pltpu.VMEM((KVH, WIN, GROUP * n), jnp.bfloat16),
            pltpu.VMEM((tokens, n), jnp.float32),
            pltpu.VMEM((width, n), jnp.float32),
            pltpu.VMEM((LANES, n), jnp.float32),
            pltpu.VMEM((tokens, GROUP * n), jnp.float32),
            pltpu.VMEM((tokens, GROUP * n), jnp.float32),
            pltpu.VMEM((8, GROUP * n), jnp.float32),
            pltpu.VMEM((8, GROUP * n), jnp.float32),
            pltpu.VMEM((tokens, GROUP * n), jnp.bfloat16),
            pltpu.SemaphoreType.DMA((3,)),
        ],
        compiler_params=params(48),
        cost_estimate=pl.CostEstimate(
            flops=1200 * n * tokens * H * WIN,
            bytes_accessed=4 * tokens * key_width,
            transcendentals=n * tokens * H,
        ),
        name="private",
    )(queries, keys, values, pages, lengths, *after)


def expand_heads(share, width):
    n = share.shape[0]
    lane = iota((n, LANES), 1)
    share = jnp.where(lane < H, share, 0.0)
    high = share.astype(jnp.bfloat16).astype(jnp.float32)
    both = (high + pltpu.roll(share - high, H, 1)).astype(jnp.bfloat16)
    row = iota((LANES, width), 0)
    head = jnp.where(row >= H, row - H, row)
    first = head * HD
    column = iota((LANES, width), 1)
    spread = (row < 2 * H) & (column >= first) & (column < first + HD)
    return jnp.dot(
        both, jnp.where(spread, 1.0, 0.0).astype(jnp.bfloat16), preferred_element_type=jnp.float32
    )


def row_blocks(rows):
    blocks, first = [], 0
    while first < rows:
        rest = rows - first
        size = min(512, max(LANES, rest // 2 // LANES * LANES))
        blocks.append(slice(first, first + size))
        first += size
    return blocks


def finish_kernel(
    half, slot_count, live_ref, groups_ref, back_ref, private_ref, private_lse_ref, w_hbm,
    out_hbm, w_ref, sum_ref, out_ref, in_sems, out_sems
):
    n, width = out_ref.shape
    blocks = row_blocks(width)
    arrivals = []
    for i, block in enumerate(blocks):
        arrivals.append(pltpu.make_async_copy(w_hbm.at[block], w_ref.at[block], in_sems.at[i]))
        arrivals[i].start()
    side = lax.axis_index("req") // half
    slot, far = slots_of(groups_ref[...], half, side, slot_count)
    slot, far = as_column(slot), as_column(far)
    hit = slot == iota((n, n), 1)
    own = jnp.where(hit & (far == 0), 1.0, 0.0).astype(jnp.bfloat16)
    other = jnp.where(hit & (far == 1), 1.0, 0.0).astype(jnp.bfloat16)
    tile = back_ref[:, 2 * width :]
    lane = iota((n, LANES), 1)
    pieces = jnp.where(
        lane < 2 * H,
        jnp.dot(own, tile, preferred_element_type=jnp.float32),
        jnp.dot(other, tile, preferred_element_type=jnp.float32),
    )
    prefix_lse = pieces
    for i in range(1, LANES // H):
        prefix_lse += pltpu.roll(pieces, LANES - i * H, 1)
    prefix_lse = jnp.where(lane < H, prefix_lse, 0.0)
    private_lse = private_lse_ref[...]
    top = jnp.maximum(prefix_lse, private_lse)
    a, b = jnp.exp(prefix_lse - top), jnp.exp(private_lse - top)
    prefix_share = expand_heads(a / (a + b), width)
    private_share = expand_heads(b / (a + b), width)
    pick = jnp.concatenate([own, other], axis=1)
    both = jnp.concatenate([back_ref[:, :width], back_ref[:, width : 2 * width]], axis=0)
    prefix = jnp.dot(pick, both, preferred_element_type=jnp.float32)
    attended = prefix_share * prefix + private_share * private_ref[...]
    attended = attended.astype(jnp.bfloat16)
    is_live = iota((n, 1), 0) < live_ref[0]
    departures = []
    for i, (arrival, block) in enumerate(zip(arrivals, blocks)):
        arrival.wait()
        for j in range(out_sems.shape[0]):
            chunk = width // out_sems.shape[0]
            cols = pl.ds(j * chunk, chunk)
            projected = jnp.dot(
                attended[:, block], w_ref[block, cols], preferred_element_type=jnp.float32
            )
            if i:
                projected += sum_ref[:, cols]
            if i < len(blocks) - 1:
                sum_ref[:, cols] = projected
                continue
            out_ref[:, cols] = jnp.where(is_live, projected, 0.0).astype(out_ref.dtype)
            departures.append(
                pltpu.make_async_copy(out_ref.at[:, cols], out_hbm.at[:, cols], out_sems.at[j])
            )
            departures[-1].start()
    for departure in departures:
        departure.wait()


def finish(live, groups, back, private, private_lse, weight, half, slot_count):
    n = back.shape[0]
    width = weight.shape[1]
    steps = len(row_blocks(width))
    return pl.pallas_call(
        functools.partial(finish_kernel, half, slot_count),
        out_shape=jax.ShapeDtypeStruct((n, width), jnp.bfloat16),
        in_specs=[SMEM] + [VMEM] * 4 + [ANY],
        out_specs=ANY,
        scratch_shapes=[
            pltpu.VMEM(weight.shape, weight.dtype),
            pltpu.VMEM((n, width), jnp.float32),
            pltpu.VMEM((n, width), jnp.bfloat16),
            pltpu.SemaphoreType.DMA((steps,)),
            pltpu.SemaphoreType.DMA((5,)),
        ],
        compiler_params=params(50),
        cost_estimate=pl.CostEstimate(
            flops=2 * n * width * width, bytes_accessed=2 * width * width, transcendentals=0
        ),
        name="finish",
    )(live, groups, back, private, private_lse, weight)


def per_device(
    queries,
    prefix_keys,
    prefix_values,
    pool_keys,
    pool_values,
    page_table,
    private_length,
    group_ids,
    live_rows,
    out_weight,
):
    devices = lax.axis_size("req")
    half = devices // 2
    row_count, width = queries.shape
    slot_count = 2 * row_count // devices
    page_size = pool_keys.shape[1]
    halves = [list(range(half)), list(range(half, devices))]
    quarter = devices // 4
    mirror = [(i, (3 - i // quarter) * quarter + i % quarter) for i in range(devices)]
    outer_pairs = [pair for pair in mirror if pair[0] // quarter in (0, 3)]
    inner_pairs = [pair for pair in mirror if pair[0] // quarter in (1, 2)]

    groups = group_ids.reshape(1, row_count)
    lengths = private_length.reshape(1, row_count)
    pages = page_table.T
    flat_keys = pool_keys.reshape(-1, pool_keys.shape[2])
    flat_values = pool_values.reshape(-1, pool_values.shape[2])

    def exchange(rows):
        blocks = rows.reshape(half, slot_count, rows.shape[1])
        blocks = lax.all_to_all(
            blocks, "req", split_axis=0, concat_axis=0, tiled=True, axis_index_groups=halves
        )
        return blocks.reshape(rows.shape)

    prompt = (prefix_keys, prefix_values)
    outer = [lax.ppermute(x, "req", outer_pairs) for x in prompt]
    inner = [lax.ppermute(x, "req", inner_pairs) for x in prompt]
    placed, token = place(queries, groups, half, slot_count)
    rows = exchange(placed)
    private, private_lse = private_part(
        queries, flat_keys, flat_values, pages, lengths, (token, outer[0]), page_size
    )
    out = prefix_part(quarter, rows, prompt, outer, inner, private_lse)
    back = exchange(out)
    return finish(
        live_rows, groups, back, private, private_lse, out_weight, half, slot_count
    )


def solution(mesh):
    placed = (
        P("req", None),
        P("req", None),
        P("req", None),
        P("req", None, None),
        P("req", None, None),
        P("req", None),
        P("req"),
        P("req", None),
        P("req"),
        P(),
    )
    return jax.shard_map(
        per_device, mesh=mesh, in_specs=placed, out_specs=P("req", None), check_vma=False
    )
```

```python
import functools
import math

import jax
import jax.numpy as jnp
from jax import lax
from jax.experimental import pallas as pl
from jax.experimental.pallas import tpu as pltpu
from jax.sharding import PartitionSpec as P

H = 32
KVH = 8
HD = 80
GROUP = H // KVH
LANES = 128
WIN = 256
SCALE = HD ** (-0.5) * math.log2(math.e)
LN2 = math.log(2.0)
NEVER = -1e30
VMEM = pl.BlockSpec(memory_space=pltpu.VMEM)
SMEM = pl.BlockSpec(memory_space=pltpu.SMEM)
ANY = pl.BlockSpec(memory_space=pl.ANY)


def window(start, width):
    base = min(start // LANES * LANES, width - WIN)
    return base, start - base


def tight_window(start, width):
    if start % LANES + HD <= LANES:
        return start // LANES * LANES, start % LANES, LANES
    return (*window(start, width), WIN)


def iota(shape, axis):
    return lax.broadcasted_iota(jnp.int32, shape, axis)


def params(mib):
    return pltpu.CompilerParams(vmem_limit_bytes=mib * 1024 * 1024)


def transpose_into(target, source):
    rows, cols = source.shape
    for c in range(0, cols, LANES):
        for r in range(0, rows, LANES):
            target[c : c + LANES, r : r + LANES] = source[r : r + LANES, c : c + LANES].T


def as_column(row):
    n = row.shape[1]
    same = iota((n, n), 0) == iota((n, n), 1)
    return jnp.sum(jnp.where(same, row, 0), axis=1, keepdims=True)


def slots_of(groups, half, side, slot_count):
    n = groups.shape[1]
    quarter = half // 2
    earlier = iota((n, n), 0) < iota((n, n), 1)
    same = (as_column(groups) == groups) & earlier
    rank = jnp.sum(jnp.where(same, 1, 0), axis=0, keepdims=True)
    upper = jnp.where(groups >= half, 1, 0)
    far = jnp.where(upper != side, 1, 0)
    host = groups - upper * half + far * quarter
    host = jnp.where(host >= half, host - half, host)
    return host * slot_count + rank, far


def place_kernel(
    half, slot_count, groups_hbm, q_hbm, out_ref, token_ref, groups_ref, q_ref,
    group_sem, in_sems
):
    n, width = q_ref.shape
    steps = in_sems.shape[0]
    chunk = width // steps
    groups_copy = pltpu.make_async_copy(groups_hbm, groups_ref, group_sem)
    groups_copy.start()
    arrivals = []
    for i in range(steps):
        cols = pl.ds(i * chunk, chunk)
        arrivals.append(pltpu.make_async_copy(q_hbm.at[:, cols], q_ref.at[:, cols], in_sems.at[i]))
        arrivals[i].start()
    token_ref[...] = jnp.zeros_like(token_ref)
    side = lax.axis_index("req") // half
    groups_copy.wait()
    slot, far = slots_of(groups_ref[...], half, side, slot_count)
    hit = slot == iota((n, n), 0)
    own = jnp.where(hit & (far == 0), 1.0, 0.0).astype(jnp.bfloat16)
    other = jnp.where(hit & (far == 1), 1.0, 0.0).astype(jnp.bfloat16)
    spread = jnp.concatenate([own, other], axis=0)
    for i, arrival in enumerate(arrivals):
        arrival.wait()
        both = jnp.dot(
            spread, q_ref[:, i * chunk : (i + 1) * chunk], preferred_element_type=jnp.float32
        ).astype(jnp.bfloat16)
        for part in range(2):
            cols = pl.ds(part * width + i * chunk, chunk)
            out_ref[:, cols] = both[part * n : (part + 1) * n]


def place(queries, groups, half, slot_count):
    n, width = queries.shape
    steps = 2
    return pl.pallas_call(
        functools.partial(place_kernel, half, slot_count),
        out_shape=(
            jax.ShapeDtypeStruct((n, 2 * width), queries.dtype),
            jax.ShapeDtypeStruct((8, LANES), jnp.float32),
        ),
        in_specs=[ANY, ANY],
        out_specs=(VMEM, VMEM),
        scratch_shapes=[
            pltpu.VMEM(groups.shape, groups.dtype),
            pltpu.VMEM((n, width), queries.dtype),
            pltpu.SemaphoreType.DMA(()),
            pltpu.SemaphoreType.DMA((steps,)),
        ],
        compiler_params=params(60),
        cost_estimate=pl.CostEstimate(
            flops=4 * n * n * width, bytes_accessed=6 * n * width, transcendentals=0
        ),
        name="place",
    )(groups, queries)


def clear_queries(qs_ref, i, first, size):
    width = qs_ref.shape[2]
    if first:
        qs_ref[i, :first] = jnp.zeros((first, width), jnp.bfloat16)
    if first + HD < size:
        qs_ref[i, first + HD : size] = jnp.zeros((size - first - HD, width), jnp.bfloat16)


def fill_queries(qs_ref, i, qt_ref, k, first):
    n = qt_ref.shape[1]
    for g in range(GROUP):
        row = (k * GROUP + g) * HD
        qs_ref[i, first : first + HD, g * n : (g + 1) * n] = qt_ref[row : row + HD]


def prefix_kernel(
    quarter, rows_hbm, near_k, near_v, outer_k, outer_v, inner_k, inner_v, after_ref, out_hbm,
    rows_ref, k_ref, v_ref, qt_ref, vt_ref, qs_ref, ot_ref, lse_ref, scores_ref, out_ref,
    in_sems, out_sems
):
    del after_ref
    n, width = rows_ref.shape
    width //= 2
    key_width = k_ref.shape[2]
    place = lax.axis_index("req") // quarter
    is_outer = (place == 0) | (place == 3)
    arrivals = []

    def arrive(target, source, inner=None):
        sem = in_sems.at[len(arrivals)]
        arrivals.append(pltpu.make_async_copy(source, target, sem))
        if inner is None:
            arrivals[-1].start()
            return
        pl.when(is_outer)(arrivals[-1].start)
        pl.when(jnp.logical_not(is_outer))(pltpu.make_async_copy(inner, target, sem).start)

    arrive(v_ref.at[0], near_v)
    arrive(rows_ref.at[:, :width], rows_hbm.at[:, :width])
    arrive(k_ref.at[0], near_k)
    arrive(v_ref.at[1], outer_v, inner_v)
    arrive(rows_ref.at[:, width:], rows_hbm.at[:, width:])
    arrive(k_ref.at[1], outer_k, inner_k)
    windows = [tight_window(k * HD, key_width) for k in range(KVH)]
    for u in range(2 * KVH):
        clear_queries(qs_ref, u, *windows[u % KVH][1:])

    def prepare(part):
        arrivals[3 * part].wait()
        transpose_into(vt_ref.at[part], v_ref.at[part])
        arrivals[3 * part + 1].wait()
        transpose_into(qt_ref.at[part * width : (part + 1) * width], rows_ref.at[:, part * width : (part + 1) * width])
        for k in range(KVH):
            fill_queries(qs_ref, part * KVH + k, qt_ref.at[part * width : (part + 1) * width], k, windows[k][1])
        arrivals[3 * part + 2].wait()

    def score(u):
        part, k = divmod(u, KVH)
        base, _, size = windows[k]
        scores = jnp.dot(
            k_ref[part, :, base : base + size], qs_ref[u, :size], preferred_element_type=jnp.float32
        )
        scores_ref[u % 2] = scores * SCALE

    def weigh(u):
        part, k = divmod(u, KVH)
        scores = scores_ref[u % 2]
        top = jnp.max(scores, axis=0, keepdims=True)
        weights = jnp.exp2(scores - top)
        total = jnp.sum(weights, axis=0, keepdims=True)
        summed = jnp.dot(
            vt_ref[part, k * HD : (k + 1) * HD],
            weights.astype(jnp.bfloat16),
            preferred_element_type=jnp.float32,
        )
        result = (summed * (1.0 / total)).astype(jnp.bfloat16)
        lse = (top + jnp.log2(total)) * LN2
        for g in range(GROUP):
            head = k * GROUP + g
            ot_ref[head * HD : (head + 1) * HD] = result[:, g * n : (g + 1) * n]
            lse_ref[part * H + head : part * H + head + 1] = lse[:, g * n : (g + 1) * n]

    def depart(cols):
        departures.append(
            pltpu.make_async_copy(
                out_ref.at[:, cols], out_hbm.at[:, cols], out_sems.at[len(departures)]
            )
        )
        departures[-1].start()

    def send(u):
        part, k = divmod(u, KVH)
        quarter = width // 4
        first = k // 2 * quarter
        cols = pl.ds(part * width + first, quarter)
        transpose_into(out_ref.at[:, cols], ot_ref.at[first : first + quarter])
        depart(cols)
        if u < 2 * KVH - 1:
            return
        lse = lse_ref[...]
        high = lse.astype(jnp.bfloat16).astype(jnp.float32)
        rest = lse - high
        pieces = jnp.concatenate([high[:H], rest[:H], high[H:], rest[H:]], axis=0)
        cols = pl.ds(2 * width, LANES)
        out_ref[:, cols] = pieces.T.astype(jnp.bfloat16)
        depart(cols)

    departures = []
    prepare(0)
    score(0)
    prepare(1)
    for u in range(2 * KVH):
        if u + 1 < 2 * KVH:
            score(u + 1)
        weigh(u)
        if u % 2:
            send(u)
    for departure in departures:
        departure.wait()


def prefix_part(quarter, rows, near, outer, inner, after):
    n, width = rows.shape
    width //= 2
    tokens, key_width = near[0].shape
    return pl.pallas_call(
        functools.partial(prefix_kernel, quarter),
        out_shape=jax.ShapeDtypeStruct((n, 2 * width + LANES), jnp.bfloat16),
        in_specs=[ANY] * 8,
        out_specs=ANY,
        scratch_shapes=[
            pltpu.VMEM(rows.shape, rows.dtype),
            pltpu.VMEM((2, tokens, key_width), jnp.bfloat16),
            pltpu.VMEM((2, tokens, key_width), jnp.bfloat16),
            pltpu.VMEM((2 * width, n), jnp.bfloat16),
            pltpu.VMEM((2, key_width, tokens), jnp.bfloat16),
            pltpu.VMEM((2 * KVH, WIN, GROUP * n), jnp.bfloat16),
            pltpu.VMEM((width, n), jnp.bfloat16),
            pltpu.VMEM((2 * H, n), jnp.float32),
            pltpu.VMEM((2, tokens, GROUP * n), jnp.float32),
            pltpu.VMEM((n, 2 * width + LANES), jnp.bfloat16),
            pltpu.SemaphoreType.DMA((6,)),
            pltpu.SemaphoreType.DMA((9,)),
        ],
        compiler_params=params(24),
        cost_estimate=pl.CostEstimate(
            flops=16000 * n * 256 * width,
            bytes_accessed=8 * n * width * 2,
            transcendentals=n * 512 * H,
        ),
        name="prefix",
    )(rows, *near, *outer, *inner, after)


def fill_bias(bias_ref, pages, lengths, page_size):
    most, n = pages.shape
    page_count = bias_ref.shape[0] // page_size
    page = iota((page_count, n), 0)
    full = jnp.zeros((page_count, n), jnp.float32)
    partial = jnp.zeros((page_count, n), jnp.float32)
    for j in range(most):
        same = pages[j : j + 1] == page
        whole = lengths >= (j + 1) * page_size
        some = (lengths > j * page_size) & (lengths < (j + 1) * page_size)
        full += jnp.where(same & whole, 1.0, 0.0)
        partial += jnp.where(same & some, 1.0, 0.0)
    seen = jnp.where(iota((page_size, n), 0) < lengths % page_size, 1.0, 0.0)
    for p in range(page_count):
        multiple = full[p : p + 1] + seen * partial[p : p + 1]
        bias_ref[p * page_size : (p + 1) * page_size] = jnp.where(
            multiple > 0.0, jnp.log2(jnp.maximum(multiple, 1.0)), NEVER
        )


def private_kernel(
    page_size, q_hbm, k_hbm, v_hbm, pages_ref, lengths_ref, *refs
):
    (
        out_ref, lse_ref, q_ref, k_ref, v_ref, qt_ref, vt_ref, qs_ref, bias_ref, ot_ref, lses_ref,
        scores_a, scores_b, top_a, top_b, weights_ref, sems,
    ) = refs[-17:]
    copies = [
        pltpu.make_async_copy(source, target, sems.at[i])
        for i, (source, target) in enumerate(((q_hbm, q_ref), (k_hbm, k_ref), (v_hbm, v_ref)))
    ]
    for copy in copies:
        copy.start()
    n = q_ref.shape[0]
    tokens, key_width = k_ref.shape
    rows = GROUP * n
    tile = 256
    fill_bias(bias_ref, pages_ref[...], lengths_ref[...], page_size)
    copies[0].wait()
    transpose_into(qt_ref, q_ref)
    for k in range(KVH):
        _, first = window(k * HD, key_width)
        clear_queries(qs_ref, k, first, WIN)
        fill_queries(qs_ref, k, qt_ref, k, first)
    copies[1].wait()

    def score(k, scores_ref, top_ref):
        base = pl.multiple_of(jnp.minimum(k * HD // LANES * LANES, key_width - WIN), LANES)
        top = None
        for t in range(0, tokens, tile):
            scores = jnp.dot(
                k_ref[t : t + tile, pl.ds(base, WIN)],
                qs_ref[k],
                preferred_element_type=jnp.float32,
            )
            bias = bias_ref[t : t + tile]
            scores = scores * SCALE + jnp.concatenate([bias] * GROUP, axis=1)
            scores_ref[t : t + tile] = scores
            highest = jnp.max(scores.reshape(tile // 8, 8, rows), axis=0)
            top = highest if top is None else jnp.maximum(top, highest)
        top_ref[...] = top

    def weigh(k, scores_ref, top_ref, lses):
        top = jnp.max(top_ref[...], axis=0, keepdims=True)
        total = jnp.zeros((8, rows), jnp.float32)
        for t in range(0, tokens, tile):
            weights = jnp.exp2(scores_ref[t : t + tile] - top)
            total += jnp.sum(weights.reshape(tile // 8, 8, rows), axis=0)
            weights_ref[t : t + tile] = weights.astype(jnp.bfloat16)
        total = jnp.sum(total, axis=0, keepdims=True)
        values = vt_ref[pl.ds(pl.multiple_of(k * HD, 16), HD)]
        summed = jnp.dot(values, weights_ref[...], preferred_element_type=jnp.float32)
        result = summed * (1.0 / total)
        lse = (top + jnp.log2(total)) * LN2
        row = iota(lses.shape, 0)
        for g in range(GROUP):
            head = k * GROUP + g
            ot_ref[pl.ds(pl.multiple_of(head * HD, 16), HD)] = result[:, g * n : (g + 1) * n]
            lses = jnp.where(row == head, lse[:, g * n : (g + 1) * n], lses)
        return lses

    score(0, scores_a, top_a)
    copies[2].wait()
    transpose_into(vt_ref, v_ref)

    def two(j, lses):
        k = 2 * j
        score(k + 1, scores_b, top_b)
        lses = weigh(k, scores_a, top_a, lses)
        score(jnp.minimum(k + 2, KVH - 1), scores_a, top_a)
        return weigh(k + 1, scores_b, top_b, lses)

    lses_ref[...] = jnp.zeros_like(lses_ref)
    lses_ref[:H] = lax.fori_loop(0, KVH // 2, two, jnp.zeros((H, n), jnp.float32))
    lse_ref[...] = lses_ref[...].T
    transpose_into(out_ref, ot_ref)


def private_part(queries, keys, values, pages, lengths, after, page_size):
    n, width = queries.shape
    tokens, key_width = keys.shape
    return pl.pallas_call(
        functools.partial(private_kernel, page_size),
        out_shape=(
            jax.ShapeDtypeStruct((n, width), jnp.float32),
            jax.ShapeDtypeStruct((n, LANES), jnp.float32),
        ),
        in_specs=[ANY] * 3 + [VMEM] * 2 + [ANY] * len(after),
        out_specs=(VMEM, VMEM),
        scratch_shapes=[
            pltpu.VMEM(queries.shape, queries.dtype),
            pltpu.VMEM(keys.shape, keys.dtype),
            pltpu.VMEM(values.shape, values.dtype),
            pltpu.VMEM((width, n), jnp.bfloat16),
            pltpu.VMEM((key_width, tokens), jnp.bfloat16),
            pltpu.VMEM((KVH, WIN, GROUP * n), jnp.bfloat16),
            pltpu.VMEM((tokens, n), jnp.float32),
            pltpu.VMEM((width, n), jnp.float32),
            pltpu.VMEM((LANES, n), jnp.float32),
            pltpu.VMEM((tokens, GROUP * n), jnp.float32),
            pltpu.VMEM((tokens, GROUP * n), jnp.float32),
            pltpu.VMEM((8, GROUP * n), jnp.float32),
            pltpu.VMEM((8, GROUP * n), jnp.float32),
            pltpu.VMEM((tokens, GROUP * n), jnp.bfloat16),
            pltpu.SemaphoreType.DMA((3,)),
        ],
        compiler_params=params(48),
        cost_estimate=pl.CostEstimate(
            flops=1200 * n * tokens * H * WIN,
            bytes_accessed=4 * tokens * key_width,
            transcendentals=n * tokens * H,
        ),
        name="private",
    )(queries, keys, values, pages, lengths, *after)


def expand_heads(share, width):
    n = share.shape[0]
    lane = iota((n, LANES), 1)
    share = jnp.where(lane < H, share, 0.0)
    high = share.astype(jnp.bfloat16).astype(jnp.float32)
    both = (high + pltpu.roll(share - high, H, 1)).astype(jnp.bfloat16)
    row = iota((LANES, width), 0)
    head = jnp.where(row >= H, row - H, row)
    first = head * HD
    column = iota((LANES, width), 1)
    spread = (row < 2 * H) & (column >= first) & (column < first + HD)
    return jnp.dot(
        both, jnp.where(spread, 1.0, 0.0).astype(jnp.bfloat16), preferred_element_type=jnp.float32
    )


def row_blocks(rows):
    blocks, first = [], 0
    while first < rows:
        rest = rows - first
        size = min(1024, max(WIN, rest // 2 // WIN * WIN))
        blocks.append(slice(first, first + size))
        first += size
    return blocks


def finish_kernel(
    half, slot_count, live_ref, groups_ref, back_ref, private_ref, private_lse_ref, w_hbm,
    out_hbm, w_ref, sum_ref, out_ref, in_sems, out_sems
):
    n, width = out_ref.shape
    blocks = row_blocks(width)
    arrivals = []
    for i, block in enumerate(blocks):
        arrivals.append(pltpu.make_async_copy(w_hbm.at[block], w_ref.at[block], in_sems.at[i]))
        arrivals[i].start()
    side = lax.axis_index("req") // half
    slot, far = slots_of(groups_ref[...], half, side, slot_count)
    slot, far = as_column(slot), as_column(far)
    hit = slot == iota((n, n), 1)
    own = jnp.where(hit & (far == 0), 1.0, 0.0).astype(jnp.bfloat16)
    other = jnp.where(hit & (far == 1), 1.0, 0.0).astype(jnp.bfloat16)
    tile = back_ref[:, 2 * width :]
    lane = iota((n, LANES), 1)
    pieces = jnp.where(
        lane < 2 * H,
        jnp.dot(own, tile, preferred_element_type=jnp.float32),
        jnp.dot(other, tile, preferred_element_type=jnp.float32),
    )
    prefix_lse = pieces
    for i in range(1, LANES // H):
        prefix_lse += pltpu.roll(pieces, LANES - i * H, 1)
    prefix_lse = jnp.where(lane < H, prefix_lse, 0.0)
    private_lse = private_lse_ref[...]
    top = jnp.maximum(prefix_lse, private_lse)
    a, b = jnp.exp(prefix_lse - top), jnp.exp(private_lse - top)
    prefix_share = expand_heads(a / (a + b), width)
    private_share = expand_heads(b / (a + b), width)
    pick = jnp.concatenate([own, other], axis=1)
    both = jnp.concatenate([back_ref[:, :width], back_ref[:, width : 2 * width]], axis=0)
    prefix = jnp.dot(pick, both, preferred_element_type=jnp.float32)
    attended = prefix_share * prefix + private_share * private_ref[...]
    attended = attended.astype(jnp.bfloat16)
    is_live = iota((n, 1), 0) < live_ref[0]
    departures = []
    for i, (arrival, block) in enumerate(zip(arrivals, blocks)):
        arrival.wait()
        for j in range(out_sems.shape[0]):
            chunk = width // out_sems.shape[0]
            cols = pl.ds(j * chunk, chunk)
            projected = jnp.dot(
                attended[:, block], w_ref[block, cols], preferred_element_type=jnp.float32
            )
            if i:
                projected += sum_ref[:, cols]
            if i < len(blocks) - 1:
                sum_ref[:, cols] = projected
                continue
            out_ref[:, cols] = jnp.where(is_live, projected, 0.0).astype(out_ref.dtype)
            departures.append(
                pltpu.make_async_copy(out_ref.at[:, cols], out_hbm.at[:, cols], out_sems.at[j])
            )
            departures[-1].start()
    for departure in departures:
        departure.wait()


def finish(live, groups, back, private, private_lse, weight, half, slot_count):
    n = back.shape[0]
    width = weight.shape[1]
    steps = len(row_blocks(width))
    return pl.pallas_call(
        functools.partial(finish_kernel, half, slot_count),
        out_shape=jax.ShapeDtypeStruct((n, width), jnp.bfloat16),
        in_specs=[SMEM] + [VMEM] * 4 + [ANY],
        out_specs=ANY,
        scratch_shapes=[
            pltpu.VMEM(weight.shape, weight.dtype),
            pltpu.VMEM((n, width), jnp.float32),
            pltpu.VMEM((n, width), jnp.bfloat16),
            pltpu.SemaphoreType.DMA((steps,)),
            pltpu.SemaphoreType.DMA((5,)),
        ],
        compiler_params=params(50),
        cost_estimate=pl.CostEstimate(
            flops=2 * n * width * width, bytes_accessed=2 * width * width, transcendentals=0
        ),
        name="finish",
    )(live, groups, back, private, private_lse, weight)


def per_device(
    queries,
    prefix_keys,
    prefix_values,
    pool_keys,
    pool_values,
    page_table,
    private_length,
    group_ids,
    live_rows,
    out_weight,
):
    devices = lax.axis_size("req")
    half = devices // 2
    row_count, width = queries.shape
    slot_count = 2 * row_count // devices
    page_size = pool_keys.shape[1]
    halves = [list(range(half)), list(range(half, devices))]
    quarter = devices // 4
    mirror = [(i, (3 - i // quarter) * quarter + i % quarter) for i in range(devices)]
    outer_pairs = [pair for pair in mirror if pair[0] // quarter in (0, 3)]
    inner_pairs = [pair for pair in mirror if pair[0] // quarter in (1, 2)]

    groups = group_ids.reshape(1, row_count)
    lengths = private_length.reshape(1, row_count)
    pages = page_table.T
    flat_keys = pool_keys.reshape(-1, pool_keys.shape[2])
    flat_values = pool_values.reshape(-1, pool_values.shape[2])

    def exchange(rows):
        blocks = rows.reshape(half, slot_count, rows.shape[1])
        blocks = lax.all_to_all(
            blocks, "req", split_axis=0, concat_axis=0, tiled=True, axis_index_groups=halves
        )
        return blocks.reshape(rows.shape)

    prompt = (prefix_keys, prefix_values)
    outer = [lax.ppermute(x, "req", outer_pairs) for x in prompt]
    inner = [lax.ppermute(x, "req", inner_pairs) for x in prompt]
    placed, token = place(queries, groups, half, slot_count)
    rows = exchange(placed)
    private, private_lse = private_part(
        queries, flat_keys, flat_values, pages, lengths, (token, outer[0]), page_size
    )
    out = prefix_part(quarter, rows, prompt, outer, inner, private_lse)
    back = exchange(out)
    return finish(
        live_rows, groups, back, private, private_lse, out_weight, half, slot_count
    )


def solution(mesh):
    placed = (
        P("req", None),
        P("req", None),
        P("req", None),
        P("req", None, None),
        P("req", None, None),
        P("req", None),
        P("req"),
        P("req", None),
        P("req"),
        P(),
    )
    return jax.shard_map(
        per_device, mesh=mesh, in_specs=placed, out_specs=P("req", None), check_vma=False
    )
```

```python
import functools
import math

import jax
import jax.numpy as jnp
from jax import lax
from jax.experimental import pallas as pl
from jax.experimental.pallas import tpu as pltpu
from jax.sharding import PartitionSpec as P

H = 32
KVH = 8
HD = 80
GROUP = H // KVH
LANES = 128
WIN = 256
SCALE = HD ** (-0.5) * math.log2(math.e)
LN2 = math.log(2.0)
NEVER = -1e30
VMEM = pl.BlockSpec(memory_space=pltpu.VMEM)
SMEM = pl.BlockSpec(memory_space=pltpu.SMEM)
ANY = pl.BlockSpec(memory_space=pl.ANY)


def window(start, width):
    base = min(start // LANES * LANES, width - WIN)
    return base, start - base


def tight_window(start, width):
    if start % LANES + HD <= LANES:
        return start // LANES * LANES, start % LANES, LANES
    return (*window(start, width), WIN)


def iota(shape, axis):
    return lax.broadcasted_iota(jnp.int32, shape, axis)


def params(mib):
    return pltpu.CompilerParams(vmem_limit_bytes=mib * 1024 * 1024)


def transpose_into(target, source):
    rows, cols = source.shape
    for c in range(0, cols, LANES):
        for r in range(0, rows, LANES):
            target[c : c + LANES, r : r + LANES] = source[r : r + LANES, c : c + LANES].T


def as_column(row):
    n = row.shape[1]
    same = iota((n, n), 0) == iota((n, n), 1)
    return jnp.sum(jnp.where(same, row, 0), axis=1, keepdims=True)


def slots_of(groups, half, side, slot_count):
    n = groups.shape[1]
    quarter = half // 2
    earlier = iota((n, n), 0) < iota((n, n), 1)
    same = (as_column(groups) == groups) & earlier
    rank = jnp.sum(jnp.where(same, 1, 0), axis=0, keepdims=True)
    upper = jnp.where(groups >= half, 1, 0)
    far = jnp.where(upper != side, 1, 0)
    host = groups - upper * half + far * quarter
    host = jnp.where(host >= half, host - half, host)
    return host * slot_count + rank, far


def place_kernel(
    half, slot_count, groups_hbm, q_hbm, out_ref, token_ref, groups_ref, q_ref,
    group_sem, in_sems
):
    n, width = q_ref.shape
    steps = in_sems.shape[0]
    chunk = width // steps
    groups_copy = pltpu.make_async_copy(groups_hbm, groups_ref, group_sem)
    groups_copy.start()
    arrivals = []
    for i in range(steps):
        cols = pl.ds(i * chunk, chunk)
        arrivals.append(pltpu.make_async_copy(q_hbm.at[:, cols], q_ref.at[:, cols], in_sems.at[i]))
        arrivals[i].start()
    token_ref[...] = jnp.zeros_like(token_ref)
    side = lax.axis_index("req") // half
    groups_copy.wait()
    slot, far = slots_of(groups_ref[...], half, side, slot_count)
    hit = slot == iota((n, n), 0)
    own = jnp.where(hit & (far == 0), 1.0, 0.0).astype(jnp.bfloat16)
    other = jnp.where(hit & (far == 1), 1.0, 0.0).astype(jnp.bfloat16)
    spread = jnp.concatenate([own, other], axis=0)
    for i, arrival in enumerate(arrivals):
        arrival.wait()
        both = jnp.dot(
            spread, q_ref[:, i * chunk : (i + 1) * chunk], preferred_element_type=jnp.float32
        ).astype(jnp.bfloat16)
        for part in range(2):
            cols = pl.ds(part * width + i * chunk, chunk)
            out_ref[:, cols] = both[part * n : (part + 1) * n]


def place(queries, groups, half, slot_count):
    n, width = queries.shape
    steps = 1
    return pl.pallas_call(
        functools.partial(place_kernel, half, slot_count),
        out_shape=(
            jax.ShapeDtypeStruct((n, 2 * width), queries.dtype),
            jax.ShapeDtypeStruct((8, LANES), jnp.float32),
        ),
        in_specs=[ANY, ANY],
        out_specs=(VMEM, VMEM),
        scratch_shapes=[
            pltpu.VMEM(groups.shape, groups.dtype),
            pltpu.VMEM((n, width), queries.dtype),
            pltpu.SemaphoreType.DMA(()),
            pltpu.SemaphoreType.DMA((steps,)),
        ],
        compiler_params=params(60),
        cost_estimate=pl.CostEstimate(
            flops=4 * n * n * width, bytes_accessed=6 * n * width, transcendentals=0
        ),
        name="place",
    )(groups, queries)


def clear_queries(qs_ref, i, first, size):
    width = qs_ref.shape[2]
    if first:
        qs_ref[i, :first] = jnp.zeros((first, width), jnp.bfloat16)
    if first + HD < size:
        qs_ref[i, first + HD : size] = jnp.zeros((size - first - HD, width), jnp.bfloat16)


def fill_queries(qs_ref, i, qt_ref, k, first):
    n = qt_ref.shape[1]
    for g in range(GROUP):
        row = (k * GROUP + g) * HD
        qs_ref[i, first : first + HD, g * n : (g + 1) * n] = qt_ref[row : row + HD]


def prefix_kernel(
    quarter, rows_hbm, near_k, near_v, outer_k, outer_v, inner_k, inner_v, after_ref, out_hbm,
    rows_ref, k_ref, v_ref, qt_ref, vt_ref, qs_ref, ot_ref, lse_ref, scores_ref, out_ref,
    in_sems, out_sems
):
    del after_ref
    n, width = rows_ref.shape
    width //= 2
    key_width = k_ref.shape[2]
    place = lax.axis_index("req") // quarter
    is_outer = (place == 0) | (place == 3)
    arrivals = []

    def arrive(target, source, inner=None):
        sem = in_sems.at[len(arrivals)]
        arrivals.append(pltpu.make_async_copy(source, target, sem))
        if inner is None:
            arrivals[-1].start()
            return
        pl.when(is_outer)(arrivals[-1].start)
        pl.when(jnp.logical_not(is_outer))(pltpu.make_async_copy(inner, target, sem).start)

    arrive(v_ref.at[0], near_v)
    arrive(rows_ref.at[:, :width], rows_hbm.at[:, :width])
    arrive(k_ref.at[0], near_k)
    arrive(v_ref.at[1], outer_v, inner_v)
    arrive(rows_ref.at[:, width:], rows_hbm.at[:, width:])
    arrive(k_ref.at[1], outer_k, inner_k)
    windows = [tight_window(k * HD, key_width) for k in range(KVH)]
    for u in range(2 * KVH):
        clear_queries(qs_ref, u, *windows[u % KVH][1:])

    def prepare(part):
        arrivals[3 * part].wait()
        transpose_into(vt_ref.at[part], v_ref.at[part])
        arrivals[3 * part + 1].wait()
        transpose_into(qt_ref.at[part * width : (part + 1) * width], rows_ref.at[:, part * width : (part + 1) * width])
        for k in range(KVH):
            fill_queries(qs_ref, part * KVH + k, qt_ref.at[part * width : (part + 1) * width], k, windows[k][1])
        arrivals[3 * part + 2].wait()

    def score(u):
        part, k = divmod(u, KVH)
        base, _, size = windows[k]
        scores = jnp.dot(
            k_ref[part, :, base : base + size], qs_ref[u, :size], preferred_element_type=jnp.float32
        )
        scores_ref[u % 2] = scores * SCALE

    def weigh(u):
        part, k = divmod(u, KVH)
        scores = scores_ref[u % 2]
        top = jnp.max(scores, axis=0, keepdims=True)
        weights = jnp.exp2(scores - top)
        total = jnp.sum(weights, axis=0, keepdims=True)
        summed = jnp.dot(
            vt_ref[part, k * HD : (k + 1) * HD],
            weights.astype(jnp.bfloat16),
            preferred_element_type=jnp.float32,
        )
        result = (summed * (1.0 / total)).astype(jnp.bfloat16)
        lse = (top + jnp.log2(total)) * LN2
        for g in range(GROUP):
            head = k * GROUP + g
            ot_ref[head * HD : (head + 1) * HD] = result[:, g * n : (g + 1) * n]
            lse_ref[part * H + head : part * H + head + 1] = lse[:, g * n : (g + 1) * n]

    def depart(cols):
        departures.append(
            pltpu.make_async_copy(
                out_ref.at[:, cols], out_hbm.at[:, cols], out_sems.at[len(departures)]
            )
        )
        departures[-1].start()

    def send(u):
        part, k = divmod(u, KVH)
        quarter = width // 4
        first = k // 2 * quarter
        cols = pl.ds(part * width + first, quarter)
        transpose_into(out_ref.at[:, cols], ot_ref.at[first : first + quarter])
        depart(cols)
        if u < 2 * KVH - 1:
            return
        lse = lse_ref[...]
        high = lse.astype(jnp.bfloat16).astype(jnp.float32)
        rest = lse - high
        pieces = jnp.concatenate([high[:H], rest[:H], high[H:], rest[H:]], axis=0)
        cols = pl.ds(2 * width, LANES)
        out_ref[:, cols] = pieces.T.astype(jnp.bfloat16)
        depart(cols)

    departures = []
    prepare(0)
    score(0)
    prepare(1)
    for u in range(2 * KVH):
        if u + 1 < 2 * KVH:
            score(u + 1)
        weigh(u)
        if u % 2:
            send(u)
    for departure in departures:
        departure.wait()


def prefix_part(quarter, rows, near, outer, inner, after):
    n, width = rows.shape
    width //= 2
    tokens, key_width = near[0].shape
    return pl.pallas_call(
        functools.partial(prefix_kernel, quarter),
        out_shape=jax.ShapeDtypeStruct((n, 2 * width + LANES), jnp.bfloat16),
        in_specs=[ANY] * 8,
        out_specs=ANY,
        scratch_shapes=[
            pltpu.VMEM(rows.shape, rows.dtype),
            pltpu.VMEM((2, tokens, key_width), jnp.bfloat16),
            pltpu.VMEM((2, tokens, key_width), jnp.bfloat16),
            pltpu.VMEM((2 * width, n), jnp.bfloat16),
            pltpu.VMEM((2, key_width, tokens), jnp.bfloat16),
            pltpu.VMEM((2 * KVH, WIN, GROUP * n), jnp.bfloat16),
            pltpu.VMEM((width, n), jnp.bfloat16),
            pltpu.VMEM((2 * H, n), jnp.float32),
            pltpu.VMEM((2, tokens, GROUP * n), jnp.float32),
            pltpu.VMEM((n, 2 * width + LANES), jnp.bfloat16),
            pltpu.SemaphoreType.DMA((6,)),
            pltpu.SemaphoreType.DMA((9,)),
        ],
        compiler_params=params(24),
        cost_estimate=pl.CostEstimate(
            flops=16000 * n * 256 * width,
            bytes_accessed=8 * n * width * 2,
            transcendentals=n * 512 * H,
        ),
        name="prefix",
    )(rows, *near, *outer, *inner, after)


def fill_bias(bias_ref, pages, lengths, page_size):
    most, n = pages.shape
    page_count = bias_ref.shape[0] // page_size
    page = iota((page_count, n), 0)
    full = jnp.zeros((page_count, n), jnp.float32)
    partial = jnp.zeros((page_count, n), jnp.float32)
    for j in range(most):
        same = pages[j : j + 1] == page
        whole = lengths >= (j + 1) * page_size
        some = (lengths > j * page_size) & (lengths < (j + 1) * page_size)
        full += jnp.where(same & whole, 1.0, 0.0)
        partial += jnp.where(same & some, 1.0, 0.0)
    seen = jnp.where(iota((page_size, n), 0) < lengths % page_size, 1.0, 0.0)
    for p in range(page_count):
        multiple = full[p : p + 1] + seen * partial[p : p + 1]
        bias_ref[p * page_size : (p + 1) * page_size] = jnp.where(
            multiple > 0.0, jnp.log2(jnp.maximum(multiple, 1.0)), NEVER
        )


def private_kernel(
    page_size, q_hbm, k_hbm, v_hbm, pages_ref, lengths_ref, *refs
):
    (
        out_ref, lse_ref, q_ref, k_ref, v_ref, qt_ref, vt_ref, qs_ref, bias_ref, ot_ref, lses_ref,
        scores_a, scores_b, top_a, top_b, weights_ref, sems,
    ) = refs[-17:]
    copies = [
        pltpu.make_async_copy(source, target, sems.at[i])
        for i, (source, target) in enumerate(((q_hbm, q_ref), (k_hbm, k_ref), (v_hbm, v_ref)))
    ]
    for copy in copies:
        copy.start()
    n = q_ref.shape[0]
    tokens, key_width = k_ref.shape
    rows = GROUP * n
    tile = 256
    fill_bias(bias_ref, pages_ref[...], lengths_ref[...], page_size)
    copies[0].wait()
    transpose_into(qt_ref, q_ref)
    for k in range(KVH):
        _, first = window(k * HD, key_width)
        clear_queries(qs_ref, k, first, WIN)
        fill_queries(qs_ref, k, qt_ref, k, first)
    copies[1].wait()

    def score(k, scores_ref, top_ref):
        base = pl.multiple_of(jnp.minimum(k * HD // LANES * LANES, key_width - WIN), LANES)
        top = None
        for t in range(0, tokens, tile):
            scores = jnp.dot(
                k_ref[t : t + tile, pl.ds(base, WIN)],
                qs_ref[k],
                preferred_element_type=jnp.float32,
            )
            bias = bias_ref[t : t + tile]
            scores = scores * SCALE + jnp.concatenate([bias] * GROUP, axis=1)
            scores_ref[t : t + tile] = scores
            highest = jnp.max(scores.reshape(tile // 8, 8, rows), axis=0)
            top = highest if top is None else jnp.maximum(top, highest)
        top_ref[...] = top

    def weigh(k, scores_ref, top_ref, lses):
        top = jnp.max(top_ref[...], axis=0, keepdims=True)
        total = jnp.zeros((8, rows), jnp.float32)
        for t in range(0, tokens, tile):
            weights = jnp.exp2(scores_ref[t : t + tile] - top)
            total += jnp.sum(weights.reshape(tile // 8, 8, rows), axis=0)
            weights_ref[t : t + tile] = weights.astype(jnp.bfloat16)
        total = jnp.sum(total, axis=0, keepdims=True)
        values = vt_ref[pl.ds(pl.multiple_of(k * HD, 16), HD)]
        summed = jnp.dot(values, weights_ref[...], preferred_element_type=jnp.float32)
        result = summed * (1.0 / total)
        lse = (top + jnp.log2(total)) * LN2
        row = iota(lses.shape, 0)
        for g in range(GROUP):
            head = k * GROUP + g
            ot_ref[pl.ds(pl.multiple_of(head * HD, 16), HD)] = result[:, g * n : (g + 1) * n]
            lses = jnp.where(row == head, lse[:, g * n : (g + 1) * n], lses)
        return lses

    score(0, scores_a, top_a)
    copies[2].wait()
    transpose_into(vt_ref, v_ref)

    def two(j, lses):
        k = 2 * j
        score(k + 1, scores_b, top_b)
        lses = weigh(k, scores_a, top_a, lses)
        score(jnp.minimum(k + 2, KVH - 1), scores_a, top_a)
        return weigh(k + 1, scores_b, top_b, lses)

    lses_ref[...] = jnp.zeros_like(lses_ref)
    lses_ref[:H] = lax.fori_loop(0, KVH // 2, two, jnp.zeros((H, n), jnp.float32))
    lse_ref[...] = lses_ref[...].T
    transpose_into(out_ref, ot_ref)


def private_part(queries, keys, values, pages, lengths, after, page_size):
    n, width = queries.shape
    tokens, key_width = keys.shape
    return pl.pallas_call(
        functools.partial(private_kernel, page_size),
        out_shape=(
            jax.ShapeDtypeStruct((n, width), jnp.float32),
            jax.ShapeDtypeStruct((n, LANES), jnp.float32),
        ),
        in_specs=[ANY] * 3 + [VMEM] * 2 + [ANY] * len(after),
        out_specs=(VMEM, VMEM),
        scratch_shapes=[
            pltpu.VMEM(queries.shape, queries.dtype),
            pltpu.VMEM(keys.shape, keys.dtype),
            pltpu.VMEM(values.shape, values.dtype),
            pltpu.VMEM((width, n), jnp.bfloat16),
            pltpu.VMEM((key_width, tokens), jnp.bfloat16),
            pltpu.VMEM((KVH, WIN, GROUP * n), jnp.bfloat16),
            pltpu.VMEM((tokens, n), jnp.float32),
            pltpu.VMEM((width, n), jnp.float32),
            pltpu.VMEM((LANES, n), jnp.float32),
            pltpu.VMEM((tokens, GROUP * n), jnp.float32),
            pltpu.VMEM((tokens, GROUP * n), jnp.float32),
            pltpu.VMEM((8, GROUP * n), jnp.float32),
            pltpu.VMEM((8, GROUP * n), jnp.float32),
            pltpu.VMEM((tokens, GROUP * n), jnp.bfloat16),
            pltpu.SemaphoreType.DMA((3,)),
        ],
        compiler_params=params(48),
        cost_estimate=pl.CostEstimate(
            flops=1200 * n * tokens * H * WIN,
            bytes_accessed=4 * tokens * key_width,
            transcendentals=n * tokens * H,
        ),
        name="private",
    )(queries, keys, values, pages, lengths, *after)


def expand_heads(share, width):
    n = share.shape[0]
    lane = iota((n, LANES), 1)
    share = jnp.where(lane < H, share, 0.0)
    high = share.astype(jnp.bfloat16).astype(jnp.float32)
    both = (high + pltpu.roll(share - high, H, 1)).astype(jnp.bfloat16)
    row = iota((LANES, width), 0)
    head = jnp.where(row >= H, row - H, row)
    first = head * HD
    column = iota((LANES, width), 1)
    spread = (row < 2 * H) & (column >= first) & (column < first + HD)
    return jnp.dot(
        both, jnp.where(spread, 1.0, 0.0).astype(jnp.bfloat16), preferred_element_type=jnp.float32
    )


def row_blocks(rows):
    blocks, first = [], 0
    while first < rows:
        rest = rows - first
        size = min(512, max(LANES, rest // 2 // LANES * LANES))
        blocks.append(slice(first, first + size))
        first += size
    return blocks


def finish_kernel(
    half, slot_count, live_ref, groups_ref, back_ref, private_ref, private_lse_ref, w_hbm,
    out_hbm, w_ref, sum_ref, out_ref, in_sems, out_sems
):
    n, width = out_ref.shape
    blocks = row_blocks(width)
    arrivals = []
    for i, block in enumerate(blocks):
        arrivals.append(pltpu.make_async_copy(w_hbm.at[block], w_ref.at[block], in_sems.at[i]))
        arrivals[i].start()
    side = lax.axis_index("req") // half
    slot, far = slots_of(groups_ref[...], half, side, slot_count)
    slot, far = as_column(slot), as_column(far)
    hit = slot == iota((n, n), 1)
    own = jnp.where(hit & (far == 0), 1.0, 0.0).astype(jnp.bfloat16)
    other = jnp.where(hit & (far == 1), 1.0, 0.0).astype(jnp.bfloat16)
    tile = back_ref[:, 2 * width :]
    lane = iota((n, LANES), 1)
    pieces = jnp.where(
        lane < 2 * H,
        jnp.dot(own, tile, preferred_element_type=jnp.float32),
        jnp.dot(other, tile, preferred_element_type=jnp.float32),
    )
    prefix_lse = pieces
    for i in range(1, LANES // H):
        prefix_lse += pltpu.roll(pieces, LANES - i * H, 1)
    prefix_lse = jnp.where(lane < H, prefix_lse, 0.0)
    private_lse = private_lse_ref[...]
    top = jnp.maximum(prefix_lse, private_lse)
    a, b = jnp.exp(prefix_lse - top), jnp.exp(private_lse - top)
    prefix_share = expand_heads(a / (a + b), width)
    private_share = expand_heads(b / (a + b), width)
    pick = jnp.concatenate([own, other], axis=1)
    both = jnp.concatenate([back_ref[:, :width], back_ref[:, width : 2 * width]], axis=0)
    prefix = jnp.dot(pick, both, preferred_element_type=jnp.float32)
    attended = prefix_share * prefix + private_share * private_ref[...]
    attended = attended.astype(jnp.bfloat16)
    is_live = iota((n, 1), 0) < live_ref[0]
    departures = []
    for i, (arrival, block) in enumerate(zip(arrivals, blocks)):
        arrival.wait()
        for j in range(out_sems.shape[0]):
            chunk = width // out_sems.shape[0]
            cols = pl.ds(j * chunk, chunk)
            projected = jnp.dot(
                attended[:, block], w_ref[block, cols], preferred_element_type=jnp.float32
            )
            if i:
                projected += sum_ref[:, cols]
            if i < len(blocks) - 1:
                sum_ref[:, cols] = projected
                continue
            out_ref[:, cols] = jnp.where(is_live, projected, 0.0).astype(out_ref.dtype)
            departures.append(
                pltpu.make_async_copy(out_ref.at[:, cols], out_hbm.at[:, cols], out_sems.at[j])
            )
            departures[-1].start()
    for departure in departures:
        departure.wait()


def finish(live, groups, back, private, private_lse, weight, half, slot_count):
    n = back.shape[0]
    width = weight.shape[1]
    steps = len(row_blocks(width))
    return pl.pallas_call(
        functools.partial(finish_kernel, half, slot_count),
        out_shape=jax.ShapeDtypeStruct((n, width), jnp.bfloat16),
        in_specs=[SMEM] + [VMEM] * 4 + [ANY],
        out_specs=ANY,
        scratch_shapes=[
            pltpu.VMEM(weight.shape, weight.dtype),
            pltpu.VMEM((n, width), jnp.float32),
            pltpu.VMEM((n, width), jnp.bfloat16),
            pltpu.SemaphoreType.DMA((steps,)),
            pltpu.SemaphoreType.DMA((5,)),
        ],
        compiler_params=params(50),
        cost_estimate=pl.CostEstimate(
            flops=2 * n * width * width, bytes_accessed=2 * width * width, transcendentals=0
        ),
        name="finish",
    )(live, groups, back, private, private_lse, weight)


def per_device(
    queries,
    prefix_keys,
    prefix_values,
    pool_keys,
    pool_values,
    page_table,
    private_length,
    group_ids,
    live_rows,
    out_weight,
):
    devices = lax.axis_size("req")
    half = devices // 2
    row_count, width = queries.shape
    slot_count = 2 * row_count // devices
    page_size = pool_keys.shape[1]
    halves = [list(range(half)), list(range(half, devices))]
    quarter = devices // 4
    mirror = [(i, (3 - i // quarter) * quarter + i % quarter) for i in range(devices)]
    outer_pairs = [pair for pair in mirror if pair[0] // quarter in (0, 3)]
    inner_pairs = [pair for pair in mirror if pair[0] // quarter in (1, 2)]

    groups = group_ids.reshape(1, row_count)
    lengths = private_length.reshape(1, row_count)
    pages = page_table.T
    flat_keys = pool_keys.reshape(-1, pool_keys.shape[2])
    flat_values = pool_values.reshape(-1, pool_values.shape[2])

    def exchange(rows):
        blocks = rows.reshape(half, slot_count, rows.shape[1])
        blocks = lax.all_to_all(
            blocks, "req", split_axis=0, concat_axis=0, tiled=True, axis_index_groups=halves
        )
        return blocks.reshape(rows.shape)

    prompt = (prefix_keys, prefix_values)
    outer = [lax.ppermute(x, "req", outer_pairs) for x in prompt]
    inner = [lax.ppermute(x, "req", inner_pairs) for x in prompt]
    placed, token = place(queries, groups, half, slot_count)
    rows = exchange(placed)
    private, private_lse = private_part(
        queries, flat_keys, flat_values, pages, lengths, (token, outer[0]), page_size
    )
    out = prefix_part(quarter, rows, prompt, outer, inner, private_lse)
    back = exchange(out)
    return finish(
        live_rows, groups, back, private, private_lse, out_weight, half, slot_count
    )


def solution(mesh):
    placed = (
        P("req", None),
        P("req", None),
        P("req", None),
        P("req", None, None),
        P("req", None, None),
        P("req", None),
        P("req"),
        P("req", None),
        P("req"),
        P(),
    )
    return jax.shard_map(
        per_device, mesh=mesh, in_specs=placed, out_specs=P("req", None), check_vma=False
    )
```
